32 devices in a mesh: pack: 4 (over z), blk: 8 (over y, x, core).
Axes of the slice: x: 2, y: 2, z: 4, core: 2. Of those that a mesh axis runs over, the one named last changes fastest.
Arguments:
- patches: bfloat16 [8, 1024, 384], P('pack', 'blk'), may hold values from -6 to 6
- specials: bfloat16 [8, 16, 384], P('pack'), may hold values from -6 to 6
- image_lengths: int32 [8, 8], P('pack'), may hold values from 1 to 1017, as said below
- pad_counts: int32 [8, 8], P('pack'), may hold values from 0 to 32, as said below
- ln1_gain: float32 [2, 384], replicated, may hold values from 0.1 to 1.9
- ln1_bias: float32 [2, 384], replicated, may hold values from -4 to 4
- w_qkv: bfloat16 [2, 384, 1152], replicated, may hold values from -0.4375 to 0.4375
- qv_bias: float32 [2, 768], replicated, may hold values from -4 to 4
- w_proj: bfloat16 [2, 384, 384], replicated, may hold values from -0.625 to 0.625
- proj_bias: float32 [2, 384], replicated, may hold values from -4 to 4
- ln2_gain: float32 [2, 384], replicated, may hold values from 0.1 to 1.9
- ln2_bias: float32 [2, 384], replicated, may hold values from -4 to 4
- w_fc1: bfloat16 [2, 384, 1536], replicated, may hold values from -0.3125 to 0.3125
- fc1_bias: float32 [2, 1536], replicated, may hold values from -4 to 4
- w_fc2: bfloat16 [2, 1536, 384], replicated, may hold values from -0.15625 to 0.15625
- fc2_bias: float32 [2, 384], replicated, may hold values from -4 to 4
- d_patches: bfloat16 [8, 1024, 384], P('pack', 'blk'), may hold values from -6 to 6
- d_specials: bfloat16 [8, 16, 384], P('pack'), may hold values from -6 to 6
Outputs:
- out_patches: bfloat16 [8, 1024, 384], P('pack', 'blk')
- out_specials: bfloat16 [8, 16, 384], P('pack')
- grad_patches: float32 [8, 1024, 384], P('pack', 'blk')
- grad_specials: float32 [8, 16, 384], P('pack')
- grad_ln1_gain: float32 [2, 384], replicated
- grad_ln1_bias: float32 [2, 384], replicated
- grad_w_qkv: float32 [2, 384, 1152], replicated
- grad_qv_bias: float32 [2, 768], replicated
- grad_w_proj: float32 [2, 384, 384], replicated
- grad_proj_bias: float32 [2, 384], replicated
- grad_ln2_gain: float32 [2, 384], replicated
- grad_ln2_bias: float32 [2, 384], replicated
- grad_w_fc1: float32 [2, 384, 1536], replicated
- grad_fc1_bias: float32 [2, 1536], replicated
- grad_w_fc2: float32 [2, 1536, 384], replicated
- grad_fc2_bias: float32 [2, 384], replicated
The draws below stay inside these ranges and needn't reach their ends.
Inputs may be any that keep to these rules, and one draw needn't show every extreme that they name: `image_lengths`: each pack's 8 image lengths sum to 1024. In each group of 2 consecutive packs one pack holds an image of 1017 patches beside 8 - 1 images of one patch; in the other packs no image has more than 255 patches. `pad_counts`: an image of n patches has at most min(n // 8, 32) padded slots; the image of 1017 patches has exactly 32.
All inputs are finite; a program needn't handle non-finite values.
Results may differ from the reference program's by a relative error of at most 0.035.
Values may be sent and summed in bfloat16 or wider, within the bound.
No kernel may reach another device: no remote copies, remote signals or barrier semaphores. Data moves between devices by JAX's collectives and lax.ppermute only.
A program may use at most 192 MiB of HBM per device.

```python
import math
import jax
import jax.numpy as jnp
from jax import lax

HEADS = 6
HEAD_DIM = 64
D = 384
FF = 1536
LAYERS = 2
SEQ_DEV = 128
PACKS_DEV = 2
IMG_MEAN = 128
SEQ = 1024
PACKS = 8
IMGS = 8
SPECIALS = 16


def image_plan(key):
    split_keys = jax.random.split(key, 5)
    half_count = IMGS // 2
    offsets = jax.random.randint(split_keys[0], (PACKS, half_count), -(IMG_MEAN - 1), IMG_MEAN)
    offsets = offsets.at[:, 0].set(IMG_MEAN - 1)
    short_lengths = jnp.concatenate([IMG_MEAN + offsets, IMG_MEAN - offsets], axis=1)
    pack_keys = jax.random.split(split_keys[1], PACKS)
    orders = jax.vmap(lambda one_key: jax.random.permutation(one_key, IMGS))(pack_keys)
    short_lengths = jnp.take_along_axis(short_lengths, orders, axis=1)
    chosen = jax.random.randint(split_keys[2], (PACKS // PACKS_DEV,), 0, PACKS_DEV)
    pack_ids = jnp.arange(PACKS)
    is_long = pack_ids % PACKS_DEV == jnp.repeat(chosen, PACKS_DEV)
    long_slot = jax.random.randint(split_keys[3], (PACKS,), 0, IMGS)
    slot_ids = jnp.arange(IMGS)
    at_slot = slot_ids[None, :] == long_slot[:, None]
    long_lengths = jnp.where(at_slot, SEQ - IMGS + 1, 1)
    lengths = jnp.where(is_long[:, None], long_lengths, short_lengths).astype(jnp.int32)
    pad_caps = jnp.minimum(lengths // 8, SEQ_DEV // 4)
    pad_values = jax.random.randint(split_keys[4], (PACKS, IMGS), 0, pad_caps + 1)
    pad_values = jnp.where(is_long[:, None] & at_slot, pad_caps, pad_values).astype(jnp.int32)
    return (lengths, pad_values)


def draw_image_lengths(key, part):
    shared = image_plan(key)
    return shared[0]


def draw_pad_counts(key, part):
    shared = image_plan(key)
    return shared[1]


def shard_levels(key, shape, cuts, smallest, high):
    level, own = 1.0, jax.random.fold_in(key, 6)
    for position, parts in cuts:
        draws = jnp.exp(jax.random.uniform(jax.random.fold_in(own, position), (parts,), jnp.float32, smallest / len(cuts), high / len(cuts)))
        level = level * jnp.repeat(draws, shape[position] // parts).reshape([-1 if axis == position else 1 for axis in range(len(shape))])
    return level


def noise(own_key, shape, scale, most, cuts=(), held_as=jnp.bfloat16):
    factor_of = shard_levels(own_key, shape, cuts, -0.22, 0.18) if cuts else 1.0
    drawn = jax.random.normal(own_key, shape, jnp.float32) * scale * factor_of
    return jnp.minimum(jnp.maximum(drawn, -most), most).astype(held_as)


def setup_inputs(seed: int = 0) -> dict:
    streams_of = jax.random.split(jax.random.key(seed), 19)
    patches = noise(streams_of[0], (PACKS, SEQ, D), 1.0, 6.0, ((0, 4), (1, 8)))
    specials = noise(streams_of[1], (PACKS, SPECIALS, D), 1.0, 6.0, ((0, 4),))
    image_lengths = draw_image_lengths(jax.random.fold_in(streams_of[18], 71), 0)
    pad_counts = draw_pad_counts(jax.random.fold_in(streams_of[18], 71), 0)
    ln1_gain = jnp.clip(1.0 + 0.18 * jax.random.normal(streams_of[4], (LAYERS, D), jnp.float32), 0.1, 1.9)
    ln1_bias = noise(streams_of[5], (LAYERS, D), 0.3, 4.0, (), jnp.float32)
    w_qkv = noise(streams_of[6], (LAYERS, D, 3 * D), (D // 2) ** -0.5, 0.4375)
    qv_bias = noise(streams_of[7], (LAYERS, 2 * D), 0.3, 4.0, (), jnp.float32)
    w_proj = noise(streams_of[8], (LAYERS, D, D), (D // 4) ** -0.5, 0.625)
    proj_bias = noise(streams_of[9], (LAYERS, D), 0.3, 4.0, (), jnp.float32)
    ln2_gain = jnp.clip(1.0 + 0.18 * jax.random.normal(streams_of[10], (LAYERS, D), jnp.float32), 0.1, 1.9)
    ln2_bias = noise(streams_of[11], (LAYERS, D), 0.3, 4.0, (), jnp.float32)
    w_fc1 = noise(streams_of[12], (LAYERS, D, FF), D ** -0.5, 0.3125)
    fc1_bias = noise(streams_of[13], (LAYERS, FF), 0.3, 4.0, (), jnp.float32)
    w_fc2 = noise(streams_of[14], (LAYERS, FF, D), FF ** -0.5, 0.15625)
    fc2_bias = noise(streams_of[15], (LAYERS, D), 0.3, 4.0, (), jnp.float32)
    d_patches = noise(streams_of[16], (PACKS, SEQ, D), 1.0, 6.0, ((0, 4), (1, 8)))
    d_specials = noise(streams_of[17], (PACKS, SPECIALS, D), 1.0, 6.0, ((0, 4),))
    return dict(patches=patches, specials=specials, image_lengths=image_lengths, pad_counts=pad_counts, ln1_gain=ln1_gain, ln1_bias=ln1_bias, w_qkv=w_qkv, qv_bias=qv_bias, w_proj=w_proj, proj_bias=proj_bias, ln2_gain=ln2_gain, ln2_bias=ln2_bias, w_fc1=w_fc1, fc1_bias=fc1_bias, w_fc2=w_fc2, fc2_bias=fc2_bias, d_patches=d_patches, d_specials=d_specials)


NEG_FILL = -1e+30
NORM_EPS = 1e-06
HIGH_PRECISION = lax.Precision.HIGHEST

@jax.custom_vjp
def low(v):
    return lax.optimization_barrier(v.astype(jnp.bfloat16)).astype(jnp.float32)

@jax.custom_vjp
def low_back(v):
    return v

def low_keep(v):
    return (low(v), None)

def low_pass(kept, grad):
    return (grad,)

def back_keep(v):
    return (v, None)

def back_low(kept, grad):
    return (low(grad),)
low.defvjp(low_keep, low_pass)
low_back.defvjp(back_keep, back_low)

def image_layout(lengths, pad_values):
    image_ends = jnp.cumsum(lengths).astype(jnp.int32)
    places = jnp.arange(SEQ, dtype=jnp.int32)
    image_of = lax.optimization_barrier(jnp.sum((places[:, None] >= image_ends[None, :]).astype(jnp.int32), axis=1)).astype(jnp.int32)
    slot_ids = jnp.arange(IMGS, dtype=jnp.int32)
    live_stops = lax.optimization_barrier(jnp.sum(jnp.where(image_of[:, None] == slot_ids[None, :], (image_ends - pad_values)[None, :], 0), axis=1)).astype(jnp.int32)
    return (image_of, places < live_stops)

def layer_norm(row_values, gain_row, shift_row):
    centre = row_values - lax.optimization_barrier(jnp.mean(row_values, axis=-1, keepdims=True))
    spread = lax.optimization_barrier(jnp.mean(centre * centre, axis=-1, keepdims=True))
    return centre * lax.rsqrt(spread + NORM_EPS) * gain_row + shift_row

def attend_rows(query_rows, query_image, key_rows, value_rows, key_image, key_live):
    scores = jnp.einsum('qhe,khe->hqk', query_rows, key_rows, precision=HIGH_PRECISION) * 0.125
    scores = low_back(scores)
    allowed = ((query_image[:, None] == key_image[None, :]) & key_live[None, :])[None]
    scores = jnp.where(allowed, scores, NEG_FILL)
    top_score = lax.optimization_barrier(jnp.max(scores, axis=-1, keepdims=True))
    weights = jnp.where(allowed, jnp.exp(scores - top_score), 0.0)
    prob_rows = low(weights / lax.optimization_barrier(jnp.sum(weights, axis=-1, keepdims=True)))
    return jnp.einsum('hqk,khe->qhe', prob_rows, value_rows, precision=HIGH_PRECISION)

def block_layer(tokens, key_image, key_live, layer_weights):
    gain_one, bias_one, qkv_weight, qv_part, proj_weight, proj_part, gain_two, bias_two, fc1_weight, fc1_part, fc2_weight, fc2_part = layer_weights
    row_total = tokens.shape[0]
    normed = low(layer_norm(tokens, gain_one, bias_one))
    qkv_shift = jnp.concatenate([qv_part[:D], jnp.zeros((D,), qv_part.dtype), qv_part[D:]])
    mixed_rows = low_back(low(jnp.dot(normed, qkv_weight, precision=HIGH_PRECISION) + qkv_shift))
    query_rows = mixed_rows[:, :D].reshape(row_total, HEADS, HEAD_DIM)
    key_rows = mixed_rows[:, D:2 * D].reshape(row_total, HEADS, HEAD_DIM)
    value_rows = mixed_rows[:, 2 * D:].reshape(row_total, HEADS, HEAD_DIM)
    attend = jax.checkpoint(attend_rows)
    query_block = math.gcd(SEQ, 512)
    patch_queries = query_rows[:SEQ].reshape(SEQ // query_block, query_block, HEADS, HEAD_DIM)
    patch_images = key_image[:SEQ].reshape(SEQ // query_block, query_block)
    patch_out = lax.map(lambda block_pair: attend(block_pair[0], block_pair[1], key_rows, value_rows, key_image, key_live), (patch_queries, patch_images))
    special_out = attend(query_rows[SEQ:], key_image[SEQ:], key_rows, value_rows, key_image, key_live)
    attended = jnp.concatenate([patch_out.reshape(SEQ, HEADS, HEAD_DIM), special_out], axis=0).reshape(row_total, D)
    attended = low_back(low(attended))
    after_attn = tokens + low_back(jnp.dot(attended, proj_weight, precision=HIGH_PRECISION) + proj_part)
    normed_two = low(layer_norm(after_attn, gain_two, bias_two))
    hidden_pre = low_back(jnp.dot(normed_two, fc1_weight, precision=HIGH_PRECISION) + fc1_part)
    hidden = low(jax.nn.gelu(hidden_pre, approximate=False))
    return after_attn + low_back(jnp.dot(hidden, fc2_weight, precision=HIGH_PRECISION) + fc2_part)

def reference(patches, specials, image_lengths, pad_counts, ln1_gain, ln1_bias, w_qkv, qv_bias, w_proj, proj_bias, ln2_gain, ln2_bias, w_fc1, fc1_bias, w_fc2, fc2_bias, d_patches, d_specials):
    params = tuple((stacked.astype(jnp.float32) for stacked in (ln1_gain, ln1_bias, w_qkv, qv_bias, w_proj, proj_bias, ln2_gain, ln2_bias, w_fc1, fc1_bias, w_fc2, fc2_bias)))
    special_image = (jnp.arange(SPECIALS, dtype=jnp.int32) // 2).astype(jnp.int32)

    def one_pack(totals, inputs):
        pack_patch, pack_special, lengths, pad_values, patch_cot, special_cot = inputs
        image_of, live = image_layout(lengths, pad_values)
        key_image = jnp.concatenate([image_of, special_image]).astype(jnp.int32)
        key_live = jnp.concatenate([live, jnp.ones((SPECIALS,), jnp.bool_)])
        tokens = jnp.concatenate([pack_patch.astype(jnp.float32), pack_special.astype(jnp.float32)], axis=0)

        def forward(start_rows, layer_params):
            current = start_rows
            for layer_index in range(LAYERS):
                current = block_layer(current, key_image, key_live, tuple((stacked[layer_index] for stacked in layer_params)))
            return current
        result, pullback = jax.vjp(forward, tokens, params)
        cotangent = jnp.concatenate([patch_cot.astype(jnp.float32) * live[:, None].astype(jnp.float32), special_cot.astype(jnp.float32)], axis=0)
        grad_rows, grad_params = pullback(cotangent)
        totals = jax.tree.map(jnp.add, totals, grad_params)
        return (totals, (result[:SEQ].astype(jnp.bfloat16), result[SEQ:].astype(jnp.bfloat16), grad_rows[:SEQ], grad_rows[SEQ:]))
    zero_grads = jax.tree.map(jnp.zeros_like, params)
    totals, outputs = lax.scan(one_pack, zero_grads, (patches, specials, image_lengths, pad_counts, d_patches, d_specials))
    return (outputs[0], outputs[1], outputs[2], outputs[3], totals[0], totals[1], totals[2], totals[3], totals[4], totals[5], totals[6], totals[7], totals[8], totals[9], totals[10], totals[11])
```

```python
import functools

import jax
import jax.numpy as jnp
from jax import lax
from jax.experimental import pallas as pl
from jax.experimental.pallas import tpu as pltpu
from jax.sharding import PartitionSpec as P

HEADS = 6
HEAD_DIM = 64
PAIRS = HEADS // 2
LANES = 128
SPLITS = 3
BLOCKED = -1e30
NORM_EPS = 1e-06
ROOT_HALF = 0.7071067811865476
INV_ROOT_TWO_PI = 0.3989422804014327
F32 = jnp.float32
LOW = jnp.bfloat16
VMEM_BYTES = 56 * 1024 * 1024


def dot(a, b):
    return jnp.dot(a, b, preferred_element_type=F32)


def dot_nt(a, b):
    return lax.dot_general(a, b, (((1,), (1,)), ((), ())), preferred_element_type=F32)


def dot_tn(a, b):
    return lax.dot_general(a, b, (((0,), (0,)), ((), ())), preferred_element_type=F32)


def lane_ids(rows):
    return lax.broadcasted_iota(jnp.int32, (rows, LANES), 1)


def row_ids(rows, lanes=LANES):
    return lax.broadcasted_iota(jnp.int32, (rows, lanes), 0)


def norm_parts(rows):
    centre = rows - jnp.mean(rows, axis=-1, keepdims=True)
    inverse = lax.rsqrt(jnp.mean(centre * centre, axis=-1, keepdims=True) + NORM_EPS)
    return centre * inverse, inverse


def normed(rows, gain, bias):
    return (norm_parts(rows)[0] * gain + bias).astype(LOW)


def norm_back(grad_out, rows, gain):
    scaled, inverse = norm_parts(rows)
    grad_scaled = grad_out * gain
    grad_rows = inverse * (
        grad_scaled
        - jnp.mean(grad_scaled, axis=-1, keepdims=True)
        - scaled * jnp.mean(grad_scaled * scaled, axis=-1, keepdims=True)
    )
    return grad_rows, scaled


def column_sum(rows):
    return jnp.sum(rows, axis=0, keepdims=True)


class Plan:
    def __init__(self, cycle, patch_count, special_count, image_count):
        self.cycle = cycle
        self.group = cycle // 2
        self.block = patch_count
        self.specials = special_count
        self.images = image_count
        self.patch_rows = cycle * patch_count
        self.special_pad = -(-special_count // LANES) * LANES
        self.rows = self.patch_rows + self.special_pad
        self.own_patch = 2 * patch_count
        self.own = self.own_patch + special_count
        self.extra = image_count + 1
        steps = [c for c in (384, 256, 128) if self.rows % c == 0]
        self.chunk = steps[0]

    def place(self):
        me = lax.axis_index("blk")
        return me // self.group, me % self.group

    def at(self, half, other):
        return pl.multiple_of((half * self.group + other) * self.block, self.block)

    def own_rows(self, ref, place):
        return jnp.concatenate(
            [
                ref[pl.ds(self.at(0, place), self.block), :],
                ref[pl.ds(self.at(1, place), self.block), :],
                ref[self.patch_rows : self.patch_rows + self.specials, :],
            ],
            axis=0,
        )


def image_lanes(plan, lengths, pads, pack):
    lane = lane_ids(1)
    start = jnp.zeros((1, LANES), jnp.int32)
    stop, live = start, start
    so_far = jnp.int32(0)
    for image in range(plan.images):
        start = jnp.where(lane == image, so_far, start)
        so_far = so_far + lengths[pack, image]
        stop = jnp.where(lane == image, so_far, stop)
        live = jnp.where(lane == image, so_far - pads[pack, image], live)
    return start, stop, live


def write_masks(plan, lengths, pads, pack, key_extra, query_extra):
    start, stop, live = image_lanes(plan, lengths, pads, pack)
    count = plan.block
    lane = lane_ids(count)
    one, zero = jnp.ones((count, LANES), F32), jnp.zeros((count, LANES), F32)

    @pl.loop(0, plan.cycle)
    def _(step):
        base = pl.multiple_of(step * count, count)
        token = row_ids(count) + base
        inside = (token >= start) & (token < stop)
        alive = (token >= start) & (token < live)
        key_extra[pl.ds(base, count), :] = jnp.where(alive, zero, one).astype(LOW)
        query_extra[pl.ds(base, count), :] = jnp.where(inside, BLOCKED, zero).astype(LOW)

    count = plan.special_pad
    lane, special = lane_ids(count), row_ids(count)
    one, zero = jnp.ones((count, LANES), F32), jnp.zeros((count, LANES), F32)
    mine = (lane == special // 2) & (special < plan.specials)
    never = (lane == plan.images) & (special >= plan.specials)
    key_extra[plan.patch_rows :, :] = jnp.where(mine, zero, one).astype(LOW)
    query_extra[plan.patch_rows :, :] = jnp.where(mine | never, BLOCKED, zero).astype(LOW)


def project(plan, all_normed, weight, shift, mixed):
    @pl.loop(0, plan.rows // plan.chunk)
    def _(step):
        here = pl.ds(pl.multiple_of(step * plan.chunk, plan.chunk), plan.chunk)
        out = (dot(all_normed[here, :], weight[...]) + shift).astype(LOW)
        for part in range(3 * PAIRS):
            mixed[part, here, :] = out[:, part * LANES : (part + 1) * LANES]


def shift_row(qv_bias):
    width = qv_bias.shape[1] // 2
    return jnp.concatenate(
        [qv_bias[:, :width], jnp.zeros((1, width), F32), qv_bias[:, width:]], axis=1
    )


def attend(plan, place, mixed, key_extra, query_extra, keys, joined, total):
    lane = lane_ids(plan.own)
    own_extra = plan.own_rows(query_extra, place)
    keys[:, LANES:] = key_extra[...]
    total[...] = jnp.zeros_like(total)

    @pl.loop(0, PAIRS)
    def _(pair):
        query = (plan.own_rows(mixed.at[pair], place).astype(F32) * 0.125).astype(LOW)
        keys[:, :LANES] = mixed[PAIRS + pair]
        out, logs = [], total[...]
        for side in range(2):
            mine = (lane // HEAD_DIM) == side
            left = jnp.concatenate([jnp.where(mine, query, 0), own_extra], axis=1)
            scores = dot_nt(left, keys[...])
            top = jnp.max(scores, axis=-1, keepdims=True)
            weights = jnp.exp(scores - top)
            amount = jnp.sum(weights, axis=-1, keepdims=True)
            out.append(dot(weights.astype(LOW), mixed[2 * PAIRS + pair]) / amount)
            logs = jnp.where(lane == 2 * pair + side, top + jnp.log(amount), logs)
        joined[pair] = jnp.where(lane < HEAD_DIM, out[0], out[1])
        total[...] = logs


def feed_forward(second_normed, fc1, fc1_bias, fc2, hidden, slope):
    out = None
    width = second_normed.shape[1]
    for first in range(0, fc1.shape[1], width):
        here = slice(first, first + width)
        pre = dot(second_normed, fc1[:, here]) + fc1_bias[:, here]
        cdf = 0.5 * (1.0 + lax.erf(pre * ROOT_HALF))
        pdf = jnp.exp(-0.5 * pre * pre) * INV_ROOT_TWO_PI
        value = (pre * cdf).astype(LOW)
        hidden[:, here] = value
        slope[:, here] = cdf + pre * pdf
        part = dot(value, fc2[here, :])
        out = part if out is None else out + part
    return out


def forward_rest(layer, start, joined, w_proj, proj_bias, ln2_gain, ln2_bias, w_fc1, fc1_bias,
                 w_fc2, fc2_bias, hidden, slope, middle):
    row = slice(layer, layer + 1)
    attended = jnp.concatenate([joined[pair] for pair in range(PAIRS)], axis=1)
    after = start + dot(attended.astype(LOW), w_proj.ready()[...]) + proj_bias[row, :]
    middle[...] = after
    second = normed(after, ln2_gain[row, :], ln2_bias[row, :])
    out = feed_forward(second, w_fc1.ready(), fc1_bias[row, :], w_fc2.ready(), hidden, slope)
    return after + out + fc2_bias[row, :]


def first_kernel(plan, *refs):
    blocks, refs = refs[: 2 * plan.group], refs[2 * plan.group :]
    (lengths, pads, specials, ln1_gain, ln1_bias, w_qkv, qv_bias, w_proj, proj_bias, ln2_gain,
     ln2_bias, w_fc1, fc1_bias, w_fc2, fc2_bias,
     key_extra, query_extra, mixed, start, middle, joined, total, hidden, slope, after, send, keep,
     all_normed, keys) = refs
    half, place = plan.place()
    gain, bias = ln1_gain[0:1, :], ln1_bias[0:1, :]
    for index, ref in enumerate(blocks):
        side = half if index < plan.group else 1 - half
        other = jnp.bitwise_xor(place, index % plan.group)
        rows = ref[...].astype(F32)
        all_normed[pl.ds(plan.at(side, other), plan.block), :] = normed(rows, gain, bias)
        if index % plan.group == 0:
            start[pl.ds(pl.multiple_of(side * plan.block, plan.block), plan.block), :] = rows
    rows = specials[half].astype(F32)
    start[plan.own_patch :, :] = rows
    all_normed[plan.patch_rows :, :] = jnp.zeros((plan.special_pad, rows.shape[1]), LOW)
    all_normed[plan.patch_rows : plan.patch_rows + plan.specials, :] = normed(rows, gain, bias)
    write_masks(plan, lengths, pads, half, key_extra, query_extra)
    project(plan, all_normed, w_qkv.ready(), shift_row(qv_bias[0:1, :]), mixed)
    attend(plan, place, mixed, key_extra, query_extra, keys, joined, total)
    out = forward_rest(0, start[...], joined, w_proj, proj_bias, ln2_gain, ln2_bias, w_fc1,
                       fc1_bias, w_fc2, fc2_bias, hidden, slope, middle)
    after[...] = out
    following = normed(out, ln1_gain[1:2, :], ln1_bias[1:2, :])
    send[...] = following[: plan.own_patch]
    keep[...] = following[plan.own_patch :]


def split_low(values):
    parts, rest = [], values
    for _ in range(SPLITS):
        part = rest.astype(LOW)
        parts.append(part)
        rest = rest - part.astype(F32)
    return parts


def backward_rest(plan, layer, grad_rows, scale, middle, joined, total, hidden, slope, ln2_gain,
                  ln2_bias, w_fc1, w_fc2, w_proj, small, second, second_grad, pre_grad,
                  attended_low, first_grad, send, out_grad, logs):
    row = slice(layer, layer + 1)
    width = grad_rows.shape[1]
    low_grad = grad_rows.astype(LOW)
    second_grad[...] = low_grad
    after = middle[...]
    second[...] = normed(after, ln2_gain[row, :], ln2_bias[row, :])
    grad_second = None
    for first in range(0, slope.shape[1], width):
        here = slice(first, first + width)
        value = (dot_nt(low_grad, w_fc2.ready()[here, :]) * slope[:, here]).astype(LOW)
        pre_grad[:, here] = value
        small[6:7, here] = column_sum(value.astype(F32) * scale)
        part = dot_nt(value, w_fc1.ready()[:, here])
        grad_second = part if grad_second is None else grad_second + part
    change, scaled = norm_back(grad_second, after, ln2_gain[row, :])
    weighted = grad_second * scale
    grad_middle = grad_rows + change
    low_middle = grad_middle.astype(LOW)
    first_grad[...] = low_middle
    small[3:4, :width] = column_sum(low_middle.astype(F32) * scale)
    small[4:5, :width] = column_sum(weighted * scaled)
    small[5:6, :width] = column_sum(weighted)
    small[7:8, :width] = column_sum(low_grad.astype(F32) * scale)
    grad_out = dot_nt(low_middle, w_proj.ready()[...]).astype(LOW)
    out_grad[...] = grad_out
    lane = lane_ids(plan.own)
    table = total[...]
    for pair in range(PAIRS):
        here = slice(pair * LANES, (pair + 1) * LANES)
        attended = joined[pair]
        attended_low[:, here] = attended.astype(LOW)
        product = grad_out[:, here].astype(F32) * attended
        for side in range(2):
            mine = (lane // HEAD_DIM) == side
            delta = jnp.sum(jnp.where(mine, product, 0.0), axis=-1, keepdims=True)
            table = jnp.where(lane == HEADS + 2 * pair + side, delta, table)
    logs[...] = table
    send[: plan.own_patch, :] = grad_out[: plan.own_patch]
    pick = jnp.where(row_ids(16) == lane_ids(16), 1.0, 0.0).astype(LOW)
    parts = split_low(table)
    for part in range(2):
        rows = slice(part * plan.block, (part + 1) * plan.block)
        turned = [dot_nt(pick, values[rows]).astype(LOW) for values in parts]
        first = plan.own_patch + 16 * part
        send[first : first + 16, :] = jnp.concatenate(turned, axis=1)
    return grad_middle


def owner_scale(plan, place):
    row = lax.broadcasted_iota(jnp.int32, (plan.own, 1), 0)
    return jnp.where((row < plan.own_patch) | (place == 0), 1.0, 0.0)


def second_kernel(plan, *refs):
    pieces, refs = refs[: plan.group], refs[plan.group :]
    (normed_specials, key_extra, query_extra, start, grad_kept, grad_swapped, grad_specials,
     ln1_gain, w_qkv, qv_bias, w_proj, proj_bias, ln2_gain, ln2_bias, w_fc1, fc1_bias, w_fc2,
     fc2_bias,
     mixed, out_kept, out_send, grad_middle, send, out_grad, logs, small, second, second_grad,
     pre_grad, attended_low, first_grad, hidden,
     all_normed, keys, joined, total, slope, middle) = refs
    half, place = plan.place()
    gather_normed(plan, place, pieces, normed_specials, all_normed)
    project(plan, all_normed, w_qkv.ready(), shift_row(qv_bias[1:2, :]), mixed)
    attend(plan, place, mixed, key_extra, query_extra, keys, joined, total)
    out = forward_rest(1, start[...], joined, w_proj, proj_bias, ln2_gain, ln2_bias, w_fc1,
                       fc1_bias, w_fc2, fc2_bias, hidden, slope, middle)
    low_out = out.astype(LOW)
    first, later = low_out[: plan.block], low_out[plan.block : plan.own_patch]
    out_kept[...] = jnp.where(half == 0, first, later)
    out_send[: plan.block, :] = jnp.where(half == 0, later, first)
    out_send[plan.block :, :] = low_out[plan.own_patch :]
    kept, swapped = grad_kept[...].astype(F32), grad_swapped[...].astype(F32)
    own_extra = plan.own_rows(key_extra, place)[: plan.own_patch].astype(F32)
    lane = lane_ids(plan.own_patch)
    live = jnp.sum(jnp.where(lane < plan.images, 1.0 - own_extra, 0.0), axis=-1, keepdims=True)
    patch_grad = jnp.concatenate(
        [jnp.where(half == 0, kept, swapped), jnp.where(half == 0, swapped, kept)], axis=0
    )
    grad_rows = jnp.concatenate([patch_grad * live, grad_specials[half].astype(F32)], axis=0)
    small[0:3, :] = jnp.zeros((3, small.shape[1]), F32)
    grad_middle[...] = backward_rest(
        plan, 1, grad_rows, owner_scale(plan, place), middle, joined, total, hidden, slope,
        ln2_gain, ln2_bias, w_fc1, w_fc2, w_proj, small, second, second_grad, pre_grad,
        attended_low, first_grad, send, out_grad, logs)


def gather_normed(plan, place, pieces, normed_specials, all_normed):
    for index, ref in enumerate(pieces):
        other = jnp.bitwise_xor(place, index)
        for half in range(2):
            all_normed[pl.ds(plan.at(half, other), plan.block), :] = ref[
                half * plan.block : (half + 1) * plan.block, :
            ]
    width = all_normed.shape[1]
    all_normed[plan.patch_rows :, :] = jnp.zeros((plan.special_pad, width), LOW)
    all_normed[plan.patch_rows : plan.patch_rows + plan.specials, :] = normed_specials[...]


def placed(plan, rows, first_row, first_lane):
    row, lane = row_ids(rows), lane_ids(rows)
    out = []
    for split in range(SPLITS):
        head = row - first_row
        hit = (head >= 0) & (head < HEADS) & (lane == first_lane + SPLITS * head + split)
        out.append(jnp.where(hit, -1.0, 0.0).astype(LOW))
    return out


def spread_logs(plan, table, first_row):
    picks = placed(plan, LANES, first_row, plan.extra)
    return sum(dot(values, pick) for values, pick in zip(split_low(table), picks)).astype(LOW)


def head_lanes(plan, lane, head):
    first = plan.extra + SPLITS * head
    return (lane >= first) & (lane < first + SPLITS)


def query_grad_kernel(plan, mixed, key_extra, query_extra, out_grad, logs, grad_query, keys, values):
    _, place = plan.place()
    lane = lane_ids(plan.own)
    own_extra = plan.own_rows(query_extra, place)
    log_extra = spread_logs(plan, logs[...], 0)
    delta_extra = spread_logs(plan, logs[...], HEADS)
    keys[:, LANES:] = key_extra[...]
    values[:, LANES:] = key_extra[...]

    @pl.loop(0, PAIRS)
    def _(pair):
        query = (plan.own_rows(mixed.at[pair], place).astype(F32) * 0.125).astype(LOW)
        here = pl.ds(pl.multiple_of(pair * LANES, LANES), LANES)
        grad_out = out_grad[:, here]
        keys[:, :LANES] = mixed[PAIRS + pair]
        values[:, :LANES] = mixed[2 * PAIRS + pair]
        out = []
        for side in range(2):
            mine = (lane // HEAD_DIM) == side
            head = head_lanes(plan, lane, 2 * pair + side)
            left = jnp.concatenate(
                [jnp.where(mine, query, 0), jnp.where(head, log_extra, own_extra)], axis=1
            )
            probs = jnp.exp(dot_nt(left, keys[...]))
            left = jnp.concatenate(
                [jnp.where(mine, grad_out, 0), jnp.where(head, delta_extra, 0)], axis=1
            )
            grad_scores = (probs * dot_nt(left, values[...])).astype(LOW)
            out.append(dot(grad_scores, mixed[PAIRS + pair]) * 0.125)
        grad_query[:, here] = jnp.where(lane < HEAD_DIM, out[0], out[1]).astype(LOW)


def key_grads(plan, place, pieces, mixed, key_extra, query_extra, out_grad, logs, grad_mixed,
              queries, grads, all_grads):
    log_rows = placed(plan, 16, 0, plan.extra)
    delta_rows = placed(plan, 16, HEADS, plan.extra)
    picks = [jnp.concatenate(two, axis=1) for two in zip(log_rows, delta_rows)]
    for index, ref in enumerate(pieces):
        other = jnp.bitwise_xor(place, index)
        for half in range(2):
            here = pl.ds(plan.at(half, other), plan.block)
            for pair in range(PAIRS):
                all_grads[pair, here, :] = ref[
                    half * plan.block : (half + 1) * plan.block, pair * LANES : (pair + 1) * LANES
                ]
            first = plan.own_patch + 16 * half
            both = sum(
                dot_tn(ref[first : first + 16, split * LANES : (split + 1) * LANES], picks[split])
                for split in range(SPLITS)
            )
            queries[here, LANES:] = (both[:, :LANES] + query_extra[here, :].astype(F32)).astype(LOW)
            grads[here, LANES:] = both[:, LANES:].astype(LOW)
    last, stop = plan.patch_rows, plan.patch_rows + plan.specials
    table = logs[plan.own_patch :, :]
    log_extra = spread_logs(plan, table, 0).astype(F32)
    queries[last:, LANES:] = query_extra[last:, :]
    queries[last:stop, LANES:] = (log_extra + query_extra[last:stop, :].astype(F32)).astype(LOW)
    grads[last:, LANES:] = jnp.zeros((plan.special_pad, LANES), LOW)
    grads[last:stop, LANES:] = spread_logs(plan, table, HEADS)
    for pair in range(PAIRS):
        all_grads[pair, last:, :] = jnp.zeros((plan.special_pad, LANES), LOW)
        all_grads[pair, last:stop, :] = out_grad[
            plan.own_patch :, pair * LANES : (pair + 1) * LANES
        ]
    lane = lane_ids(plan.own)
    own_extra = plan.own_rows(key_extra, place)
    own_extra = jnp.where(lane < plan.extra, own_extra, 0)

    @pl.loop(0, PAIRS)
    def _(pair):
        queries[:, :LANES] = (mixed[pair].astype(F32) * 0.125).astype(LOW)
        grads[:, :LANES] = all_grads[pair]
        key = plan.own_rows(mixed.at[PAIRS + pair], place)
        value = plan.own_rows(mixed.at[2 * PAIRS + pair], place)
        grad_key, grad_value = [], []
        for side in range(2):
            mine = (lane // HEAD_DIM) == side
            head = head_lanes(plan, lane, 2 * pair + side)
            extra = jnp.where(head, 1.0, own_extra.astype(F32)).astype(LOW)
            left = jnp.concatenate([jnp.where(mine, key, 0), extra], axis=1)
            probs = jnp.exp(dot_nt(left, queries[...]))
            left = jnp.concatenate([jnp.where(mine, value, 0), extra], axis=1)
            grad_scores = (probs * dot_nt(left, grads[...])).astype(LOW)
            grad_key.append(dot(grad_scores, queries[:, :LANES]))
            grad_value.append(dot(probs.astype(LOW), all_grads[pair]))
        width = PAIRS * LANES
        here = pl.ds(pl.multiple_of(width + pair * LANES, LANES), LANES)
        grad_mixed[:, here] = jnp.where(lane < HEAD_DIM, *grad_key).astype(LOW)
        here = pl.ds(pl.multiple_of(2 * width + pair * LANES, LANES), LANES)
        grad_mixed[:, here] = jnp.where(lane < HEAD_DIM, *grad_value).astype(LOW)


def first_norm_back(plan, layer, scale, grad_mixed, w_qkv, start, ln1_gain, small):
    width = start.shape[1]
    mixed = grad_mixed[...]
    sums = column_sum(mixed.astype(F32) * scale)
    small[2:3, : 2 * width] = jnp.concatenate([sums[:, :width], sums[:, 2 * width :]], axis=1)
    grad_normed = dot_nt(mixed, w_qkv.ready()[...])
    change, scaled = norm_back(grad_normed, start[...], ln1_gain[layer : layer + 1, :])
    weighted = grad_normed * scale
    small[0:1, :width] = column_sum(weighted * scaled)
    small[1:2, :width] = column_sum(weighted)
    return change


def third_kernel(plan, *refs):
    pieces, refs = refs[: plan.group], refs[plan.group :]
    (mixed, key_extra, query_extra, later_grad, later_logs, grad_query, later_start, later_middle,
     later_small, ln1_gain, later_qkv,
     middle, joined, total, hidden, slope, ln2_gain, ln2_bias, w_fc1, w_fc2, w_proj,
     grad_mixed, small_out, grad_middle, send, out_grad, logs, small, second, second_grad,
     pre_grad, attended_low, first_grad,
     queries, grads, all_grads) = refs
    _, place = plan.place()
    scale = owner_scale(plan, place)
    grad_mixed[:, : grad_query.shape[1]] = grad_query[...]
    key_grads(plan, place, pieces, mixed, key_extra, query_extra, later_grad, later_logs,
              grad_mixed, queries, grads, all_grads)
    small_out[...] = later_small[...]
    grad_rows = later_middle[...] + first_norm_back(
        plan, 1, scale, grad_mixed, later_qkv, later_start, ln1_gain, small_out
    )
    small[0:3, :] = jnp.zeros((3, small.shape[1]), F32)
    grad_middle[...] = backward_rest(
        plan, 0, grad_rows, scale, middle, joined, total, hidden, slope, ln2_gain, ln2_bias,
        w_fc1, w_fc2, w_proj, small, second, second_grad, pre_grad, attended_low, first_grad,
        send, out_grad, logs)


def fourth_kernel(plan, *refs):
    pieces, refs = refs[: plan.group], refs[plan.group :]
    (mixed, key_extra, query_extra, out_grad, logs, grad_query, start, grad_middle, small, ln1_gain,
     w_qkv,
     grad_mixed, small_out, grad_kept, grad_send,
     queries, grads, all_grads) = refs
    half, place = plan.place()
    scale = owner_scale(plan, place)
    grad_mixed[:, : grad_query.shape[1]] = grad_query[...]
    key_grads(plan, place, pieces, mixed, key_extra, query_extra, out_grad, logs, grad_mixed,
              queries, grads, all_grads)
    small_out[...] = small[...]
    out = grad_middle[...] + first_norm_back(
        plan, 0, scale, grad_mixed, w_qkv, start, ln1_gain, small_out
    )
    first, later = out[: plan.block], out[plan.block : plan.own_patch]
    grad_kept[...] = jnp.where(half == 0, first, later)
    grad_send[: plan.block, :] = jnp.where(half == 0, later, first)
    grad_send[plan.block :, :] = out[plan.own_patch :]


def weight_kernel(plan, count, small_rows, used, *refs):
    out = refs[-1]
    place = plan.place()[1]
    keep = owner_scale(plan, place)
    at = 0
    for index in range(count):
        left = (refs[2 * index][...].astype(F32) * keep).astype(LOW)
        right = refs[2 * index + 1]
        step = min(384, right.shape[1])
        for first in range(0, right.shape[1], step):
            product = dot_tn(left, right[:, first : first + step]).astype(LOW)
            for column in range(0, step, LANES):
                out[at : at + left.shape[1], :] = product[:, column : column + LANES]
                at += left.shape[1]
    if small_rows:
        small = refs[2 * count][...]
        for column in range(0, small.shape[1], 2 * LANES):
            two = [small[:, column : column + LANES], small[:, column + LANES : column + 2 * LANES]]
            out[at : at + 16, :] = jnp.concatenate(two, axis=0).astype(LOW)
            at += 16
    if used < out.shape[0]:
        out[used:, :] = jnp.zeros((out.shape[0] - used, LANES), LOW)


VMEM = pl.BlockSpec(memory_space=pltpu.VMEM)
SMEM = pl.BlockSpec(memory_space=pltpu.SMEM)


ANY = pl.BlockSpec(memory_space=pl.ANY)


class Staged:
    def __init__(self, source, layer, target, semaphore):
        self.target = target
        self.copy = pltpu.make_async_copy(source.at[layer], target, semaphore)
        self.copy.start()
        self.waits = True

    def ready(self):
        if self.waits:
            self.copy.wait()
            self.waits = False
        return self.target


def staged_kernel(kernel, layers, out_count, *refs):
    ins, outs = refs[: len(layers)], refs[len(layers) : len(layers) + out_count]
    rest = refs[len(layers) + out_count :]
    chosen = [index for index, layer in enumerate(layers) if layer is not None]
    if not chosen:
        return kernel(*refs)
    buffers, semaphores = rest[: len(chosen)], rest[len(chosen)]
    ins = list(ins)
    for number, index in enumerate(chosen):
        ins[index] = Staged(ins[index], layers[index], buffers[number], semaphores.at[number])
    kernel(*ins, *outs, *rest[len(chosen) + 1 :])
    for index in chosen:
        ins[index].ready()


def run(kernel, name, outs, ins, scratch=(), flops=0):
    specs, values, layers, buffers = [], [], [], []
    for item in ins:
        value, layer = item if isinstance(item, tuple) else (item, None)
        if layer is None:
            specs.append(SMEM if value.dtype == jnp.int32 else VMEM)
        else:
            specs.append(ANY)
            buffers.append(pltpu.VMEM(value.shape[1:], value.dtype))
        layers.append(layer)
        values.append(value)
    if buffers:
        buffers.append(pltpu.SemaphoreType.DMA((len(buffers),)))
    moved = sum(v.size * v.dtype.itemsize for v in values) + sum(
        jnp.dtype(kind).itemsize * functools.reduce(lambda a, b: a * b, shape) for shape, kind in outs
    )
    return pl.pallas_call(
        functools.partial(staged_kernel, kernel, layers, len(outs)),
        out_shape=[jax.ShapeDtypeStruct(shape, kind) for shape, kind in outs],
        in_specs=specs,
        out_specs=[VMEM] * len(outs),
        scratch_shapes=buffers + [pltpu.VMEM(shape, kind) for shape, kind in scratch],
        compiler_params=pltpu.CompilerParams(vmem_limit_bytes=VMEM_BYTES),
        cost_estimate=pl.CostEstimate(flops=int(flops), bytes_accessed=int(moved), transcendentals=0),
        name=name,
    )(*values)


def swap(value, mask):
    size = lax.axis_size("blk")
    return lax.ppermute(value, "blk", [(i, i ^ mask) for i in range(size)])


def spread(value, group):
    held = {0: value}
    mask = group // 2
    while mask:
        for index, item in list(held.items()):
            held[index | mask] = swap(item, mask)
        mask //= 2
    return [held[index] for index in range(group)]


def reduce_axes(pack_size, cycle):
    me, pack = lax.axis_index("blk"), lax.axis_index("pack")
    axes = []
    for bit in range(cycle.bit_length() - 1):
        axes.append(("blk", 1 << bit, (me >> bit) & 1))
    gray = jnp.bitwise_xor(pack, pack >> 1)
    around = []
    for bit in range(pack_size.bit_length() - 1):
        around.append(("pack", (2 << bit) - 1, (gray >> bit) & 1))
    return axes[:1] + around + axes[1:]


def exchange(value, axis, mask):
    size = lax.axis_size(axis)
    return lax.ppermute(value, axis, [(i, i ^ mask) for i in range(size)])


def reduce_all(rows, axes):
    value = rows
    for axis, mask, side in axes:
        halves = value.reshape(2, value.shape[0] // 2, LANES)
        sent = lax.dynamic_index_in_dim(halves, 1 - side, 0, keepdims=False)
        kept = lax.dynamic_index_in_dim(halves, side, 0, keepdims=False)
        got = exchange(sent, axis, mask)
        value = (kept.astype(F32) + got.astype(F32)).astype(LOW)
    for axis, mask, side in reversed(axes):
        got = exchange(value, axis, mask)
        first = jnp.where(side == 0, value, got)
        later = jnp.where(side == 0, got, value)
        value = jnp.concatenate([first, later], axis=0)
    return value


def unpack(rows, at, height, width):
    blocks = width // LANES
    part = rows[at : at + height * blocks].reshape(blocks, height, LANES)
    return part.transpose(1, 0, 2).reshape(height, width).astype(F32), at + height * blocks


def unpack_small(rows, at, width):
    part = rows[at : at + 8 * (width // LANES)].reshape(width // LANES, 8, LANES)
    return part.transpose(1, 0, 2).reshape(8, width).astype(F32)


def on_device(patches, specials, image_lengths, pad_counts, ln1_gain, ln1_bias, w_qkv, qv_bias,
              w_proj, proj_bias, ln2_gain, ln2_bias, w_fc1, fc1_bias, w_fc2, fc2_bias, d_patches,
              d_specials):
    cycle, pack_size = lax.axis_size("blk"), lax.axis_size("pack")
    patch_count, special_count, width = patches.shape[1], specials.shape[1], patches.shape[2]
    hidden_width = w_fc1.shape[2]
    plan = Plan(cycle, patch_count, special_count, image_lengths.shape[1])
    own, rows, group = plan.own, plan.rows, plan.group
    half = lax.axis_index("blk") // group

    def kept_and_sent(pair):
        return (lax.dynamic_index_in_dim(pair, half, 0, keepdims=False),
                lax.dynamic_index_in_dim(pair, 1 - half, 0, keepdims=False))

    def both_packs(kept, got):
        return jnp.stack([jnp.where(half == 0, kept, got), jnp.where(half == 0, got, kept)])

    kept, sent = kept_and_sent(patches)
    blocks = spread(kept, group) + spread(swap(sent, group), group)
    grad_kept, grad_sent = kept_and_sent(d_patches)
    grad_swapped = swap(grad_sent, group)

    extra_shape = ((rows, LANES), LOW)
    mixed_shape = ((3 * PAIRS, rows, LANES), LOW)
    joined_shape = ((PAIRS, own, LANES), F32)
    wide, wide_low = ((own, width), F32), ((own, width), LOW)
    hidden_shape, slope_shape = ((own, hidden_width), LOW), ((own, hidden_width), F32)
    table_shape = ((own, LANES), F32)
    small_shape = ((8, hidden_width), F32)
    send_shape = ((plan.own_patch + 32, width), LOW)
    normed_shape = ((rows, width), LOW)
    double_shape = ((rows, 2 * LANES), LOW)
    attend_flops = 4 * 2 * own * rows * LANES * HEADS
    dense_flops = 2 * own * width * (width + 2 * hidden_width)
    mix_flops = 2 * rows * width * 3 * width

    (key_extra, query_extra, mixed_0, start_0, middle_0, joined_0, total_0, hidden_0, slope_0,
     start_1, send, normed_specials) = run(
        functools.partial(first_kernel, plan), "layer_0_forward",
        [extra_shape, extra_shape, mixed_shape, wide, wide, joined_shape, table_shape, hidden_shape,
         slope_shape, wide, ((plan.own_patch, width), LOW), ((special_count, width), LOW)],
        blocks + [image_lengths, pad_counts, specials, ln1_gain, ln1_bias,
                  (w_qkv, 0), qv_bias, (w_proj, 0), proj_bias, ln2_gain, ln2_bias, (w_fc1, 0),
                  fc1_bias, (w_fc2, 0), fc2_bias],
        [normed_shape, double_shape], attend_flops + dense_flops + mix_flops)
    pieces = spread(send, group)
    (mixed_1, out_kept, out_send, grad_middle_1, send, out_grad_1, logs_1, small_1, second_1,
     second_grad_1, pre_grad_1, attended_1, first_grad_1, hidden_1) = run(
        functools.partial(second_kernel, plan), "layer_1_forward",
        [mixed_shape, ((patch_count, width), LOW), ((patch_count + special_count, width), LOW),
         wide, send_shape, wide_low, table_shape, small_shape, wide_low, wide_low, hidden_shape,
         wide_low, wide_low, hidden_shape],
        pieces + [normed_specials, key_extra, query_extra, start_1, grad_kept, grad_swapped,
                  d_specials, ln1_gain, (w_qkv, 1), qv_bias, (w_proj, 1), proj_bias, ln2_gain,
                  ln2_bias, (w_fc1, 1), fc1_bias, (w_fc2, 1), fc2_bias],
        [normed_shape, double_shape, joined_shape, table_shape, slope_shape, wide],
        attend_flops + 3 * dense_flops + mix_flops)
    out_got = swap(out_send, group)
    later_pieces = spread(send, group)

    def weights(name, products, small, multiple):
        used = sum(a.shape[1] * b.shape[1] // LANES for a, b in products)
        used += 0 if small is None else 8 * hidden_width // LANES
        total = -(-used // multiple) * multiple
        flat = [x for pair in products for x in pair] + ([] if small is None else [small])
        kernel = functools.partial(weight_kernel, plan, len(products), small is not None, used)
        flops = sum(2 * own * a.shape[1] * b.shape[1] for a, b in products)
        return run(kernel, name, [((total, LANES), LOW)], flat, (), flops)[0]

    multiple = 16 * cycle * pack_size
    axes = reduce_axes(pack_size, cycle)
    weights_1 = weights(
        "layer_1_weights",
        [(hidden_1, second_grad_1), (second_1, pre_grad_1), (attended_1, first_grad_1)],
        None, multiple)
    weights_1 = reduce_all(weights_1, axes)

    def query_grad(name, mixed, out_grad, logs):
        kernel = functools.partial(query_grad_kernel, plan)
        ins = [mixed, key_extra, query_extra, out_grad, logs]
        return run(kernel, name, [wide_low], ins, [double_shape, double_shape], 5 * attend_flops // 4)[0]

    all_grads_shape = ((PAIRS, rows, LANES), LOW)
    grad_query_1 = query_grad("layer_1_query_grad", mixed_1, out_grad_1, logs_1)
    (grad_mixed_1, small_1, grad_middle_0, send, out_grad_0, logs_0, small_0, second_0,
     second_grad_0, pre_grad_0, attended_0, first_grad_0) = run(
        functools.partial(third_kernel, plan), "layer_1_key_grad",
        [((own, 3 * width), LOW), small_shape, wide, send_shape, wide_low, table_shape, small_shape,
         wide_low, wide_low, hidden_shape, wide_low, wide_low],
        later_pieces + [mixed_1, key_extra, query_extra, out_grad_1, logs_1, grad_query_1, start_1,
                        grad_middle_1, small_1, ln1_gain, (w_qkv, 1), middle_0, joined_0, total_0,
                        hidden_0, slope_0, ln2_gain, ln2_bias, (w_fc1, 0), (w_fc2, 0), (w_proj, 0)],
        [double_shape, double_shape, all_grads_shape],
        3 * attend_flops // 2 + 2 * dense_flops)
    later_pieces = spread(send, group)
    normed_0 = normed(start_0, ln1_gain[0:1], ln1_bias[0:1])
    normed_1 = normed(start_1, ln1_gain[1:2], ln1_bias[1:2])
    weights_0 = weights(
        "layer_0_weights",
        [(normed_1, grad_mixed_1), (hidden_0, second_grad_0), (second_0, pre_grad_0),
         (attended_0, first_grad_0)],
        small_1, multiple)
    weights_0 = reduce_all(weights_0, axes)
    grad_query_0 = query_grad("layer_0_query_grad", mixed_0, out_grad_0, logs_0)
    grad_mixed_0, small_0, grad_kept_out, grad_send = run(
        functools.partial(fourth_kernel, plan), "layer_0_key_grad",
        [((own, 3 * width), LOW), small_shape, ((patch_count, width), F32),
         ((patch_count + special_count, width), F32)],
        later_pieces + [mixed_0, key_extra, query_extra, out_grad_0, logs_0, grad_query_0, start_0,
                        grad_middle_0, small_0, ln1_gain, (w_qkv, 0)],
        [double_shape, double_shape, all_grads_shape],
        3 * attend_flops // 2)
    grad_got = swap(grad_send, group)
    last_weights = weights("layer_0_mix_weights", [(normed_0, grad_mixed_0)], small_0, multiple)
    last_weights = reduce_all(last_weights, axes)

    at = 0
    fc2_1, at = unpack(weights_1, at, hidden_width, width)
    fc1_1, at = unpack(weights_1, at, width, hidden_width)
    proj_1, at = unpack(weights_1, at, width, width)
    at = 0
    qkv_1, at = unpack(weights_0, at, width, 3 * width)
    fc2_0, at = unpack(weights_0, at, hidden_width, width)
    fc1_0, at = unpack(weights_0, at, width, hidden_width)
    proj_0, at = unpack(weights_0, at, width, width)
    sums_1 = unpack_small(weights_0, at, hidden_width)
    at = 0
    qkv_0, at = unpack(last_weights, at, width, 3 * width)
    sums_0 = unpack_small(last_weights, at, hidden_width)
    sums = jnp.stack([sums_0, sums_1])
    return (
        both_packs(out_kept, out_got[:patch_count]),
        both_packs(out_send[patch_count:], out_got[patch_count:]),
        both_packs(grad_kept_out, grad_got[:patch_count]),
        both_packs(grad_send[patch_count:], grad_got[patch_count:]),
        sums[:, 0, :width],
        sums[:, 1, :width],
        jnp.stack([qkv_0, qkv_1]),
        sums[:, 2, : 2 * width],
        jnp.stack([proj_0, proj_1]),
        sums[:, 3, :width],
        sums[:, 4, :width],
        sums[:, 5, :width],
        jnp.stack([fc1_0, fc1_1]),
        sums[:, 6, :],
        jnp.stack([fc2_0, fc2_1]),
        sums[:, 7, :width],
    )


def solution(mesh):
    rows, one = P("pack", "blk", None), P("pack", None, None)
    in_specs = (rows, one, P("pack", None), P("pack", None)) + (P(),) * 12 + (rows, one)
    out_specs = (rows, one, rows, one) + (P(),) * 12
    return jax.shard_map(
        on_device, mesh=mesh, in_specs=in_specs, out_specs=out_specs, check_vma=False
    )
```

```python
import functools

import jax
import jax.numpy as jnp
from jax import lax
from jax.experimental import pallas as pl
from jax.experimental.pallas import tpu as pltpu
from jax.sharding import PartitionSpec as P

HEADS = 6
HEAD_DIM = 64
LAYERS = 2
PAIRS = HEADS // 2
LANES = 128
SPLITS = 3
BLOCKED = -1e30
NORM_EPS = 1e-06
ROOT_HALF = 0.7071067811865476
INV_ROOT_TWO_PI = 0.3989422804014327
F32 = jnp.float32
LOW = jnp.bfloat16
MIB = 1024 * 1024
ORDER = "acbcbacagbcabcacbGoacbbOcc"
FLOPS_PER_MICRO = 1.1e9
MICROS = {
    "layer_0_forward": 14.0, "layer_1_forward": 15.5, "layer_1_query_grad": 4.0,
    "layer_1_weights": 5.0, "layer_1_key_grad": 14.0, "layer_0_weights": 1.0,
    "layer_0_query_grad": 7.5, "layer_0_key_grad": 1.0, "mix_weights": 2.0, "unpack": 4.0,
    "sum": 10.0,
}


def dot(a, b):
    return jnp.dot(a, b, preferred_element_type=F32)


def dot_nt(a, b):
    return lax.dot_general(a, b, (((1,), (1,)), ((), ())), preferred_element_type=F32)


def dot_tn(a, b):
    return lax.dot_general(a, b, (((0,), (0,)), ((), ())), preferred_element_type=F32)


def lane_ids(rows):
    return lax.broadcasted_iota(jnp.int32, (rows, LANES), 1)


def row_ids(rows, lanes=LANES):
    return lax.broadcasted_iota(jnp.int32, (rows, lanes), 0)


def norm_parts(rows):
    centre = rows - jnp.mean(rows, axis=-1, keepdims=True)
    inverse = lax.rsqrt(jnp.mean(centre * centre, axis=-1, keepdims=True) + NORM_EPS)
    return centre * inverse, inverse


def normed(rows, gain, bias):
    return (norm_parts(rows)[0] * gain + bias).astype(LOW)


def norm_back(grad_out, rows, gain):
    scaled, inverse = norm_parts(rows)
    grad_scaled = grad_out * gain
    grad_rows = inverse * (
        grad_scaled
        - jnp.mean(grad_scaled, axis=-1, keepdims=True)
        - scaled * jnp.mean(grad_scaled * scaled, axis=-1, keepdims=True)
    )
    return grad_rows, scaled


def column_sum(rows):
    return jnp.sum(rows, axis=0, keepdims=True)


class Plan:
    def __init__(self, cycle, patch_count, special_count, image_count):
        self.cycle = cycle
        self.group = cycle // 2
        self.block = patch_count
        self.specials = special_count
        self.images = image_count
        self.patch_rows = cycle * patch_count
        self.special_pad = -(-special_count // LANES) * LANES
        self.rows = self.patch_rows + self.special_pad
        self.own_patch = 2 * patch_count
        self.own = self.own_patch + special_count
        self.extra = image_count + 1
        steps = [c for c in (384, 256, 128) if self.rows % c == 0]
        self.chunk = steps[0]
        self.unroll = PAIRS if self.rows <= 2048 else 1

    def place(self):
        me = lax.axis_index("blk")
        return me // self.group, me % self.group

    def at(self, half, other):
        return pl.multiple_of((half * self.group + other) * self.block, self.block)

    def own_rows(self, ref, place):
        return jnp.concatenate(
            [
                ref[pl.ds(self.at(0, place), self.block), :],
                ref[pl.ds(self.at(1, place), self.block), :],
                ref[self.patch_rows : self.patch_rows + self.specials, :],
            ],
            axis=0,
        )


def image_lanes(plan, lengths, pads, pack):
    lane = lane_ids(1)
    start = jnp.zeros((1, LANES), jnp.int32)
    stop, live = start, start
    so_far = jnp.int32(0)
    for image in range(plan.images):
        start = jnp.where(lane == image, so_far, start)
        so_far = so_far + lengths[pack, image]
        stop = jnp.where(lane == image, so_far, stop)
        live = jnp.where(lane == image, so_far - pads[pack, image], live)
    return start, stop, live


def write_masks(plan, lengths, pads, pack, key_extra, query_extra):
    start, stop, live = image_lanes(plan, lengths, pads, pack)
    count = plan.block
    lane = lane_ids(count)
    one, zero = jnp.ones((count, LANES), F32), jnp.zeros((count, LANES), F32)

    @pl.loop(0, plan.cycle)
    def _(step):
        base = pl.multiple_of(step * count, count)
        token = row_ids(count) + base
        inside = (token >= start) & (token < stop)
        alive = (token >= start) & (token < live)
        key_extra[pl.ds(base, count), :] = jnp.where(alive, zero, one).astype(LOW)
        query_extra[pl.ds(base, count), :] = jnp.where(inside, BLOCKED, zero).astype(LOW)

    count = plan.special_pad
    lane, special = lane_ids(count), row_ids(count)
    one, zero = jnp.ones((count, LANES), F32), jnp.zeros((count, LANES), F32)
    mine = (lane == special // 2) & (special < plan.specials)
    never = (lane == plan.images) & (special >= plan.specials)
    key_extra[plan.patch_rows :, :] = jnp.where(mine, zero, one).astype(LOW)
    query_extra[plan.patch_rows :, :] = jnp.where(mine | never, BLOCKED, zero).astype(LOW)


def project(plan, all_normed, weight, shift, mixed):
    @pl.loop(0, plan.rows // plan.chunk)
    def _(step):
        here = pl.ds(pl.multiple_of(step * plan.chunk, plan.chunk), plan.chunk)
        out = (dot(all_normed[here, :], weight[...]) + shift).astype(LOW)
        for part in range(3 * PAIRS):
            mixed[part, here, :] = out[:, part * LANES : (part + 1) * LANES]


def shift_row(qv_bias):
    width = qv_bias.shape[1] // 2
    return jnp.concatenate(
        [qv_bias[:, :width], jnp.zeros((1, width), F32), qv_bias[:, width:]], axis=1
    )


def attend(plan, place, mixed, key_extra, query_extra, keys, joined, total):
    lane = lane_ids(plan.own)
    own_extra = plan.own_rows(query_extra, place)
    keys[:, LANES:] = key_extra[...]
    total[...] = jnp.zeros_like(total)

    ones = jnp.ones((plan.rows, LANES), LOW)

    @pl.loop(0, PAIRS, unroll=plan.unroll)
    def _(pair):
        query = (plan.own_rows(mixed.at[pair], place).astype(F32) * 0.125).astype(LOW)
        keys[:, :LANES] = mixed[PAIRS + pair]
        values = jnp.concatenate([mixed[2 * PAIRS + pair], ones], axis=1)
        scores, out, logs = [], [], total[...]
        for side in range(2):
            mine = (lane // HEAD_DIM) == side
            left = jnp.concatenate([jnp.where(mine, query, 0), own_extra], axis=1)
            scores.append(dot_nt(left, keys[...]))
        for side in range(2):
            top = jnp.max(scores[side], axis=-1, keepdims=True)
            both = dot(jnp.exp(scores[side] - top).astype(LOW), values)
            out.append(both[:, :LANES] / both[:, LANES:])
            logs = jnp.where(lane == 2 * pair + side, top + jnp.log(both[:, LANES:]), logs)
        joined[pair] = jnp.where(lane < HEAD_DIM, out[0], out[1])
        total[...] = logs


def feed_forward(second_normed, fc1, fc1_bias, fc2, hidden, slope):
    out = None
    width = second_normed.shape[1]
    for first in range(0, fc1.shape[1], width):
        here = slice(first, first + width)
        pre = dot(second_normed, fc1[:, here]) + fc1_bias[:, here]
        cdf = 0.5 * (1.0 + lax.erf(pre * ROOT_HALF))
        pdf = jnp.exp(-0.5 * pre * pre) * INV_ROOT_TWO_PI
        value = (pre * cdf).astype(LOW)
        hidden[:, here] = value
        slope[:, here] = (cdf + pre * pdf).astype(LOW)
        part = dot(value, fc2[here, :])
        out = part if out is None else out + part
    return out


def forward_rest(layer, start, joined, w_proj, proj_bias, ln2_gain, ln2_bias, w_fc1, fc1_bias,
                 w_fc2, fc2_bias, hidden, slope, middle):
    row = slice(layer, layer + 1)
    attended = jnp.concatenate([joined[pair] for pair in range(PAIRS)], axis=1)
    after = start + dot(attended.astype(LOW), w_proj.ready()[...]) + proj_bias[row, :]
    middle[...] = after
    second = normed(after, ln2_gain[row, :], ln2_bias[row, :])
    out = feed_forward(second, w_fc1.ready(), fc1_bias[row, :], w_fc2.ready(), hidden, slope)
    return after + out + fc2_bias[row, :]


def first_kernel(plan, *refs):
    blocks, refs = refs[: 2 * plan.group], refs[2 * plan.group :]
    (lengths, pads, specials, ln1_gain, ln1_bias, w_qkv, qv_bias, w_proj, proj_bias, ln2_gain,
     ln2_bias, w_fc1, fc1_bias, w_fc2, fc2_bias,
     key_extra, query_extra, mixed, start, middle, joined, total, hidden, slope, after, send, keep,
     own_normed, next_normed, all_normed, keys) = refs
    half, place = plan.place()
    gain, bias = ln1_gain[0:1, :], ln1_bias[0:1, :]
    for index, ref in enumerate(blocks):
        side = half if index < plan.group else 1 - half
        other = jnp.bitwise_xor(place, index % plan.group)
        rows = ref[...].astype(F32)
        all_normed[pl.ds(plan.at(side, other), plan.block), :] = normed(rows, gain, bias)
        if index % plan.group == 0:
            start[pl.ds(pl.multiple_of(side * plan.block, plan.block), plan.block), :] = rows
    rows = specials[half].astype(F32)
    start[plan.own_patch :, :] = rows
    all_normed[plan.patch_rows :, :] = jnp.zeros((plan.special_pad, rows.shape[1]), LOW)
    all_normed[plan.patch_rows : plan.patch_rows + plan.specials, :] = normed(rows, gain, bias)
    write_masks(plan, lengths, pads, half, key_extra, query_extra)
    project(plan, all_normed, w_qkv.ready(), shift_row(qv_bias[0:1, :]), mixed)
    attend(plan, place, mixed, key_extra, query_extra, keys, joined, total)
    joined.send()
    out = forward_rest(0, start[...], joined, w_proj, proj_bias, ln2_gain, ln2_bias, w_fc1,
                       fc1_bias, w_fc2, fc2_bias, hidden, slope, middle)
    for ref in (middle, slope):
        ref.send()
    after[...] = out
    following = normed(out, ln1_gain[1:2, :], ln1_bias[1:2, :])
    send[...] = following[: plan.own_patch]
    keep[...] = following[plan.own_patch :]
    next_normed[...] = following
    own_normed[...] = plan.own_rows(all_normed, place)


def split_low(values):
    parts, rest = [], values
    for _ in range(SPLITS):
        part = rest.astype(LOW)
        parts.append(part)
        rest = rest - part.astype(F32)
    return parts


def backward_rest(plan, layer, grad_rows, scale, middle, joined, total, hidden, slope, ln2_gain,
                  ln2_bias, w_fc1, w_fc2, w_proj, small, second, second_grad, pre_grad,
                  attended_low, first_grad, send, out_grad, logs):
    row = slice(layer, layer + 1)
    width = grad_rows.shape[1]
    low_grad = grad_rows.astype(LOW)
    second_grad[...] = low_grad
    after = middle[...]
    second[...] = normed(after, ln2_gain[row, :], ln2_bias[row, :])
    grad_second = None
    for first in range(0, slope.shape[1], width):
        here = slice(first, first + width)
        value = (dot_nt(low_grad, w_fc2.ready()[here, :]) * slope[:, here].astype(F32)).astype(LOW)
        pre_grad[:, here] = value
        small[6:7, here] = column_sum(value.astype(F32) * scale)
        part = dot_nt(value, w_fc1.ready()[:, here])
        grad_second = part if grad_second is None else grad_second + part
    change, scaled = norm_back(grad_second, after, ln2_gain[row, :])
    weighted = grad_second * scale
    grad_middle = grad_rows + change
    low_middle = grad_middle.astype(LOW)
    first_grad[...] = low_middle
    small[3:4, :width] = column_sum(low_middle.astype(F32) * scale)
    small[4:5, :width] = column_sum(weighted * scaled)
    small[5:6, :width] = column_sum(weighted)
    small[7:8, :width] = column_sum(low_grad.astype(F32) * scale)
    grad_out = dot_nt(low_middle, w_proj.ready()[...]).astype(LOW)
    out_grad[...] = grad_out
    lane = lane_ids(plan.own)
    table = total[...]
    for pair in range(PAIRS):
        here = slice(pair * LANES, (pair + 1) * LANES)
        attended = joined[pair]
        attended_low[:, here] = attended.astype(LOW)
        product = grad_out[:, here].astype(F32) * attended
        for side in range(2):
            mine = (lane // HEAD_DIM) == side
            delta = jnp.sum(jnp.where(mine, product, 0.0), axis=-1, keepdims=True)
            table = jnp.where(lane == HEADS + 2 * pair + side, delta, table)
    logs[...] = table
    send[: plan.own_patch, :] = grad_out[: plan.own_patch]
    pick = jnp.where(row_ids(16) == lane_ids(16), 1.0, 0.0).astype(LOW)
    parts = split_low(table)
    for part in range(2):
        rows = slice(part * plan.block, (part + 1) * plan.block)
        turned = [dot_nt(pick, values[rows]).astype(LOW) for values in parts]
        first = plan.own_patch + 16 * part
        send[first : first + 16, :] = jnp.concatenate(turned, axis=1)
    return grad_middle


def owner_scale(plan, place):
    row = lax.broadcasted_iota(jnp.int32, (plan.own, 1), 0)
    return jnp.where((row < plan.own_patch) | (place == 0), 1.0, 0.0)


def second_kernel(plan, *refs):
    pieces, refs = refs[: plan.group], refs[plan.group :]
    (normed_specials, key_extra, query_extra, start, grad_kept, grad_swapped, grad_specials,
     ln1_gain, w_qkv, qv_bias, w_proj, proj_bias, ln2_gain, ln2_bias, w_fc1, fc1_bias, w_fc2,
     fc2_bias,
     mixed, out_kept, out_send, grad_middle, send, out_grad, logs, small, second, second_grad,
     pre_grad, attended_low, first_grad, hidden,
     all_normed, keys, joined, total, slope, middle) = refs
    half, place = plan.place()
    gather_normed(plan, place, pieces, normed_specials, all_normed)
    project(plan, all_normed, w_qkv.ready(), shift_row(qv_bias[1:2, :]), mixed)
    attend(plan, place, mixed, key_extra, query_extra, keys, joined, total)
    out = forward_rest(1, start[...], joined, w_proj, proj_bias, ln2_gain, ln2_bias, w_fc1,
                       fc1_bias, w_fc2, fc2_bias, hidden, slope, middle)
    low_out = out.astype(LOW)
    first, later = low_out[: plan.block], low_out[plan.block : plan.own_patch]
    out_kept[...] = jnp.where(half == 0, first, later)
    out_send[: plan.block, :] = jnp.where(half == 0, later, first)
    out_send[plan.block :, :] = low_out[plan.own_patch :]
    kept, swapped = grad_kept[...].astype(F32), grad_swapped[...].astype(F32)
    own_extra = plan.own_rows(key_extra, place)[: plan.own_patch].astype(F32)
    lane = lane_ids(plan.own_patch)
    live = jnp.sum(jnp.where(lane < plan.images, 1.0 - own_extra, 0.0), axis=-1, keepdims=True)
    patch_grad = jnp.concatenate(
        [jnp.where(half == 0, kept, swapped), jnp.where(half == 0, swapped, kept)], axis=0
    )
    grad_rows = jnp.concatenate([patch_grad * live, grad_specials[half].astype(F32)], axis=0)
    small[0:3, :] = jnp.zeros((3, small.shape[1]), F32)
    grad_middle[...] = backward_rest(
        plan, 1, grad_rows, owner_scale(plan, place), middle, joined, total, hidden, slope,
        ln2_gain, ln2_bias, w_fc1, w_fc2, w_proj, small, second, second_grad, pre_grad,
        attended_low, first_grad, send, out_grad, logs)


def gather_normed(plan, place, pieces, normed_specials, all_normed):
    for index, ref in enumerate(pieces):
        other = jnp.bitwise_xor(place, index)
        for half in range(2):
            all_normed[pl.ds(plan.at(half, other), plan.block), :] = ref[
                half * plan.block : (half + 1) * plan.block, :
            ]
    width = all_normed.shape[1]
    all_normed[plan.patch_rows :, :] = jnp.zeros((plan.special_pad, width), LOW)
    all_normed[plan.patch_rows : plan.patch_rows + plan.specials, :] = normed_specials[...]


def placed(plan, rows, first_row, first_lane):
    row, lane = row_ids(rows), lane_ids(rows)
    out = []
    for split in range(SPLITS):
        head = row - first_row
        hit = (head >= 0) & (head < HEADS) & (lane == first_lane + SPLITS * head + split)
        out.append(jnp.where(hit, -1.0, 0.0).astype(LOW))
    return out


def spread_logs(plan, table, first_row):
    picks = placed(plan, LANES, first_row, plan.extra)
    return sum(dot(values, pick) for values, pick in zip(split_low(table), picks)).astype(LOW)


def head_lanes(plan, lane, head):
    first = plan.extra + SPLITS * head
    return (lane >= first) & (lane < first + SPLITS)


def query_grad_kernel(plan, mixed, key_extra, query_extra, out_grad, logs, grad_query, keys, values):
    _, place = plan.place()
    lane = lane_ids(plan.own)
    own_extra = plan.own_rows(query_extra, place)
    log_extra = spread_logs(plan, logs[...], 0)
    delta_extra = spread_logs(plan, logs[...], HEADS)
    keys[:, LANES:] = key_extra[...]
    values[:, LANES:] = key_extra[...]

    @pl.loop(0, PAIRS, unroll=plan.unroll)
    def _(pair):
        query = (plan.own_rows(mixed.at[pair], place).astype(F32) * 0.125).astype(LOW)
        here = pl.ds(pl.multiple_of(pair * LANES, LANES), LANES)
        grad_out = out_grad[:, here]
        keys[:, :LANES] = mixed[PAIRS + pair]
        values[:, :LANES] = mixed[2 * PAIRS + pair]
        out = []
        for side in range(2):
            mine = (lane // HEAD_DIM) == side
            head = head_lanes(plan, lane, 2 * pair + side)
            left = jnp.concatenate(
                [jnp.where(mine, query, 0), jnp.where(head, log_extra, own_extra)], axis=1
            )
            probs = jnp.exp(dot_nt(left, keys[...]))
            left = jnp.concatenate(
                [jnp.where(mine, grad_out, 0), jnp.where(head, delta_extra, 0)], axis=1
            )
            grad_scores = (probs * dot_nt(left, values[...])).astype(LOW)
            out.append(dot(grad_scores, mixed[PAIRS + pair]) * 0.125)
        grad_query[:, here] = jnp.where(lane < HEAD_DIM, out[0], out[1]).astype(LOW)


def key_grads(plan, place, pieces, mixed, key_extra, query_extra, out_grad, logs, grad_mixed,
              queries, grads, all_grads):
    log_rows = placed(plan, 16, 0, plan.extra)
    delta_rows = placed(plan, 16, HEADS, plan.extra)
    picks = [jnp.concatenate(two, axis=1) for two in zip(log_rows, delta_rows)]
    for index, ref in enumerate(pieces):
        other = jnp.bitwise_xor(place, index)
        for half in range(2):
            here = pl.ds(plan.at(half, other), plan.block)
            for pair in range(PAIRS):
                all_grads[pair, here, :] = ref[
                    half * plan.block : (half + 1) * plan.block, pair * LANES : (pair + 1) * LANES
                ]
            first = plan.own_patch + 16 * half
            both = sum(
                dot_tn(ref[first : first + 16, split * LANES : (split + 1) * LANES], picks[split])
                for split in range(SPLITS)
            )
            queries[here, LANES:] = (both[:, :LANES] + query_extra[here, :].astype(F32)).astype(LOW)
            grads[here, LANES:] = both[:, LANES:].astype(LOW)
    last, stop = plan.patch_rows, plan.patch_rows + plan.specials
    table = logs[plan.own_patch :, :]
    log_extra = spread_logs(plan, table, 0).astype(F32)
    queries[last:, LANES:] = query_extra[last:, :]
    queries[last:stop, LANES:] = (log_extra + query_extra[last:stop, :].astype(F32)).astype(LOW)
    grads[last:, LANES:] = jnp.zeros((plan.special_pad, LANES), LOW)
    grads[last:stop, LANES:] = spread_logs(plan, table, HEADS)
    for pair in range(PAIRS):
        all_grads[pair, last:, :] = jnp.zeros((plan.special_pad, LANES), LOW)
        all_grads[pair, last:stop, :] = out_grad[
            plan.own_patch :, pair * LANES : (pair + 1) * LANES
        ]
    lane = lane_ids(plan.own)
    own_extra = plan.own_rows(key_extra, place)
    own_extra = jnp.where(lane < plan.extra, own_extra, 0)

    @pl.loop(0, PAIRS)
    def _(pair):
        queries[:, :LANES] = (mixed[pair].astype(F32) * 0.125).astype(LOW)
        grads[:, :LANES] = all_grads[pair]
        key = plan.own_rows(mixed.at[PAIRS + pair], place)
        value = plan.own_rows(mixed.at[2 * PAIRS + pair], place)
        grad_key, grad_value = [], []
        for side in range(2):
            mine = (lane // HEAD_DIM) == side
            head = head_lanes(plan, lane, 2 * pair + side)
            extra = jnp.where(head, 1.0, own_extra.astype(F32)).astype(LOW)
            left = jnp.concatenate([jnp.where(mine, key, 0), extra], axis=1)
            probs = jnp.exp(dot_nt(left, queries[...]))
            left = jnp.concatenate([jnp.where(mine, value, 0), extra], axis=1)
            grad_scores = (probs * dot_nt(left, grads[...])).astype(LOW)
            grad_key.append(dot(grad_scores, queries[:, :LANES]))
            grad_value.append(dot(probs.astype(LOW), all_grads[pair]))
        width = PAIRS * LANES
        here = pl.ds(pl.multiple_of(width + pair * LANES, LANES), LANES)
        grad_mixed[:, here] = jnp.where(lane < HEAD_DIM, *grad_key).astype(LOW)
        here = pl.ds(pl.multiple_of(2 * width + pair * LANES, LANES), LANES)
        grad_mixed[:, here] = jnp.where(lane < HEAD_DIM, *grad_value).astype(LOW)


def first_norm_back(plan, layer, scale, grad_mixed, w_qkv, start, ln1_gain, small):
    width = start.shape[1]
    mixed = grad_mixed[...]
    sums = column_sum(mixed.astype(F32) * scale)
    small[2:3, : 2 * width] = jnp.concatenate([sums[:, :width], sums[:, 2 * width :]], axis=1)
    grad_normed = dot_nt(mixed, w_qkv.ready()[...])
    change, scaled = norm_back(grad_normed, start[...], ln1_gain[layer : layer + 1, :])
    weighted = grad_normed * scale
    small[0:1, :width] = column_sum(weighted * scaled)
    small[1:2, :width] = column_sum(weighted)
    return change


def third_kernel(plan, *refs):
    pieces, refs = refs[: plan.group], refs[plan.group :]
    (mixed, key_extra, query_extra, later_grad, later_logs, grad_query, later_start, later_middle,
     later_small, ln1_gain, later_qkv,
     middle, joined, total, hidden, slope, ln2_gain, ln2_bias, w_fc1, w_fc2, w_proj,
     grad_mixed, small_out, grad_middle, send, out_grad, logs, small, second, second_grad,
     pre_grad, attended_low, first_grad,
     queries, grads, all_grads) = refs
    _, place = plan.place()
    scale = owner_scale(plan, place)
    grad_mixed[:, : grad_query.shape[1]] = grad_query[...]
    key_grads(plan, place, pieces, mixed, key_extra, query_extra, later_grad, later_logs,
              grad_mixed, queries, grads, all_grads)
    small_out[...] = later_small[...]
    grad_rows = later_middle[...] + first_norm_back(
        plan, 1, scale, grad_mixed, later_qkv, later_start, ln1_gain, small_out
    )
    small[0:3, :] = jnp.zeros((3, small.shape[1]), F32)
    grad_middle[...] = backward_rest(
        plan, 0, grad_rows, scale, middle, joined, total, hidden, slope, ln2_gain, ln2_bias,
        w_fc1, w_fc2, w_proj, small, second, second_grad, pre_grad, attended_low, first_grad,
        send, out_grad, logs)


def fourth_kernel(plan, *refs):
    pieces, refs = refs[: plan.group], refs[plan.group :]
    (mixed, key_extra, query_extra, out_grad, logs, grad_query, start, grad_middle, small, ln1_gain,
     w_qkv,
     grad_mixed, small_out, grad_kept, grad_send,
     queries, grads, all_grads) = refs
    half, place = plan.place()
    scale = owner_scale(plan, place)
    grad_mixed[:, : grad_query.shape[1]] = grad_query[...]
    key_grads(plan, place, pieces, mixed, key_extra, query_extra, out_grad, logs, grad_mixed,
              queries, grads, all_grads)
    small_out[...] = small[...]
    out = grad_middle[...] + first_norm_back(
        plan, 0, scale, grad_mixed, w_qkv, start, ln1_gain, small_out
    )
    first, later = out[: plan.block], out[plan.block : plan.own_patch]
    grad_kept[...] = jnp.where(half == 0, first, later)
    grad_send[: plan.block, :] = jnp.where(half == 0, later, first)
    grad_send[plan.block :, :] = out[plan.own_patch :]


def weight_kernel(plan, count, small_count, used, *refs):
    kept, sent, out = refs[-3:]
    place = plan.place()[1]
    keep = owner_scale(plan, place)
    at = 0
    for index in range(count):
        left = (refs[2 * index][...].astype(F32) * keep).astype(LOW)
        right = refs[2 * index + 1]
        step = min(384, right.shape[1])
        for first in range(0, right.shape[1], step):
            product = dot_tn(left, right[:, first : first + step]).astype(LOW)
            for column in range(0, step, LANES):
                out[at : at + left.shape[1], :] = product[:, column : column + LANES]
                at += left.shape[1]
    for ref in refs[2 * count : 2 * count + small_count]:
        small = ref[...]
        for column in range(0, small.shape[1], 2 * LANES):
            two = [small[:, column : column + LANES], small[:, column + LANES : column + 2 * LANES]]
            out[at : at + 16, :] = jnp.concatenate(two, axis=0).astype(LOW)
            at += 16
    if used < out.shape[0]:
        out[used:, :] = jnp.zeros((out.shape[0] - used, LANES), LOW)
    size = kept.shape[0]
    core = lax.axis_index("blk") % 2
    kept[...] = out[pl.ds(pl.multiple_of(core * size, 16), size), :]
    sent[...] = out[pl.ds(pl.multiple_of((1 - core) * size, 16), size), :]


def side_of(axis, bits):
    place = lax.axis_index("blk")
    bit = jnp.where(place % 2 == 0, bits[0], bits[1])
    if axis == "blk":
        return (place >> bit) & 1
    return (lax.axis_index("pack") >> bit) & 1


def split_kernel(axis, bits, mine, got, kept, sent):
    size = kept.shape[0]
    side = side_of(axis, bits)
    for which, out in ((side, kept), (1 - side, sent)):
        here = pl.ds(pl.multiple_of(which * size, 16), size)
        out[...] = (mine[here, :].astype(F32) + got[here, :].astype(F32)).astype(LOW)


def add_kernel(mine, got, out):
    out[...] = (mine[...].astype(F32) + got[...].astype(F32)).astype(LOW)


def join_kernel(axis, bits, mine, got, out):
    size = mine.shape[0]
    side = side_of(axis, bits)
    out[pl.ds(pl.multiple_of(side * size, 16), size), :] = mine[...]
    out[pl.ds(pl.multiple_of((1 - side) * size, 16), size), :] = got[...]


def unpack_kernel(entries, stacked, filled, width, *refs):
    own, got = refs[0], refs[1]
    outs = refs[2 + filled :]
    rows, semaphores = outs[-2], outs[-1]
    buffers = outs[len(outs) - 2 - len(entries) : -2]
    core = lax.axis_index("blk") % 2
    size = own.shape[0]
    rows[pl.ds(pl.multiple_of(core * size, 16), size), :] = own[...]
    rows[pl.ds(pl.multiple_of((1 - core) * size, 16), size), :] = got[...]
    at, copies = 0, []
    for number, (output, layer, height, columns) in enumerate(entries):
        buffer = buffers[number]
        for first in range(0, columns, LANES):
            buffer[:, first : first + LANES] = rows[at : at + height, :].astype(F32)
            at += height
        copies.append(
            pltpu.make_async_copy(buffer, outs[output].at[layer], semaphores.at[number])
        )
        copies[-1].start()
    if width:
        small = []
        for _ in range(LAYERS):
            blocks = []
            for _ in range(width // (2 * LANES)):
                both = rows[at : at + 16, :].astype(F32)
                blocks += [both[:8], both[8:]]
                at += 16
            small.append(jnp.concatenate(blocks, axis=1))
        for row, out in enumerate(outs[stacked : stacked + 8]):
            columns = out.shape[1]
            out[...] = jnp.concatenate([part[row : row + 1, :columns] for part in small], axis=0)
    for copy in copies:
        copy.wait()


VMEM = pl.BlockSpec(memory_space=pltpu.VMEM)


ANY = pl.BlockSpec(memory_space=pl.ANY)
HBM = pl.BlockSpec(memory_space=pltpu.HBM)


WHOLE = -1


class Staged:
    def __init__(self, source, layer, target, semaphore):
        self.target = target
        source = source if layer == WHOLE else source.at[layer]
        self.copy = pltpu.make_async_copy(source, target, semaphore)
        self.copy.start()
        self.waits = True

    def ready(self):
        if self.waits:
            self.copy.wait()
            self.waits = False
        return self.target

    @property
    def shape(self):
        return self.target.shape

    def __getitem__(self, index):
        return self.ready()[index]


class Late:
    def __init__(self, out, buffer, semaphore):
        self.buffer, self.copy, self.sent = buffer, pltpu.make_async_copy(buffer, out, semaphore), False

    @property
    def shape(self):
        return self.buffer.shape

    def __getitem__(self, index):
        return self.buffer[index]

    def __setitem__(self, index, value):
        self.buffer[index] = value

    def send(self):
        self.copy.start()
        self.sent = True

    def finish(self):
        if not self.sent:
            self.send()
        self.copy.wait()


def staged_kernel(kernel, layers, out_count, late, *refs):
    ins, outs = list(refs[: len(layers)]), list(refs[len(layers) : len(layers) + out_count])
    rest = refs[len(layers) + out_count :]
    chosen = [index for index, layer in enumerate(layers) if layer is not None]
    if not chosen and not late:
        return kernel(*refs)
    count = len(chosen) + len(late)
    buffers, semaphores = rest[:count], rest[count]
    for number, index in enumerate(chosen):
        ins[index] = Staged(ins[index], layers[index], buffers[number], semaphores.at[number])
    for number, index in enumerate(late, len(chosen)):
        outs[index] = Late(outs[index], buffers[number], semaphores.at[number])
    kernel(*ins, *outs, *rest[count + 1 :])
    for index in late:
        outs[index].finish()
    for index in chosen:
        ins[index].ready()


def run(kernel, name, outs, ins, scratch=(), far_outs=(), aliases=None, plain=(), mib=12,
        late=()):
    micros = MICROS.get(name) or MICROS["unpack" if name.startswith("unpack") else "sum"]
    specs, values, layers, buffers = [], [], [], []
    far_ins = set(aliases or ())
    for index, item in enumerate(ins):
        value, layer = item if isinstance(item, tuple) else (item, None)
        if layer is not None:
            specs.append(HBM)
        elif index in far_ins:
            specs.append(ANY)
        else:
            specs.append(VMEM)
        if layer is not None:
            space = pltpu.SMEM if value.dtype == jnp.int32 else pltpu.VMEM
            buffers.append(space(value.shape[0 if layer == WHOLE else 1 :], value.dtype))
            value = pltpu.with_memory_space_constraint(value, pltpu.HBM)
        layers.append(layer)
        values.append(value)
    buffers += [pltpu.VMEM(*outs[index]) for index in late]
    if buffers:
        buffers.append(pltpu.SemaphoreType.DMA((len(buffers),)))
    return pl.pallas_call(
        functools.partial(staged_kernel, kernel, layers, len(outs), late),
        out_shape=[
            (pltpu.HBM if index in late else jax.ShapeDtypeStruct)(shape, kind)
            for index, (shape, kind) in enumerate(outs)
        ],
        in_specs=specs,
        out_specs=[
            HBM if index in late else ANY if index in far_outs else VMEM for index in range(len(outs))
        ],
        scratch_shapes=buffers + [pltpu.VMEM(shape, kind) for shape, kind in scratch] + list(plain),
        input_output_aliases=aliases or {},
        compiler_params=pltpu.CompilerParams(vmem_limit_bytes=mib * MIB),
        cost_estimate=pl.CostEstimate(
            flops=int(micros * FLOPS_PER_MICRO), bytes_accessed=0, transcendentals=0
        ),
        name=name,
    )(*values)


def swap(value, mask):
    size = lax.axis_size("blk")
    return lax.ppermute(value, "blk", [(i, i ^ mask) for i in range(size)])


def spread(value, group, then=None):
    held = {0: value}
    mask = group // 2
    if then is not None:
        held[mask] = swap(value, mask)
        (held[0], held[mask]), then = tie([held[0], held[mask]], then)
        mask //= 2
    while mask:
        for index, item in list(held.items()):
            held[index | mask] = swap(item, mask)
        mask //= 2
    pieces = [held[index] for index in range(group)]
    return pieces if then is None else (pieces, then)


def exchange(value, axis, bits):
    masks = [1 << bit for bit in bits]
    cycle = lax.axis_size("blk")
    pairs = []
    for device in range(lax.axis_size("pack") * cycle):
        pack, place = divmod(device, cycle)
        mask = masks[place % 2]
        other = (pack, place ^ mask) if axis == "blk" else (pack ^ mask, place)
        pairs.append((device, other[0] * cycle + other[1]))
    return lax.ppermute(value, ("pack", "blk"), pairs)


def tie(*groups):
    return lax.optimization_barrier(groups)


class Summing:
    def __init__(self, name, kept, sent):
        self.name = name
        self.values = [kept, swap(sent, 1)]
        chips = list(range(1, lax.axis_size("blk").bit_length() - 1))
        packs = list(range(lax.axis_size("pack").bit_length() - 1))
        parts = [("blk", pair) for pair in zip(chips, reversed(chips))]
        parts += [("pack", (bit, bit)) for bit in packs[:-1]]
        self.steps = [("split", part, part) for part in parts]
        self.steps += [("add", None, ("pack", (packs[-1], packs[-1]))), ("add", None, parts[-1])]
        for part, then in zip(parts[::-1], parts[-2::-1] + [None]):
            self.steps.append(("join", part, then))

    def after(self, *others):
        tied = tie(self.values, list(others))
        self.values = tied[0]
        return tied[1] if len(others) > 1 else tied[1][0]

    def step(self, last=None):
        if last is not None:
            self.after(last)
        kind, part, then = self.steps.pop(0)
        name = f"{self.name}_{kind}{len(self.steps)}"
        size = self.values[0].shape[0]
        shape = lambda count: ((count, LANES), LOW)
        if kind == "split":
            kernel = functools.partial(split_kernel, *part)
            mine, sent = run(kernel, name, [shape(size // 2)] * 2, self.values)
        elif kind == "add":
            mine = sent = run(add_kernel, name, [shape(size)], self.values)[0]
        else:
            kernel = functools.partial(join_kernel, *part)
            mine = sent = run(kernel, name, [shape(2 * size)], self.values)[0]
        self.values = [mine, swap(sent, 1) if then is None else exchange(sent, *then)]
        return mine


def unpacked(name, values, entries, shapes, filled, width=0, sums=()):
    ins = list(values) + [filled[k] for k in sorted(filled)]
    aliases = {2 + index: output for index, output in enumerate(sorted(filled))}
    outs = [(shape, F32) for shape in shapes] + list(sums)
    half = values[0].shape[0]
    scratch = [((rows, columns), F32) for _, _, rows, columns in entries] + [((2 * half, LANES), LOW)]
    kernel = functools.partial(unpack_kernel, entries, len(shapes), len(filled), width)
    return run(kernel, name, outs, ins, scratch, set(range(len(shapes))), aliases,
               [pltpu.SemaphoreType.DMA((len(entries),))], 24)


def on_device(patches, specials, image_lengths, pad_counts, ln1_gain, ln1_bias, w_qkv, qv_bias,
              w_proj, proj_bias, ln2_gain, ln2_bias, w_fc1, fc1_bias, w_fc2, fc2_bias, d_patches,
              d_specials):
    ln1, ln1_shift, ln2, ln2_shift = [(v, WHOLE) for v in (ln1_gain, ln1_bias, ln2_gain, ln2_bias)]
    qv_shift, proj_shift = (qv_bias, WHOLE), (proj_bias, WHOLE)
    fc1_shift, fc2_shift = (fc1_bias, WHOLE), (fc2_bias, WHOLE)
    cycle, pack_size = lax.axis_size("blk"), lax.axis_size("pack")
    patch_count, special_count, width = patches.shape[1], specials.shape[1], patches.shape[2]
    hidden_width = w_fc1.shape[2]
    plan = Plan(cycle, patch_count, special_count, image_lengths.shape[1])
    own, rows, group = plan.own, plan.rows, plan.group
    half = lax.axis_index("blk") // group

    def kept_and_sent(pair):
        return (lax.dynamic_index_in_dim(pair, half, 0, keepdims=False),
                lax.dynamic_index_in_dim(pair, 1 - half, 0, keepdims=False))

    def both_packs(kept, got):
        return jnp.stack([jnp.where(half == 0, kept, got), jnp.where(half == 0, got, kept)])

    kept, sent = kept_and_sent(patches)
    blocks = spread(kept, group) + spread(swap(sent, group), group)
    grad_kept, grad_sent = kept_and_sent(d_patches)
    grad_swapped = swap(grad_sent, group)

    blocks, (grad_swapped,) = tie(blocks, [grad_swapped])
    mib = max(12, rows // 90)
    more = max(26, rows // 90)
    extra_shape = ((rows, LANES), LOW)
    mixed_shape = ((3 * PAIRS, rows, LANES), LOW)
    joined_shape = ((PAIRS, own, LANES), F32)
    wide, wide_low = ((own, width), F32), ((own, width), LOW)
    hidden_shape, slope_shape = ((own, hidden_width), LOW), ((own, hidden_width), LOW)
    table_shape = ((own, LANES), F32)
    small_shape = ((8, hidden_width), F32)
    send_shape = ((plan.own_patch + 32, width), LOW)
    normed_shape = ((rows, width), LOW)
    double_shape = ((rows, 2 * LANES), LOW)
    all_grads_shape = ((PAIRS, rows, LANES), LOW)

    def weights(name, products, small=()):
        sizes = [(a[0] if isinstance(a, tuple) else a).shape[1] * b.shape[1] for a, b in products]
        used = sum(sizes) // LANES
        small = list(small)
        used += len(small) * 8 * hidden_width // LANES
        multiple = 16 * cycle * pack_size
        total = -(-used // multiple) * multiple
        flat = [x for pair in products for x in pair] + small
        kernel = functools.partial(weight_kernel, plan, len(products), len(small), used)
        half_rows = ((total // 2, LANES), LOW)
        return run(kernel, name, [half_rows, half_rows], flat, [((total, LANES), LOW)], mib=mib)

    def query_grad(name, mixed, out_grad, logs):
        kernel = functools.partial(query_grad_kernel, plan)
        ins = [mixed, key_extra, query_extra, out_grad, logs]
        return run(kernel, name, [wide_low], ins, [double_shape, double_shape], mib=more)[0]

    (key_extra, query_extra, mixed_0, start_0, middle_0, joined_0, total_0, hidden_0, slope_0,
     start_1, send, normed_specials, normed_0, normed_1) = run(
        functools.partial(first_kernel, plan), "layer_0_forward",
        [extra_shape, extra_shape, mixed_shape, wide, wide, joined_shape, table_shape, hidden_shape,
         slope_shape, wide, ((plan.own_patch, width), LOW), ((special_count, width), LOW), wide_low,
         wide_low],
        blocks + [(image_lengths, WHOLE), (pad_counts, WHOLE), (specials, WHOLE), ln1, ln1_shift,
                  (w_qkv, 0), qv_shift, (w_proj, 0), proj_shift, ln2, ln2_shift, (w_fc1, 0),
                  fc1_shift, (w_fc2, 0), fc2_shift],
        [normed_shape, double_shape], mib=more, late=(4, 5, 8))
    middle_0, joined_0, slope_0 = [(v, WHOLE) for v in (middle_0, joined_0, slope_0)]
    pieces = spread(send, group)
    (mixed_1, out_kept, out_send, grad_middle_1, send, out_grad_1, logs_1, small_1, second_1,
     second_grad_1, pre_grad_1, attended_1, first_grad_1, hidden_1) = run(
        functools.partial(second_kernel, plan), "layer_1_forward",
        [mixed_shape, ((patch_count, width), LOW), ((patch_count + special_count, width), LOW),
         wide, send_shape, wide_low, table_shape, small_shape, wide_low, wide_low, hidden_shape,
         wide_low, wide_low, hidden_shape],
        pieces + [normed_specials, key_extra, query_extra, start_1, grad_kept, grad_swapped,
                  (d_specials, WHOLE), ln1, (w_qkv, 1), qv_shift, (w_proj, 1), proj_shift, ln2,
                  ln2_shift, (w_fc1, 1), fc1_shift, (w_fc2, 1), fc2_shift],
        [normed_shape, double_shape, joined_shape, table_shape, slope_shape, wide], mib=more)
    grad_query_1 = query_grad("layer_1_query_grad", mixed_1, out_grad_1, logs_1)
    later_pieces, (grad_query_1,) = spread(send, group, [grad_query_1])
    (second_grad_1,), (grad_query_1,) = tie([second_grad_1], [grad_query_1])
    halves = weights(
        "layer_1_weights",
        [(hidden_1, second_grad_1), (second_1, pre_grad_1), (attended_1, first_grad_1)],
    )
    first_sum = Summing("first_sum", *halves)
    first_sum.step()
    (grad_query_1,), _ = tie([grad_query_1], first_sum.values[:1])
    (grad_mixed_1, small_1, grad_middle_0, send, out_grad_0, logs_0, small_0, second_0,
     second_grad_0, pre_grad_0, attended_0, first_grad_0) = run(
        functools.partial(third_kernel, plan), "layer_1_key_grad",
        [((own, 3 * width), LOW), small_shape, wide, send_shape, wide_low, table_shape, small_shape,
         wide_low, wide_low, hidden_shape, wide_low, wide_low],
        later_pieces + [mixed_1, key_extra, query_extra, out_grad_1, logs_1, grad_query_1, start_1,
                        grad_middle_1, small_1, ln1, (w_qkv, 1), middle_0, joined_0, total_0,
                        hidden_0, slope_0, ln2, ln2_shift, (w_fc1, 0), (w_fc2, 0), (w_proj, 0)],
        [double_shape, double_shape, all_grads_shape], mib=mib)
    out_grad_0 = first_sum.after(out_grad_0)
    last = first_sum.step()
    second_grad_0 = tie([second_grad_0], [last])[0][0]
    halves = weights(
        "layer_0_weights",
        [(hidden_0, second_grad_0), (second_0, pre_grad_0), (attended_0, first_grad_0)])
    later_pieces, halves = spread(send, group, list(halves))
    second_sum = Summing("second_sum", *halves)
    (out_grad_0,), _ = tie([out_grad_0], halves)
    grad_query_0 = query_grad("layer_0_query_grad", mixed_0, out_grad_0, logs_0)
    last = first_sum.step(grad_query_0)
    last = second_sum.step(last)
    (grad_query_0,), _ = tie([grad_query_0], [last])
    grad_mixed_0, small_0, grad_kept_out, grad_send = run(
        functools.partial(fourth_kernel, plan), "layer_0_key_grad",
        [((own, 3 * width), LOW), small_shape, ((patch_count, width), F32),
         ((patch_count + special_count, width), F32)],
        later_pieces + [mixed_0, key_extra, query_extra, out_grad_0, logs_0, grad_query_0, start_0,
                        grad_middle_0, small_0, ln1, (w_qkv, 0)],
        [double_shape, double_shape, all_grads_shape], mib=mib)
    halves = weights(
        "mix_weights", [(normed_0, grad_mixed_0), (normed_1, grad_mixed_1)], (small_0, small_1)
    )
    last = second_sum.step(halves[0])
    last_sum = Summing("last_sum", *tie(list(halves), [last])[0])
    fc2_shape, fc1_shape, proj_shape = w_fc2.shape, w_fc1.shape, w_proj.shape
    entries = [(0,) + fc2_shape[1:], (1,) + fc1_shape[1:], (2,) + proj_shape[1:]]
    stacked = {}
    sums = {"a": (first_sum, 1, "unpack_first"), "b": (second_sum, 0, "unpack_second")}
    order = list(ORDER) + ["a", "b", "c"] * 9
    while order:
        which = order.pop(0)
        if which == "c" and last_sum.steps:
            last = last_sum.step(last)
        elif which == "g":
            grad_got = swap(tie([grad_send], [last])[0][0], group)
        elif which == "o":
            out_got = swap(tie([out_send], [last])[0][0], group)
        elif which == "G":
            grad_got = last_sum.after(grad_got)
        elif which == "O":
            out_got = last_sum.after(out_got)
        elif which in sums:
            this, layer, name = sums[which]
            if this.steps:
                last = this.step(last)
                continue
            del sums[which]
            this.after(last)
            where = [(output, layer, *shape) for output, *shape in entries]
            shapes = [fc2_shape, fc1_shape, proj_shape]
            stacked = dict(enumerate(unpacked(name, this.values, where, shapes, stacked)))
            last = stacked[2]
    fc2, fc1, proj = stacked[0], stacked[1], stacked[2]
    widths = [width, width, 2 * width, width, width, width, hidden_width, width]
    qkv, *sums = unpacked(
        "unpack_last", last_sum.values, [(0, 0) + w_qkv.shape[1:], (0, 1) + w_qkv.shape[1:]],
        [w_qkv.shape], {}, hidden_width, [((LAYERS, columns), F32) for columns in widths])
    return (
        both_packs(out_kept, out_got[:patch_count]),
        both_packs(out_send[patch_count:], out_got[patch_count:]),
        both_packs(grad_kept_out, grad_got[:patch_count]),
        both_packs(grad_send[patch_count:], grad_got[patch_count:]),
        sums[0], sums[1], qkv, sums[2], proj, sums[3], sums[4], sums[5], fc1, sums[6], fc2, sums[7],
    )


def solution(mesh):
    rows, one = P("pack", "blk", None), P("pack", None, None)
    in_specs = (rows, one, P("pack", None), P("pack", None)) + (P(),) * 12 + (rows, one)
    out_specs = (rows, one, rows, one) + (P(),) * 12
    return jax.shard_map(
        on_device, mesh=mesh, in_specs=in_specs, out_specs=out_specs, check_vma=False
    )
```

```python
import functools

import jax
import jax.numpy as jnp
from jax import lax
from jax.experimental import pallas as pl
from jax.experimental.pallas import tpu as pltpu
from jax.sharding import PartitionSpec as P

HEADS = 6
HEAD_DIM = 64
LAYERS = 2
PAIRS = HEADS // 2
LANES = 128
SPLITS = 3
BLOCKED = -1e30
NORM_EPS = 1e-06
ROOT_HALF = 0.7071067811865476
INV_ROOT_TWO_PI = 0.3989422804014327
F32 = jnp.float32
LOW = jnp.bfloat16
MIB = 1024 * 1024
ORDER = "acbcabcagbcabcGacbocabbOcc"
FLOPS_PER_MICRO = 1.1e9
MICROS = {
    "layer_0_early": 1.0, "layer_1_early": 1.0, "layer_0_forward": 14.0, "layer_1_forward": 15.5, "layer_1_query_grad": 4.0,
    "layer_1_weights": 1.0, "layer_1_key_grad": 14.0, "layer_0_weights": 1.0,
    "layer_0_query_grad": 5.0, "layer_0_key_grad": 1.0, "mix_weights": 2.0, "unpack": 4.0,
    "sum": 10.0,
}


def dot(a, b):
    return jnp.dot(a, b, preferred_element_type=F32)


def dot_nt(a, b):
    return lax.dot_general(a, b, (((1,), (1,)), ((), ())), preferred_element_type=F32)


def dot_tn(a, b):
    return lax.dot_general(a, b, (((0,), (0,)), ((), ())), preferred_element_type=F32)


def lane_ids(rows):
    return lax.broadcasted_iota(jnp.int32, (rows, LANES), 1)


def row_ids(rows, lanes=LANES):
    return lax.broadcasted_iota(jnp.int32, (rows, lanes), 0)


def norm_parts(rows):
    centre = rows - jnp.mean(rows, axis=-1, keepdims=True)
    inverse = lax.rsqrt(jnp.mean(centre * centre, axis=-1, keepdims=True) + NORM_EPS)
    return centre * inverse, inverse


def normed(rows, gain, bias):
    return (norm_parts(rows)[0] * gain + bias).astype(LOW)


def norm_back(grad_out, rows, gain):
    scaled, inverse = norm_parts(rows)
    grad_scaled = grad_out * gain
    grad_rows = inverse * (
        grad_scaled
        - jnp.mean(grad_scaled, axis=-1, keepdims=True)
        - scaled * jnp.mean(grad_scaled * scaled, axis=-1, keepdims=True)
    )
    return grad_rows, scaled


def column_sum(rows):
    return jnp.sum(rows, axis=0, keepdims=True)


class Plan:
    def __init__(self, cycle, patch_count, special_count, image_count):
        self.cycle = cycle
        self.group = cycle // 2
        self.block = patch_count
        self.specials = special_count
        self.images = image_count
        self.patch_rows = cycle * patch_count
        self.special_pad = -(-special_count // LANES) * LANES
        self.rows = self.patch_rows + self.special_pad
        self.own_patch = 2 * patch_count
        self.own = self.own_patch + special_count
        self.extra = image_count + 1
        self.unroll = PAIRS if self.rows <= 2048 else 1

    def place(self):
        me = lax.axis_index("blk")
        return me // self.group, me % self.group

    def at(self, half, other):
        return pl.multiple_of((half * self.group + other) * self.block, self.block)

    def own_rows(self, ref, place):
        return jnp.concatenate(
            [
                ref[pl.ds(self.at(0, place), self.block), :],
                ref[pl.ds(self.at(1, place), self.block), :],
                ref[self.patch_rows : self.patch_rows + self.specials, :],
            ],
            axis=0,
        )


def image_lanes(plan, lengths, pads, pack):
    lane = lane_ids(1)
    start = jnp.zeros((1, LANES), jnp.int32)
    stop, live = start, start
    so_far = jnp.int32(0)
    for image in range(plan.images):
        start = jnp.where(lane == image, so_far, start)
        so_far = so_far + lengths[pack, image]
        stop = jnp.where(lane == image, so_far, stop)
        live = jnp.where(lane == image, so_far - pads[pack, image], live)
    return start, stop, live


def write_masks(plan, lengths, pads, pack, key_extra, query_extra):
    start, stop, live = image_lanes(plan, lengths, pads, pack)
    count = plan.block
    lane = lane_ids(count)
    one, zero = jnp.ones((count, LANES), F32), jnp.zeros((count, LANES), F32)

    @pl.loop(0, plan.cycle)
    def _(step):
        base = pl.multiple_of(step * count, count)
        token = row_ids(count) + base
        inside = (token >= start) & (token < stop)
        alive = (token >= start) & (token < live)
        key_extra[pl.ds(base, count), :] = jnp.where(alive, zero, one).astype(LOW)
        query_extra[pl.ds(base, count), :] = jnp.where(inside, BLOCKED, zero).astype(LOW)

    count = plan.special_pad
    lane, special = lane_ids(count), row_ids(count)
    one, zero = jnp.ones((count, LANES), F32), jnp.zeros((count, LANES), F32)
    mine = (lane == special // 2) & (special < plan.specials)
    never = (lane == plan.images) & (special >= plan.specials)
    key_extra[plan.patch_rows :, :] = jnp.where(mine, zero, one).astype(LOW)
    query_extra[plan.patch_rows :, :] = jnp.where(mine | never, BLOCKED, zero).astype(LOW)


def project(plan, rows, places, weight, shift, mixed):
    out = (dot(rows, weight[...]) + shift).astype(LOW)
    at = 0
    for first, count in places:
        here = pl.ds(first, count)
        for part in range(3 * PAIRS):
            mixed[part, here, :] = out[at : at + count, part * LANES : (part + 1) * LANES]
        at += count


def project_pieces(plan, place, pieces, masks, weight, shift, mixed):
    for piece, mask in zip(pieces, masks):
        other = jnp.bitwise_xor(place, mask)
        places = [(plan.at(half, other), plan.block) for half in range(2)]
        project(plan, piece[...], places, weight, shift, mixed)


def padded_specials(plan, rows):
    pad = jnp.zeros((plan.special_pad - plan.specials, rows.shape[1]), LOW)
    return jnp.concatenate([rows, pad], axis=0) if pad.shape[0] else rows


def shift_row(qv_bias):
    width = qv_bias.shape[1] // 2
    return jnp.concatenate(
        [qv_bias[:, :width], jnp.zeros((1, width), F32), qv_bias[:, width:]], axis=1
    )


def attend(plan, place, mixed, key_extra, query_extra, keys, joined, total):
    lane = lane_ids(plan.own)
    own_extra = plan.own_rows(query_extra, place)
    keys[:, LANES:] = key_extra[...]
    total[...] = jnp.zeros_like(total)

    ones = jnp.ones((plan.rows, LANES), LOW)

    @pl.loop(0, PAIRS, unroll=plan.unroll)
    def _(pair):
        query = (plan.own_rows(mixed.at[pair], place).astype(F32) * 0.125).astype(LOW)
        keys[:, :LANES] = mixed[PAIRS + pair]
        values = jnp.concatenate([mixed[2 * PAIRS + pair], ones], axis=1)
        scores, out, logs = [], [], total[...]
        for side in range(2):
            mine = (lane // HEAD_DIM) == side
            left = jnp.concatenate([jnp.where(mine, query, 0), own_extra], axis=1)
            scores.append(dot_nt(left, keys[...]))
        for side in range(2):
            top = jnp.max(scores[side], axis=-1, keepdims=True)
            both = dot(jnp.exp(scores[side] - top).astype(LOW), values)
            out.append(both[:, :LANES] / both[:, LANES:])
            logs = jnp.where(lane == 2 * pair + side, top + jnp.log(both[:, LANES:]), logs)
        joined[pair] = jnp.where(lane < HEAD_DIM, out[0], out[1])
        total[...] = logs


def feed_forward(second_normed, fc1, fc1_bias, fc2, hidden, slope):
    out = None
    width = second_normed.shape[1]
    for first in range(0, fc1.shape[1], width):
        here = slice(first, first + width)
        pre = dot(second_normed, fc1[:, here]) + fc1_bias[:, here]
        cdf = 0.5 * (1.0 + lax.erf(pre * ROOT_HALF))
        pdf = jnp.exp(-0.5 * pre * pre) * INV_ROOT_TWO_PI
        value = (pre * cdf).astype(LOW)
        hidden[:, here] = value
        slope[:, here] = (cdf + pre * pdf).astype(LOW)
        part = dot(value, fc2[here, :])
        out = part if out is None else out + part
    return out


def forward_rest(layer, start, joined, w_proj, proj_bias, ln2_gain, ln2_bias, w_fc1, fc1_bias,
                 w_fc2, fc2_bias, hidden, slope, middle):
    row = slice(layer, layer + 1)
    attended = jnp.concatenate([joined[pair] for pair in range(PAIRS)], axis=1)
    after = start + dot(attended.astype(LOW), w_proj.ready()[...]) + proj_bias[row, :]
    middle[...] = after
    second = normed(after, ln2_gain[row, :], ln2_bias[row, :])
    out = feed_forward(second, w_fc1.ready(), fc1_bias[row, :], w_fc2.ready(), hidden, slope)
    return after + out + fc2_bias[row, :]


def block_places(plan, place, half, indices):
    return [
        plan.at(half if index < plan.group else 1 - half, jnp.bitwise_xor(place, index % plan.group))
        for index in indices
    ]


def early_kernel(plan, indices, *refs):
    blocks, refs = refs[: len(indices)], refs[len(indices) :]
    (lengths, pads, specials, ln1_gain, ln1_bias, w_qkv, qv_bias,
     key_extra, query_extra, mixed, start, own_normed, weight) = refs
    half, place = plan.place()
    write_masks(plan, lengths, pads, half, key_extra, query_extra)
    gain, bias = ln1_gain[0:1, :], ln1_bias[0:1, :]
    low_rows = []
    for index, ref in zip(indices, blocks):
        rows = ref[...].astype(F32)
        low_rows.append(normed(rows, gain, bias))
        if index % plan.group == 0:
            side = half if index < plan.group else 1 - half
            here = pl.ds(pl.multiple_of(side * plan.block, plan.block), plan.block)
            start[here, :] = rows
            own_normed[here, :] = low_rows[-1]
    rows = specials[half].astype(F32)
    special_rows = normed(rows, gain, bias)
    start[plan.own_patch :, :] = rows
    own_normed[plan.own_patch :, :] = special_rows
    shift = shift_row(qv_bias[0:1, :])
    count = len(indices) * plan.block
    rows = jnp.concatenate(low_rows, axis=0)
    project(plan, rows, [(0, count)], w_qkv.ready(), shift, mixed)
    rows = padded_specials(plan, special_rows)
    project(plan, rows, [(count, plan.special_pad)], w_qkv.ready(), shift, mixed)
    weight[...] = w_qkv[...]


def take_early(plan, early, firsts, mixed):
    at = 0
    for first, count in [(first, plan.block) for first in firsts] + [(plan.patch_rows, plan.special_pad)]:
        mixed[:, pl.ds(first, count), :] = early[:, at : at + count, :]
        at += count


def first_kernel(plan, early, indices, *refs):
    blocks, refs = refs[: len(indices)], refs[len(indices) :]
    (mixed_in, key_extra, query_extra, start,
     weight, ln1_gain, ln1_bias, qv_bias, w_proj, proj_bias, ln2_gain,
     ln2_bias, w_fc1, fc1_bias, w_fc2, fc2_bias,
     mixed, middle, joined, total, hidden, slope, after, send, keep, next_normed, keys) = refs
    half, place = plan.place()
    gain, bias = ln1_gain[0:1, :], ln1_bias[0:1, :]
    take_early(plan, mixed_in, block_places(plan, place, half, early), mixed)
    places = block_places(plan, place, half, indices)
    for first in range(0, len(indices), 4):
        some = slice(first, first + 4)
        rows = [normed(ref[...].astype(F32), gain, bias) for ref in blocks[some]]
        project(plan, jnp.concatenate(rows, axis=0), [(at, plan.block) for at in places[some]],
                weight, shift_row(qv_bias[0:1, :]), mixed)
    attend(plan, place, mixed, key_extra, query_extra, keys, joined, total)
    joined.send()
    out = forward_rest(0, start[...], joined, w_proj, proj_bias, ln2_gain, ln2_bias, w_fc1,
                       fc1_bias, w_fc2, fc2_bias, hidden, slope, middle)
    for ref in (middle, slope):
        ref.send()
    after[...] = out
    following = normed(out, ln1_gain[1:2, :], ln1_bias[1:2, :])
    send[...] = following[: plan.own_patch]
    keep[...] = following[plan.own_patch :]
    next_normed[...] = following


def split_low(values):
    parts, rest = [], values
    for _ in range(SPLITS):
        part = rest.astype(LOW)
        parts.append(part)
        rest = rest - part.astype(F32)
    return parts


def backward_rest(plan, layer, grad_rows, scale, middle, joined, total, hidden, slope, ln2_gain,
                  ln2_bias, w_fc1, w_fc2, w_proj, small, second, second_grad, pre_grad,
                  attended_low, first_grad, send, out_grad, logs):
    row = slice(layer, layer + 1)
    width = grad_rows.shape[1]
    low_grad = grad_rows.astype(LOW)
    second_grad[...] = low_grad
    after = middle[...]
    second[...] = normed(after, ln2_gain[row, :], ln2_bias[row, :])
    grad_second = None
    for first in range(0, slope.shape[1], width):
        here = slice(first, first + width)
        value = (dot_nt(low_grad, w_fc2.ready()[here, :]) * slope[:, here].astype(F32)).astype(LOW)
        pre_grad[:, here] = value
        small[6:7, here] = column_sum(value.astype(F32) * scale)
        part = dot_nt(value, w_fc1.ready()[:, here])
        grad_second = part if grad_second is None else grad_second + part
    change, scaled = norm_back(grad_second, after, ln2_gain[row, :])
    weighted = grad_second * scale
    grad_middle = grad_rows + change
    low_middle = grad_middle.astype(LOW)
    first_grad[...] = low_middle
    small[3:4, :width] = column_sum(low_middle.astype(F32) * scale)
    small[4:5, :width] = column_sum(weighted * scaled)
    small[5:6, :width] = column_sum(weighted)
    small[7:8, :width] = column_sum(low_grad.astype(F32) * scale)
    grad_out = dot_nt(low_middle, w_proj.ready()[...]).astype(LOW)
    out_grad[...] = grad_out
    lane = lane_ids(plan.own)
    table = total[...]
    for pair in range(PAIRS):
        here = slice(pair * LANES, (pair + 1) * LANES)
        attended = joined[pair]
        attended_low[:, here] = attended.astype(LOW)
        product = grad_out[:, here].astype(F32) * attended
        for side in range(2):
            mine = (lane // HEAD_DIM) == side
            delta = jnp.sum(jnp.where(mine, product, 0.0), axis=-1, keepdims=True)
            table = jnp.where(lane == HEADS + 2 * pair + side, delta, table)
    logs[...] = table
    send[: plan.own_patch, :] = grad_out[: plan.own_patch]
    pick = jnp.where(row_ids(16) == lane_ids(16), 1.0, 0.0).astype(LOW)
    parts = split_low(table)
    for part in range(2):
        rows = slice(part * plan.block, (part + 1) * plan.block)
        turned = [dot_nt(pick, values[rows]).astype(LOW) for values in parts]
        first = plan.own_patch + 16 * part
        send[first : first + 16, :] = jnp.concatenate(turned, axis=1)
    return grad_middle


def assemble_kernel(plan, *refs):
    half = plan.place()[0]
    for (kept, sent, got), (rows, specials) in ((refs[:3], refs[6:8]), (refs[3:6], refs[8:10])):
        rows[half] = kept[...]
        rows[1 - half] = got[: plan.block, :]
        specials[half] = sent[plan.block :, :]
        specials[1 - half] = got[plan.block :, :]


def owner_scale(plan, place):
    row = lax.broadcasted_iota(jnp.int32, (plan.own, 1), 0)
    return jnp.where((row < plan.own_patch) | (place == 0), 1.0, 0.0)


def second_early_kernel(plan, masks, *refs):
    pieces, refs = refs[: len(masks)], refs[len(masks) :]
    normed_specials, w_qkv, qv_bias, mixed, weight = refs
    shift = shift_row(qv_bias[1:2, :])
    at = 0
    for piece in pieces:
        project(plan, piece[...], [(at, plan.own_patch)], w_qkv.ready(), shift, mixed)
        at += plan.own_patch
    rows = padded_specials(plan, normed_specials[...])
    project(plan, rows, [(at, plan.special_pad)], w_qkv.ready(), shift, mixed)
    weight[...] = w_qkv[...]


def second_kernel(plan, early, masks, *refs):
    pieces, refs = refs[: len(masks)], refs[len(masks) :]
    (mixed_in, key_extra, query_extra, start, grad_kept, grad_swapped, grad_specials,
     weight, qv_bias, w_proj, proj_bias, ln2_gain, ln2_bias, w_fc1, fc1_bias, w_fc2, fc2_bias,
     mixed, out_kept, out_send, grad_middle, send, out_grad, logs, small, second, second_grad,
     pre_grad, attended_low, first_grad, hidden,
     keys, joined, total, slope, middle) = refs
    half, place = plan.place()
    others = [jnp.bitwise_xor(place, mask) for mask in early]
    firsts = [plan.at(which, other) for other in others for which in range(2)]
    take_early(plan, mixed_in, firsts, mixed)
    project_pieces(plan, place, pieces, masks, weight, shift_row(qv_bias[1:2, :]), mixed)
    attend(plan, place, mixed, key_extra, query_extra, keys, joined, total)
    out = forward_rest(1, start[...], joined, w_proj, proj_bias, ln2_gain, ln2_bias, w_fc1,
                       fc1_bias, w_fc2, fc2_bias, hidden, slope, middle)
    low_out = out.astype(LOW)
    first, later = low_out[: plan.block], low_out[plan.block : plan.own_patch]
    out_kept[...] = jnp.where(half == 0, first, later)
    out_send[: plan.block, :] = jnp.where(half == 0, later, first)
    out_send[plan.block :, :] = low_out[plan.own_patch :]
    kept, swapped = grad_kept[...].astype(F32), grad_swapped[...].astype(F32)
    own_extra = plan.own_rows(key_extra, place)[: plan.own_patch].astype(F32)
    lane = lane_ids(plan.own_patch)
    live = jnp.sum(jnp.where(lane < plan.images, 1.0 - own_extra, 0.0), axis=-1, keepdims=True)
    patch_grad = jnp.concatenate(
        [jnp.where(half == 0, kept, swapped), jnp.where(half == 0, swapped, kept)], axis=0
    )
    grad_rows = jnp.concatenate([patch_grad * live, grad_specials[half].astype(F32)], axis=0)
    small[0:3, :] = jnp.zeros((3, small.shape[1]), F32)
    grad_middle[...] = backward_rest(
        plan, 1, grad_rows, owner_scale(plan, place), middle, joined, total, hidden, slope,
        ln2_gain, ln2_bias, w_fc1, w_fc2, w_proj, small, second, second_grad, pre_grad,
        attended_low, first_grad, send, out_grad, logs)


def placed(plan, rows, first_row, first_lane):
    row, lane = row_ids(rows), lane_ids(rows)
    out = []
    for split in range(SPLITS):
        head = row - first_row
        hit = (head >= 0) & (head < HEADS) & (lane == first_lane + SPLITS * head + split)
        out.append(jnp.where(hit, -1.0, 0.0).astype(LOW))
    return out


def spread_logs(plan, table, first_row):
    picks = placed(plan, LANES, first_row, plan.extra)
    return sum(dot(values, pick) for values, pick in zip(split_low(table), picks)).astype(LOW)


def head_lanes(plan, lane, head):
    first = plan.extra + SPLITS * head
    return (lane >= first) & (lane < first + SPLITS)


def query_grad_kernel(plan, mixed, key_extra, query_extra, out_grad, logs, grad_query, keys, values):
    _, place = plan.place()
    lane = lane_ids(plan.own)
    own_extra = plan.own_rows(query_extra, place)
    log_extra = spread_logs(plan, logs[...], 0)
    delta_extra = spread_logs(plan, logs[...], HEADS)
    keys[:, LANES:] = key_extra[...]
    values[:, LANES:] = key_extra[...]

    @pl.loop(0, PAIRS, unroll=plan.unroll)
    def _(pair):
        query = (plan.own_rows(mixed.at[pair], place).astype(F32) * 0.125).astype(LOW)
        here = pl.ds(pl.multiple_of(pair * LANES, LANES), LANES)
        grad_out = out_grad[:, here]
        keys[:, :LANES] = mixed[PAIRS + pair]
        values[:, :LANES] = mixed[2 * PAIRS + pair]
        out = []
        for side in range(2):
            mine = (lane // HEAD_DIM) == side
            head = head_lanes(plan, lane, 2 * pair + side)
            left = jnp.concatenate(
                [jnp.where(mine, query, 0), jnp.where(head, log_extra, own_extra)], axis=1
            )
            probs = jnp.exp(dot_nt(left, keys[...]))
            left = jnp.concatenate(
                [jnp.where(mine, grad_out, 0), jnp.where(head, delta_extra, 0)], axis=1
            )
            grad_scores = (probs * dot_nt(left, values[...])).astype(LOW)
            out.append(dot(grad_scores, mixed[PAIRS + pair]) * 0.125)
        grad_query[:, here] = jnp.where(lane < HEAD_DIM, out[0], out[1]).astype(LOW)


def key_grads(plan, place, pieces, mixed, key_extra, query_extra, out_grad, logs, grad_mixed,
              queries, grads, all_grads):
    log_rows = placed(plan, 16, 0, plan.extra)
    delta_rows = placed(plan, 16, HEADS, plan.extra)
    picks = [jnp.concatenate(two, axis=1) for two in zip(log_rows, delta_rows)]
    for index, ref in enumerate(pieces):
        other = jnp.bitwise_xor(place, index)
        for half in range(2):
            here = pl.ds(plan.at(half, other), plan.block)
            for pair in range(PAIRS):
                all_grads[pair, here, :] = ref[
                    half * plan.block : (half + 1) * plan.block, pair * LANES : (pair + 1) * LANES
                ]
            first = plan.own_patch + 16 * half
            both = sum(
                dot_tn(ref[first : first + 16, split * LANES : (split + 1) * LANES], picks[split])
                for split in range(SPLITS)
            )
            queries[here, LANES:] = (both[:, :LANES] + query_extra[here, :].astype(F32)).astype(LOW)
            grads[here, LANES:] = both[:, LANES:].astype(LOW)
    last, stop = plan.patch_rows, plan.patch_rows + plan.specials
    table = logs[plan.own_patch :, :]
    log_extra = spread_logs(plan, table, 0).astype(F32)
    queries[last:, LANES:] = query_extra[last:, :]
    queries[last:stop, LANES:] = (log_extra + query_extra[last:stop, :].astype(F32)).astype(LOW)
    grads[last:, LANES:] = jnp.zeros((plan.special_pad, LANES), LOW)
    grads[last:stop, LANES:] = spread_logs(plan, table, HEADS)
    for pair in range(PAIRS):
        all_grads[pair, last:, :] = jnp.zeros((plan.special_pad, LANES), LOW)
        all_grads[pair, last:stop, :] = out_grad[
            plan.own_patch :, pair * LANES : (pair + 1) * LANES
        ]
    lane = lane_ids(plan.own)
    own_extra = plan.own_rows(key_extra, place)
    own_extra = jnp.where(lane < plan.extra, own_extra, 0)

    @pl.loop(0, PAIRS)
    def _(pair):
        queries[:, :LANES] = (mixed[pair].astype(F32) * 0.125).astype(LOW)
        grads[:, :LANES] = all_grads[pair]
        key = plan.own_rows(mixed.at[PAIRS + pair], place)
        value = plan.own_rows(mixed.at[2 * PAIRS + pair], place)
        grad_key, grad_value = [], []
        for side in range(2):
            mine = (lane // HEAD_DIM) == side
            head = head_lanes(plan, lane, 2 * pair + side)
            extra = jnp.where(head, 1.0, own_extra.astype(F32)).astype(LOW)
            left = jnp.concatenate([jnp.where(mine, key, 0), extra], axis=1)
            probs = jnp.exp(dot_nt(left, queries[...]))
            left = jnp.concatenate([jnp.where(mine, value, 0), extra], axis=1)
            grad_scores = (probs * dot_nt(left, grads[...])).astype(LOW)
            grad_key.append(dot(grad_scores, queries[:, :LANES]))
            grad_value.append(dot(probs.astype(LOW), all_grads[pair]))
        width = PAIRS * LANES
        here = pl.ds(pl.multiple_of(width + pair * LANES, LANES), LANES)
        grad_mixed[:, here] = jnp.where(lane < HEAD_DIM, *grad_key).astype(LOW)
        here = pl.ds(pl.multiple_of(2 * width + pair * LANES, LANES), LANES)
        grad_mixed[:, here] = jnp.where(lane < HEAD_DIM, *grad_value).astype(LOW)


def first_norm_back(plan, layer, scale, grad_mixed, w_qkv, start, ln1_gain, small):
    width = start.shape[1]
    mixed = grad_mixed[...]
    sums = column_sum(mixed.astype(F32) * scale)
    small[2:3, : 2 * width] = jnp.concatenate([sums[:, :width], sums[:, 2 * width :]], axis=1)
    grad_normed = dot_nt(mixed, w_qkv.ready()[...])
    change, scaled = norm_back(grad_normed, start[...], ln1_gain[layer : layer + 1, :])
    weighted = grad_normed * scale
    small[0:1, :width] = column_sum(weighted * scaled)
    small[1:2, :width] = column_sum(weighted)
    return change


def third_kernel(plan, *refs):
    pieces, refs = refs[: plan.group], refs[plan.group :]
    (mixed, key_extra, query_extra, later_grad, later_logs, grad_query, later_start, later_middle,
     later_small, ln1_gain, later_qkv,
     middle, joined, total, hidden, slope, ln2_gain, ln2_bias, w_fc1, w_fc2, w_proj,
     grad_mixed, small_out, grad_middle, send, out_grad, logs, small, second, second_grad,
     pre_grad, attended_low, first_grad,
     queries, grads, all_grads) = refs
    _, place = plan.place()
    scale = owner_scale(plan, place)
    grad_mixed[:, : grad_query.shape[1]] = grad_query[...]
    key_grads(plan, place, pieces, mixed, key_extra, query_extra, later_grad, later_logs,
              grad_mixed, queries, grads, all_grads)
    small_out[...] = later_small[...]
    grad_rows = later_middle[...] + first_norm_back(
        plan, 1, scale, grad_mixed, later_qkv, later_start, ln1_gain, small_out
    )
    small[0:3, :] = jnp.zeros((3, small.shape[1]), F32)
    grad_middle[...] = backward_rest(
        plan, 0, grad_rows, scale, middle, joined, total, hidden, slope, ln2_gain, ln2_bias,
        w_fc1, w_fc2, w_proj, small, second, second_grad, pre_grad, attended_low, first_grad,
        send, out_grad, logs)


def fourth_kernel(plan, *refs):
    pieces, refs = refs[: plan.group], refs[plan.group :]
    (mixed, key_extra, query_extra, out_grad, logs, grad_query, start, grad_middle, small, ln1_gain,
     w_qkv,
     grad_mixed, small_out, grad_kept, grad_send,
     queries, grads, all_grads) = refs
    half, place = plan.place()
    scale = owner_scale(plan, place)
    grad_mixed[:, : grad_query.shape[1]] = grad_query[...]
    key_grads(plan, place, pieces, mixed, key_extra, query_extra, out_grad, logs, grad_mixed,
              queries, grads, all_grads)
    small_out[...] = small[...]
    out = grad_middle[...] + first_norm_back(
        plan, 0, scale, grad_mixed, w_qkv, start, ln1_gain, small_out
    )
    first, later = out[: plan.block], out[plan.block : plan.own_patch]
    grad_kept[...] = jnp.where(half == 0, first, later)
    grad_send[: plan.block, :] = jnp.where(half == 0, later, first)
    grad_send[plan.block :, :] = out[plan.own_patch :]


def weight_kernel(plan, count, small_count, used, *refs):
    kept, sent, out = refs[-3:]
    place = plan.place()[1]
    keep = owner_scale(plan, place)
    at = 0
    for index in range(count):
        left = (refs[2 * index][...].astype(F32) * keep).astype(LOW)
        right = refs[2 * index + 1]
        step = min(384, right.shape[1])
        for first in range(0, right.shape[1], step):
            product = dot_tn(left, right[:, first : first + step]).astype(LOW)
            for column in range(0, step, LANES):
                out[at : at + left.shape[1], :] = product[:, column : column + LANES]
                at += left.shape[1]
    for ref in refs[2 * count : 2 * count + small_count]:
        small = ref[...]
        for column in range(0, small.shape[1], 2 * LANES):
            two = [small[:, column : column + LANES], small[:, column + LANES : column + 2 * LANES]]
            out[at : at + 16, :] = jnp.concatenate(two, axis=0).astype(LOW)
            at += 16
    if used < out.shape[0]:
        out[used:, :] = jnp.zeros((out.shape[0] - used, LANES), LOW)
    size = kept.shape[0]
    core = lax.axis_index("blk") % 2
    kept[...] = out[pl.ds(pl.multiple_of(core * size, 16), size), :]
    sent[...] = out[pl.ds(pl.multiple_of((1 - core) * size, 16), size), :]


def side_of(axis, bits):
    place = lax.axis_index("blk")
    bit = jnp.where(place % 2 == 0, bits[0], bits[1])
    if axis == "blk":
        return (place >> bit) & 1
    return (lax.axis_index("pack") >> bit) & 1


def split_kernel(axis, bits, mine, got, kept, sent):
    size = kept.shape[0]
    side = side_of(axis, bits)
    for which, out in ((side, kept), (1 - side, sent)):
        here = pl.ds(pl.multiple_of(which * size, 16), size)
        out[...] = (mine[here, :].astype(F32) + got[here, :].astype(F32)).astype(LOW)


def add_kernel(mine, got, out):
    out[...] = (mine[...].astype(F32) + got[...].astype(F32)).astype(LOW)


def join_kernel(axis, bits, mine, got, out):
    size = mine.shape[0]
    side = side_of(axis, bits)
    out[pl.ds(pl.multiple_of(side * size, 16), size), :] = mine[...]
    out[pl.ds(pl.multiple_of((1 - side) * size, 16), size), :] = got[...]


def unpack_kernel(entries, stacked, filled, width, *refs):
    own, got = refs[0], refs[1]
    outs = refs[2 + filled :]
    rows, semaphores = outs[-2], outs[-1]
    buffers = outs[len(outs) - 2 - len(entries) : -2]
    core = lax.axis_index("blk") % 2
    size = own.shape[0]
    rows[pl.ds(pl.multiple_of(core * size, 16), size), :] = own[...]
    rows[pl.ds(pl.multiple_of((1 - core) * size, 16), size), :] = got[...]
    at, copies = 0, []
    for number, (output, layer, height, columns) in enumerate(entries):
        buffer = buffers[number]
        for first in range(0, columns, LANES):
            buffer[:, first : first + LANES] = rows[at : at + height, :].astype(F32)
            at += height
        copies.append(
            pltpu.make_async_copy(buffer, outs[output].at[layer], semaphores.at[number])
        )
        copies[-1].start()
    if width:
        small = []
        for _ in range(LAYERS):
            blocks = []
            for _ in range(width // (2 * LANES)):
                both = rows[at : at + 16, :].astype(F32)
                blocks += [both[:8], both[8:]]
                at += 16
            small.append(jnp.concatenate(blocks, axis=1))
        for row, out in enumerate(outs[stacked : stacked + 8]):
            columns = out.shape[1]
            out[...] = jnp.concatenate([part[row : row + 1, :columns] for part in small], axis=0)
    for copy in copies:
        copy.wait()


VMEM = pl.BlockSpec(memory_space=pltpu.VMEM)


ANY = pl.BlockSpec(memory_space=pl.ANY)
HBM = pl.BlockSpec(memory_space=pltpu.HBM)


WHOLE = -1


class Staged:
    def __init__(self, source, layer, target, semaphore):
        self.target = target
        source = source if layer == WHOLE else source.at[layer]
        self.copy = pltpu.make_async_copy(source, target, semaphore)
        self.copy.start()
        self.waits = True

    def ready(self):
        if self.waits:
            self.copy.wait()
            self.waits = False
        return self.target

    @property
    def shape(self):
        return self.target.shape

    def __getitem__(self, index):
        return self.ready()[index]


class Late:
    def __init__(self, out, buffer, semaphore):
        self.buffer, self.copy, self.sent = buffer, pltpu.make_async_copy(buffer, out, semaphore), False

    @property
    def shape(self):
        return self.buffer.shape

    def __getitem__(self, index):
        return self.buffer[index]

    def __setitem__(self, index, value):
        self.buffer[index] = value

    def send(self):
        self.copy.start()
        self.sent = True

    def finish(self):
        if not self.sent:
            self.send()
        self.copy.wait()


def staged_kernel(kernel, layers, out_count, late, *refs):
    ins, outs = list(refs[: len(layers)]), list(refs[len(layers) : len(layers) + out_count])
    rest = refs[len(layers) + out_count :]
    chosen = [index for index, layer in enumerate(layers) if layer is not None]
    if not chosen and not late:
        return kernel(*refs)
    count = len(chosen) + len(late)
    buffers, semaphores = rest[:count], rest[count]
    for number, index in enumerate(chosen):
        ins[index] = Staged(ins[index], layers[index], buffers[number], semaphores.at[number])
    for number, index in enumerate(late, len(chosen)):
        outs[index] = Late(outs[index], buffers[number], semaphores.at[number])
    kernel(*ins, *outs, *rest[count + 1 :])
    for index in late:
        outs[index].finish()
    for index in chosen:
        ins[index].ready()


def run(kernel, name, outs, ins, scratch=(), far_outs=(), aliases=None, plain=(), mib=12,
        late=()):
    micros = MICROS.get(name) or MICROS["unpack" if name.startswith("unpack") else "sum"]
    specs, values, layers, buffers = [], [], [], []
    far_ins = {index for index, output in (aliases or {}).items() if output in far_outs}
    for index, item in enumerate(ins):
        value, layer = item if isinstance(item, tuple) else (item, None)
        if layer is not None:
            specs.append(HBM)
        elif index in far_ins:
            specs.append(ANY)
        else:
            specs.append(VMEM)
        if layer is not None:
            space = pltpu.SMEM if value.dtype == jnp.int32 else pltpu.VMEM
            buffers.append(space(value.shape[0 if layer == WHOLE else 1 :], value.dtype))
            value = pltpu.with_memory_space_constraint(value, pltpu.HBM)
        layers.append(layer)
        values.append(value)
    buffers += [pltpu.VMEM(*outs[index]) for index in late]
    if buffers:
        buffers.append(pltpu.SemaphoreType.DMA((len(buffers),)))
    return pl.pallas_call(
        functools.partial(staged_kernel, kernel, layers, len(outs), late),
        out_shape=[
            (pltpu.HBM if index in late else jax.ShapeDtypeStruct)(shape, kind)
            for index, (shape, kind) in enumerate(outs)
        ],
        in_specs=specs,
        out_specs=[
            HBM if index in late else ANY if index in far_outs else VMEM for index in range(len(outs))
        ],
        scratch_shapes=buffers + [pltpu.VMEM(shape, kind) for shape, kind in scratch] + list(plain),
        input_output_aliases=aliases or {},
        compiler_params=pltpu.CompilerParams(vmem_limit_bytes=mib * MIB),
        cost_estimate=pl.CostEstimate(
            flops=int(micros * FLOPS_PER_MICRO), bytes_accessed=0, transcendentals=0
        ),
        name=name,
    )(*values)


def swap(value, mask):
    size = lax.axis_size("blk")
    return lax.ppermute(value, "blk", [(i, i ^ mask) for i in range(size)])


def spread(value, group, then=None, near=None):
    held = {0: value}
    mask = group // 2
    if then is not None:
        held[mask] = swap(value, mask)
        (held[0], held[mask]), then = tie([held[0], held[mask]], then)
        mask //= 2
    while mask:
        for index, item in list(held.items()):
            held[index | mask] = (near or {}).get(index | mask)
            if held[index | mask] is None:
                held[index | mask] = swap(item, mask)
        mask //= 2
    pieces = [held[index] for index in range(group)]
    return pieces if then is None else (pieces, then)


def exchange(value, axis, bits):
    masks = [1 << bit for bit in bits]
    cycle = lax.axis_size("blk")
    pairs = []
    for device in range(lax.axis_size("pack") * cycle):
        pack, place = divmod(device, cycle)
        mask = masks[place % 2]
        other = (pack, place ^ mask) if axis == "blk" else (pack ^ mask, place)
        pairs.append((device, other[0] * cycle + other[1]))
    return lax.ppermute(value, ("pack", "blk"), pairs)


def tie(*groups):
    return lax.optimization_barrier(groups)


class Summing:
    def __init__(self, name, kept, sent):
        self.name = name
        self.values = [kept, sent, None]
        chips = list(range(1, lax.axis_size("blk").bit_length() - 1))
        packs = list(range(lax.axis_size("pack").bit_length() - 1))
        parts = [("blk", pair) for pair in zip(chips, reversed(chips))]
        parts += [("pack", (bit, bit)) for bit in packs[:-1]]
        self.steps = [("split", part, part) for part in parts]
        self.steps += [("add", None, ("pack", (packs[-1], packs[-1]))), ("add", None, parts[-1])]
        for part, then in zip(parts[::-1], parts[-2::-1] + [None]):
            self.steps.append(("join", part, then))

    def after(self, *others):
        tied = tie(self.values[:1], list(others))
        self.values[0] = tied[0][0]
        return tied[1] if len(others) > 1 else tied[1][0]

    def arrived(self):
        if len(self.values) == 3:
            mine, sent, then = self.values
            self.values = [mine, swap(sent, 1) if then is None else exchange(sent, *then)]
        return self.values

    def step(self, last=None):
        if last is not None:
            self.after(last)
        self.arrived()
        kind, part, then = self.steps.pop(0)
        name = f"{self.name}_{kind}{len(self.steps)}"
        size = self.values[0].shape[0]
        shape = lambda count: ((count, LANES), LOW)
        if kind == "split":
            kernel = functools.partial(split_kernel, *part)
            mine, sent = run(kernel, name, [shape(size // 2)] * 2, self.values)
        elif kind == "add":
            mine = sent = run(add_kernel, name, [shape(size)], self.values)[0]
        else:
            kernel = functools.partial(join_kernel, *part)
            mine = sent = run(kernel, name, [shape(2 * size)], self.values)[0]
        self.values = [mine, swap(sent, 1) if then is None else exchange(sent, *then)]
        return mine


def unpacked(name, values, entries, shapes, filled, width=0, sums=()):
    ins = list(values) + [filled[k] for k in sorted(filled)]
    aliases = {2 + index: output for index, output in enumerate(sorted(filled))}
    outs = [(shape, F32) for shape in shapes] + list(sums)
    half = values[0].shape[0]
    scratch = [((rows, columns), F32) for _, _, rows, columns in entries] + [((2 * half, LANES), LOW)]
    kernel = functools.partial(unpack_kernel, entries, len(shapes), len(filled), width)
    return run(kernel, name, outs, ins, scratch, set(range(len(shapes))), aliases,
               [pltpu.SemaphoreType.DMA((len(entries),))], 24)


def on_device(patches, specials, image_lengths, pad_counts, ln1_gain, ln1_bias, w_qkv, qv_bias,
              w_proj, proj_bias, ln2_gain, ln2_bias, w_fc1, fc1_bias, w_fc2, fc2_bias, d_patches,
              d_specials):
    ln1, ln1_shift, ln2, ln2_shift = [(v, WHOLE) for v in (ln1_gain, ln1_bias, ln2_gain, ln2_bias)]
    qv_shift, proj_shift = (qv_bias, WHOLE), (proj_bias, WHOLE)
    fc1_shift, fc2_shift = (fc1_bias, WHOLE), (fc2_bias, WHOLE)
    cycle, pack_size = lax.axis_size("blk"), lax.axis_size("pack")
    patch_count, special_count, width = patches.shape[1], specials.shape[1], patches.shape[2]
    hidden_width = w_fc1.shape[2]
    plan = Plan(cycle, patch_count, special_count, image_lengths.shape[1])
    own, rows, group = plan.own, plan.rows, plan.group
    half = lax.axis_index("blk") // group

    def kept_and_sent(pair):
        return (lax.dynamic_index_in_dim(pair, half, 0, keepdims=False),
                lax.dynamic_index_in_dim(pair, 1 - half, 0, keepdims=False))

    kept, sent = kept_and_sent(patches)
    swapped = swap(sent, group)
    blocks = spread(kept, group) + [swapped]
    early = [0, group, 1 % group, group // 2]
    early = sorted(set(early))
    rest = [index for index in range(2 * group) if index not in early]

    mib = max(12, rows // 90)
    more = max(26, rows // 90)
    extra_shape = ((rows, LANES), LOW)
    mixed_shape = ((3 * PAIRS, rows, LANES), LOW)
    joined_shape = ((PAIRS, own, LANES), F32)
    wide, wide_low = ((own, width), F32), ((own, width), LOW)
    hidden_shape, slope_shape = ((own, hidden_width), LOW), ((own, hidden_width), LOW)
    table_shape = ((own, LANES), F32)
    small_shape = ((8, hidden_width), F32)
    send_shape = ((plan.own_patch + 32, width), LOW)
    double_shape = ((rows, 2 * LANES), LOW)
    all_grads_shape = ((PAIRS, rows, LANES), LOW)

    def weights(name, products, small=()):
        sizes = [(a[0] if isinstance(a, tuple) else a).shape[1] * b.shape[1] for a, b in products]
        used = sum(sizes) // LANES
        small = list(small)
        used += len(small) * 8 * hidden_width // LANES
        multiple = 16 * cycle * pack_size
        total = -(-used // multiple) * multiple
        flat = [x for pair in products for x in pair] + small
        kernel = functools.partial(weight_kernel, plan, len(products), len(small), used)
        half_rows = ((total // 2, LANES), LOW)
        return run(kernel, name, [half_rows, half_rows], flat, [((total, LANES), LOW)], mib=mib)

    def query_grad(name, mixed, out_grad, logs):
        kernel = functools.partial(query_grad_kernel, plan)
        ins = [mixed, key_extra, query_extra, out_grad, logs]
        return run(kernel, name, [wide_low], ins, [double_shape, double_shape], mib=more)[0]

    weight_shape = (w_qkv.shape[1:], LOW)

    def early_shape(count):
        return ((3 * PAIRS, count * patch_count + plan.special_pad, LANES), LOW)

    key_extra, query_extra, mixed_0, start_0, normed_0, weight_0 = run(
        functools.partial(early_kernel, plan, early), "layer_0_early",
        [extra_shape, extra_shape, early_shape(len(early)), wide, wide_low, weight_shape],
        [blocks[index] for index in early] + [(image_lengths, WHOLE), (pad_counts, WHOLE),
         (specials, WHOLE), ln1, ln1_shift, (w_qkv, 0), qv_shift], mib=more)
    swapped, (mixed_0,) = spread(swapped, group, [mixed_0], {1: swap(swapped, 1)})
    blocks += swapped[1:]
    (mixed_0, middle_0, joined_0, total_0, hidden_0, slope_0, start_1, send, normed_specials,
     normed_1) = run(
        functools.partial(first_kernel, plan, early, rest), "layer_0_forward",
        [mixed_shape, wide, joined_shape, table_shape, hidden_shape,
         slope_shape, wide, ((plan.own_patch, width), LOW), ((special_count, width), LOW), wide_low],
        [blocks[index] for index in rest] + [mixed_0, key_extra, query_extra, start_0, weight_0, ln1,
         ln1_shift, qv_shift, (w_proj, 0), proj_shift, ln2, ln2_shift, (w_fc1, 0),
         fc1_shift, (w_fc2, 0), fc2_shift],
        [double_shape], mib=more, late=(1, 2, 5))
    middle_0, joined_0, slope_0 = [(v, WHOLE) for v in (middle_0, joined_0, slope_0)]
    grad_kept, grad_sent = kept_and_sent(tie([d_patches], [send])[0][0])
    grad_swapped = swap(grad_sent, group)
    near = {0: send, 1: swap(send, 1)}
    mixed_1, weight_1 = run(
        functools.partial(second_early_kernel, plan, list(near)), "layer_1_early",
        [early_shape(2 * len(near)), weight_shape],
        list(near.values()) + [normed_specials, (w_qkv, 1), qv_shift], mib=more)
    pieces, (mixed_1, grad_swapped) = spread(send, group, [mixed_1, grad_swapped], near)
    masks = [mask for mask in range(group) if mask not in near]
    pieces = [pieces[mask] for mask in masks]
    (mixed_1, out_kept, out_send, grad_middle_1, send, out_grad_1, logs_1, small_1, second_1,
     second_grad_1, pre_grad_1, attended_1, first_grad_1, hidden_1) = run(
        functools.partial(second_kernel, plan, list(near), masks), "layer_1_forward",
        [mixed_shape, ((patch_count, width), LOW), ((patch_count + special_count, width), LOW),
         wide, send_shape, wide_low, table_shape, small_shape, wide_low, wide_low, hidden_shape,
         wide_low, wide_low, hidden_shape],
        pieces + [mixed_1, key_extra, query_extra, start_1, grad_kept, grad_swapped,
                  (d_specials, WHOLE), weight_1, qv_shift, (w_proj, 1), proj_shift, ln2,
                  ln2_shift, (w_fc1, 1), fc1_shift, (w_fc2, 1), fc2_shift],
        [double_shape, joined_shape, table_shape, slope_shape, wide], mib=more)
    grad_query_1 = query_grad("layer_1_query_grad", mixed_1, out_grad_1, logs_1)
    later_pieces, (grad_query_1,) = spread(send, group, [grad_query_1])
    (second_grad_1,), (grad_query_1,) = tie([second_grad_1], [grad_query_1])
    halves = weights(
        "layer_1_weights",
        [(hidden_1, second_grad_1), (second_1, pre_grad_1), (attended_1, first_grad_1)],
    )
    first_sum = Summing("first_sum", *halves)
    first_sum.step()
    (grad_query_1,), _ = tie([grad_query_1], first_sum.values[:1])
    (grad_mixed_1, small_1, grad_middle_0, send, out_grad_0, logs_0, small_0, second_0,
     second_grad_0, pre_grad_0, attended_0, first_grad_0) = run(
        functools.partial(third_kernel, plan), "layer_1_key_grad",
        [((own, 3 * width), LOW), small_shape, wide, send_shape, wide_low, table_shape, small_shape,
         wide_low, wide_low, hidden_shape, wide_low, wide_low],
        later_pieces + [mixed_1, key_extra, query_extra, out_grad_1, logs_1, grad_query_1, start_1,
                        grad_middle_1, small_1, ln1, (w_qkv, 1), middle_0, joined_0, total_0,
                        hidden_0, slope_0, ln2, ln2_shift, (w_fc1, 0), (w_fc2, 0), (w_proj, 0)],
        [double_shape, double_shape, all_grads_shape], mib=mib)
    out_grad_0 = first_sum.after(out_grad_0)
    last = first_sum.step()
    second_grad_0 = tie([second_grad_0], [last])[0][0]
    halves = weights(
        "layer_0_weights",
        [(hidden_0, second_grad_0), (second_0, pre_grad_0), (attended_0, first_grad_0)])
    later_pieces, halves = spread(send, group, list(halves))
    second_sum = Summing("second_sum", *halves)
    (out_grad_0,), _ = tie([out_grad_0], halves)
    grad_query_0 = query_grad("layer_0_query_grad", mixed_0, out_grad_0, logs_0)
    last = first_sum.step(grad_query_0)
    last = second_sum.step(last)
    (grad_query_0,), _ = tie([grad_query_0], [last])
    grad_mixed_0, small_0, grad_kept_out, grad_send = run(
        functools.partial(fourth_kernel, plan), "layer_0_key_grad",
        [((own, 3 * width), LOW), small_shape, ((patch_count, width), F32),
         ((patch_count + special_count, width), F32)],
        later_pieces + [mixed_0, key_extra, query_extra, out_grad_0, logs_0, grad_query_0, start_0,
                        grad_middle_0, small_0, ln1, (w_qkv, 0)],
        [double_shape, double_shape, all_grads_shape], mib=mib)
    halves = weights(
        "mix_weights", [(normed_0, grad_mixed_0), (normed_1, grad_mixed_1)], (small_0, small_1)
    )
    last = second_sum.step(halves[0])
    last_sum = Summing("last_sum", *tie(list(halves), [last])[0])
    fc2_shape, fc1_shape, proj_shape = w_fc2.shape, w_fc1.shape, w_proj.shape
    entries = [(0,) + fc2_shape[1:], (1,) + fc1_shape[1:], (2,) + proj_shape[1:]]
    stacked = {}
    sums = {"a": (first_sum, 1, "unpack_first"), "b": (second_sum, 0, "unpack_second")}
    order = list(ORDER) + ["a", "b", "c"] * 9
    while order:
        which = order.pop(0)
        if which == "c" and last_sum.steps:
            last = last_sum.step(last)
        elif which == "g":
            grad_got = swap(tie([grad_send], [last])[0][0], group)
        elif which == "o":
            out_got = swap(tie([out_send], [last])[0][0], group)
        elif which == "G":
            grad_got = last_sum.after(grad_got)
        elif which == "O":
            out_got = last_sum.after(out_got)
        elif which in sums:
            this, layer, name = sums[which]
            if this.steps:
                last = this.step(last)
                continue
            del sums[which]
            this.after(last)
            where = [(output, layer, *shape) for output, *shape in entries]
            shapes = [fc2_shape, fc1_shape, proj_shape]
            stacked = dict(enumerate(unpacked(name, this.arrived(), where, shapes, stacked)))
            last = stacked[2]
    fc2, fc1, proj = stacked[0], stacked[1], stacked[2]
    widths = [width, width, 2 * width, width, width, width, hidden_width, width]
    qkv, *sums = unpacked(
        "unpack_last", last_sum.arrived(), [(0, 0) + w_qkv.shape[1:], (0, 1) + w_qkv.shape[1:]],
        [w_qkv.shape], {}, hidden_width, [((LAYERS, columns), F32) for columns in widths])
    pair = lambda count, kind: ((2, count, width), kind)
    out_patches, out_specials, grad_patches, grad_specials = run(
        functools.partial(assemble_kernel, plan), "assemble",
        [pair(patch_count, LOW), pair(special_count, LOW), pair(patch_count, F32),
         pair(special_count, F32)],
        [out_kept, out_send, out_got, grad_kept_out, grad_send, grad_got])
    return (
        out_patches, out_specials, grad_patches, grad_specials,
        sums[0], sums[1], qkv, sums[2], proj, sums[3], sums[4], sums[5], fc1, sums[6], fc2, sums[7],
    )


def solution(mesh):
    rows, one = P("pack", "blk", None), P("pack", None, None)
    in_specs = (rows, one, P("pack", None), P("pack", None)) + (P(),) * 12 + (rows, one)
    out_specs = (rows, one, rows, one) + (P(),) * 12
    return jax.shard_map(
        on_device, mesh=mesh, in_specs=in_specs, out_specs=out_specs, check_vma=False
    )
```

```python
import functools

import jax
import jax.numpy as jnp
from jax import lax
from jax.experimental import pallas as pl
from jax.experimental.pallas import tpu as pltpu
from jax.sharding import PartitionSpec as P

HEADS = 6
HEAD_DIM = 64
LAYERS = 2
PAIRS = HEADS // 2
LANES = 128
SPLITS = 3
BLOCKED = -1e30
NORM_EPS = 1e-06
ROOT_HALF = 0.7071067811865476
INV_ROOT_TWO_PI = 0.3989422804014327
F32 = jnp.float32
LOW = jnp.bfloat16
MIB = 1024 * 1024
ORDER = "acbcagbcaobcabcGOacbcabbcc"
FLOPS_PER_MICRO = 1.1e9
MICROS = {
    "layer_0_early": 1.0, "layer_1_early": 1.0, "layer_0_forward": 14.0, "layer_1_forward": 15.5, "layer_1_query_grad": 4.0,
    "layer_1_weights": 1.0, "layer_1_key_grad": 14.0, "layer_0_weights": 1.0,
    "layer_0_query_grad": 5.0, "layer_0_key_grad": 1.0, "mix_weights": 2.0, "unpack": 4.0,
    "sum": 10.0,
    "first_sum_split7": 10.0,
    "first_sum_split6": 10.0,
    "first_sum_split5": 10.0,
    "first_sum_add4": 10.0,
    "first_sum_add3": 1.0,
    "first_sum_join2": 10.0,
    "first_sum_join1": 10.0,
    "first_sum_join0": 10.0,
    "second_sum_split7": 10.0,
    "second_sum_split6": 10.0,
    "second_sum_split5": 10.0,
    "second_sum_add4": 10.0,
    "second_sum_add3": 3.0,
    "second_sum_join2": 10.0,
    "second_sum_join1": 10.0,
    "second_sum_join0": 1.0,
    "last_sum_split7": 1.0,
    "last_sum_split6": 10.0,
    "last_sum_split5": 10.0,
    "last_sum_add4": 10.0,
    "last_sum_add3": 10.0,
    "last_sum_join2": 10.0,
    "last_sum_join1": 10.0,
    "last_sum_join0": 10.0,
}


def dot(a, b):
    return jnp.dot(a, b, preferred_element_type=F32)


def dot_nt(a, b):
    return lax.dot_general(a, b, (((1,), (1,)), ((), ())), preferred_element_type=F32)


def dot_tn(a, b):
    return lax.dot_general(a, b, (((0,), (0,)), ((), ())), preferred_element_type=F32)


def lane_ids(rows):
    return lax.broadcasted_iota(jnp.int32, (rows, LANES), 1)


def row_ids(rows, lanes=LANES):
    return lax.broadcasted_iota(jnp.int32, (rows, lanes), 0)


def norm_parts(rows):
    centre = rows - jnp.mean(rows, axis=-1, keepdims=True)
    inverse = lax.rsqrt(jnp.mean(centre * centre, axis=-1, keepdims=True) + NORM_EPS)
    return centre * inverse, inverse


def normed(rows, gain, bias):
    return (norm_parts(rows)[0] * gain + bias).astype(LOW)


def norm_back(grad_out, rows, gain):
    scaled, inverse = norm_parts(rows)
    grad_scaled = grad_out * gain
    grad_rows = inverse * (
        grad_scaled
        - jnp.mean(grad_scaled, axis=-1, keepdims=True)
        - scaled * jnp.mean(grad_scaled * scaled, axis=-1, keepdims=True)
    )
    return grad_rows, scaled


def column_sum(rows):
    return jnp.sum(rows, axis=0, keepdims=True)


class Plan:
    def __init__(self, cycle, patch_count, special_count, image_count):
        self.cycle = cycle
        self.group = cycle // 2
        self.block = patch_count
        self.specials = special_count
        self.images = image_count
        self.patch_rows = cycle * patch_count
        self.special_pad = -(-special_count // LANES) * LANES
        self.rows = self.patch_rows + self.special_pad
        self.own_patch = 2 * patch_count
        self.own = self.own_patch + special_count
        self.extra = image_count + 1
        self.unroll = PAIRS if self.rows <= 2048 else 1

    def place(self):
        me = lax.axis_index("blk")
        return me // self.group, me % self.group

    def at(self, half, other):
        return pl.multiple_of((half * self.group + other) * self.block, self.block)

    def own_rows(self, ref, place):
        return jnp.concatenate(
            [
                ref[pl.ds(self.at(0, place), self.block), :],
                ref[pl.ds(self.at(1, place), self.block), :],
                ref[self.patch_rows : self.patch_rows + self.specials, :],
            ],
            axis=0,
        )


def image_lanes(plan, lengths, pads, pack):
    lane = lane_ids(1)
    start = jnp.zeros((1, LANES), jnp.int32)
    stop, live = start, start
    so_far = jnp.int32(0)
    for image in range(plan.images):
        start = jnp.where(lane == image, so_far, start)
        so_far = so_far + lengths[pack, image]
        stop = jnp.where(lane == image, so_far, stop)
        live = jnp.where(lane == image, so_far - pads[pack, image], live)
    return start, stop, live


def write_masks(plan, lengths, pads, pack, key_extra, query_extra):
    start, stop, live = image_lanes(plan, lengths, pads, pack)
    count = plan.block
    lane = lane_ids(count)
    one, zero = jnp.ones((count, LANES), F32), jnp.zeros((count, LANES), F32)

    @pl.loop(0, plan.cycle)
    def _(step):
        base = pl.multiple_of(step * count, count)
        token = row_ids(count) + base
        inside = (token >= start) & (token < stop)
        alive = (token >= start) & (token < live)
        key_extra[pl.ds(base, count), :] = jnp.where(alive, zero, one).astype(LOW)
        query_extra[pl.ds(base, count), :] = jnp.where(inside, BLOCKED, zero).astype(LOW)

    count = plan.special_pad
    lane, special = lane_ids(count), row_ids(count)
    one, zero = jnp.ones((count, LANES), F32), jnp.zeros((count, LANES), F32)
    mine = (lane == special // 2) & (special < plan.specials)
    never = (lane == plan.images) & (special >= plan.specials)
    key_extra[plan.patch_rows :, :] = jnp.where(mine, zero, one).astype(LOW)
    query_extra[plan.patch_rows :, :] = jnp.where(mine | never, BLOCKED, zero).astype(LOW)


def project(plan, rows, places, weight, shift, mixed):
    out = (dot(rows, weight[...]) + shift).astype(LOW)
    at = 0
    for first, count in places:
        here = pl.ds(first, count)
        for part in range(3 * PAIRS):
            mixed[part, here, :] = out[at : at + count, part * LANES : (part + 1) * LANES]
        at += count


def project_pieces(plan, place, pieces, masks, weight, shift, mixed):
    for piece, mask in zip(pieces, masks):
        other = jnp.bitwise_xor(place, mask)
        places = [(plan.at(half, other), plan.block) for half in range(2)]
        project(plan, piece[...], places, weight, shift, mixed)


def padded_specials(plan, rows):
    pad = jnp.zeros((plan.special_pad - plan.specials, rows.shape[1]), LOW)
    return jnp.concatenate([rows, pad], axis=0) if pad.shape[0] else rows


def shift_row(qv_bias):
    width = qv_bias.shape[1] // 2
    return jnp.concatenate(
        [qv_bias[:, :width], jnp.zeros((1, width), F32), qv_bias[:, width:]], axis=1
    )


def attend(plan, place, mixed, key_extra, query_extra, keys, joined, total):
    lane = lane_ids(plan.own)
    own_extra = plan.own_rows(query_extra, place)
    keys[:, LANES:] = key_extra[...]
    total[...] = jnp.zeros_like(total)

    ones = jnp.ones((plan.rows, LANES), LOW)

    @pl.loop(0, PAIRS, unroll=plan.unroll)
    def _(pair):
        query = (plan.own_rows(mixed.at[pair], place).astype(F32) * 0.125).astype(LOW)
        keys[:, :LANES] = mixed[PAIRS + pair]
        values = jnp.concatenate([mixed[2 * PAIRS + pair], ones], axis=1)
        scores, out, logs = [], [], total[...]
        for side in range(2):
            mine = (lane // HEAD_DIM) == side
            left = jnp.concatenate([jnp.where(mine, query, 0), own_extra], axis=1)
            scores.append(dot_nt(left, keys[...]))
        for side in range(2):
            top = jnp.max(scores[side], axis=-1, keepdims=True)
            both = dot(jnp.exp(scores[side] - top).astype(LOW), values)
            out.append(both[:, :LANES] / both[:, LANES:])
            logs = jnp.where(lane == 2 * pair + side, top + jnp.log(both[:, LANES:]), logs)
        joined[pair] = jnp.where(lane < HEAD_DIM, out[0], out[1])
        total[...] = logs


def feed_forward(second_normed, fc1, fc1_bias, fc2, hidden, slope):
    out = None
    width = second_normed.shape[1]
    for first in range(0, fc1.shape[1], width):
        here = slice(first, first + width)
        pre = dot(second_normed, fc1[:, here]) + fc1_bias[:, here]
        cdf = 0.5 * (1.0 + lax.erf(pre * ROOT_HALF))
        pdf = jnp.exp(-0.5 * pre * pre) * INV_ROOT_TWO_PI
        value = (pre * cdf).astype(LOW)
        hidden[:, here] = value
        slope[:, here] = (cdf + pre * pdf).astype(LOW)
        part = dot(value, fc2[here, :])
        out = part if out is None else out + part
    return out


def forward_rest(layer, start, joined, w_proj, proj_bias, ln2_gain, ln2_bias, w_fc1, fc1_bias,
                 w_fc2, fc2_bias, hidden, slope, middle):
    row = slice(layer, layer + 1)
    attended = jnp.concatenate([joined[pair] for pair in range(PAIRS)], axis=1)
    after = start + dot(attended.astype(LOW), w_proj.ready()[...]) + proj_bias[row, :]
    middle[...] = after
    second = normed(after, ln2_gain[row, :], ln2_bias[row, :])
    out = feed_forward(second, w_fc1.ready(), fc1_bias[row, :], w_fc2.ready(), hidden, slope)
    return after + out + fc2_bias[row, :]


def block_places(plan, place, half, indices):
    return [
        plan.at(half if index < plan.group else 1 - half, jnp.bitwise_xor(place, index % plan.group))
        for index in indices
    ]


def early_kernel(plan, indices, *refs):
    blocks, refs = refs[: len(indices)], refs[len(indices) :]
    (lengths, pads, specials, ln1_gain, ln1_bias, w_qkv, qv_bias,
     key_extra, query_extra, mixed, start, own_normed, weight) = refs
    half, place = plan.place()
    write_masks(plan, lengths, pads, half, key_extra, query_extra)
    gain, bias = ln1_gain[0:1, :], ln1_bias[0:1, :]
    low_rows = []
    for index, ref in zip(indices, blocks):
        rows = ref[...].astype(F32)
        low_rows.append(normed(rows, gain, bias))
        if index % plan.group == 0:
            side = half if index < plan.group else 1 - half
            here = pl.ds(pl.multiple_of(side * plan.block, plan.block), plan.block)
            start[here, :] = rows
            own_normed[here, :] = low_rows[-1]
    rows = specials[half].astype(F32)
    special_rows = normed(rows, gain, bias)
    start[plan.own_patch :, :] = rows
    own_normed[plan.own_patch :, :] = special_rows
    shift = shift_row(qv_bias[0:1, :])
    count = len(indices) * plan.block
    rows = jnp.concatenate(low_rows, axis=0)
    project(plan, rows, [(0, count)], w_qkv.ready(), shift, mixed)
    rows = padded_specials(plan, special_rows)
    project(plan, rows, [(count, plan.special_pad)], w_qkv.ready(), shift, mixed)
    weight[...] = w_qkv[...]


def take_early(plan, early, firsts, mixed):
    at = 0
    for first, count in [(first, plan.block) for first in firsts] + [(plan.patch_rows, plan.special_pad)]:
        mixed[:, pl.ds(first, count), :] = early[:, at : at + count, :]
        at += count


def first_kernel(plan, early, indices, *refs):
    blocks, refs = refs[: len(indices)], refs[len(indices) :]
    (mixed_in, key_extra, query_extra, start,
     weight, ln1_gain, ln1_bias, qv_bias, w_proj, proj_bias, ln2_gain,
     ln2_bias, w_fc1, fc1_bias, w_fc2, fc2_bias,
     mixed, middle, joined, total, hidden, slope, after, send, keep, next_normed, keys) = refs
    half, place = plan.place()
    gain, bias = ln1_gain[0:1, :], ln1_bias[0:1, :]
    take_early(plan, mixed_in, block_places(plan, place, half, early), mixed)
    places = block_places(plan, place, half, indices)
    for first in range(0, len(indices), 4):
        some = slice(first, first + 4)
        rows = [normed(ref[...].astype(F32), gain, bias) for ref in blocks[some]]
        project(plan, jnp.concatenate(rows, axis=0), [(at, plan.block) for at in places[some]],
                weight, shift_row(qv_bias[0:1, :]), mixed)
    attend(plan, place, mixed, key_extra, query_extra, keys, joined, total)
    joined.send()
    out = forward_rest(0, start[...], joined, w_proj, proj_bias, ln2_gain, ln2_bias, w_fc1,
                       fc1_bias, w_fc2, fc2_bias, hidden, slope, middle)
    for ref in (middle, slope):
        ref.send()
    after[...] = out
    following = normed(out, ln1_gain[1:2, :], ln1_bias[1:2, :])
    send[...] = following[: plan.own_patch]
    keep[...] = following[plan.own_patch :]
    next_normed[...] = following


def split_low(values):
    parts, rest = [], values
    for _ in range(SPLITS):
        part = rest.astype(LOW)
        parts.append(part)
        rest = rest - part.astype(F32)
    return parts


def backward_rest(plan, layer, grad_rows, scale, middle, joined, total, hidden, slope, ln2_gain,
                  ln2_bias, w_fc1, w_fc2, w_proj, small, second, second_grad, pre_grad,
                  attended_low, first_grad, send, out_grad, logs):
    row = slice(layer, layer + 1)
    width = grad_rows.shape[1]
    low_grad = grad_rows.astype(LOW)
    second_grad[...] = low_grad
    after = middle[...]
    second[...] = normed(after, ln2_gain[row, :], ln2_bias[row, :])
    grad_second = None
    for first in range(0, slope.shape[1], width):
        here = slice(first, first + width)
        value = (dot_nt(low_grad, w_fc2.ready()[here, :]) * slope[:, here].astype(F32)).astype(LOW)
        pre_grad[:, here] = value
        small[6:7, here] = column_sum(value.astype(F32) * scale)
        part = dot_nt(value, w_fc1.ready()[:, here])
        grad_second = part if grad_second is None else grad_second + part
    change, scaled = norm_back(grad_second, after, ln2_gain[row, :])
    weighted = grad_second * scale
    grad_middle = grad_rows + change
    low_middle = grad_middle.astype(LOW)
    first_grad[...] = low_middle
    small[3:4, :width] = column_sum(low_middle.astype(F32) * scale)
    small[4:5, :width] = column_sum(weighted * scaled)
    small[5:6, :width] = column_sum(weighted)
    small[7:8, :width] = column_sum(low_grad.astype(F32) * scale)
    grad_out = dot_nt(low_middle, w_proj.ready()[...]).astype(LOW)
    out_grad[...] = grad_out
    lane = lane_ids(plan.own)
    table = total[...]
    for pair in range(PAIRS):
        here = slice(pair * LANES, (pair + 1) * LANES)
        attended = joined[pair]
        attended_low[:, here] = attended.astype(LOW)
        product = grad_out[:, here].astype(F32) * attended
        for side in range(2):
            mine = (lane // HEAD_DIM) == side
            delta = jnp.sum(jnp.where(mine, product, 0.0), axis=-1, keepdims=True)
            table = jnp.where(lane == HEADS + 2 * pair + side, delta, table)
    logs[...] = table
    send[: plan.own_patch, :] = grad_out[: plan.own_patch]
    pick = jnp.where(row_ids(16) == lane_ids(16), 1.0, 0.0).astype(LOW)
    parts = split_low(table)
    for part in range(2):
        rows = slice(part * plan.block, (part + 1) * plan.block)
        turned = [dot_nt(pick, values[rows]).astype(LOW) for values in parts]
        first = plan.own_patch + 16 * part
        send[first : first + 16, :] = jnp.concatenate(turned, axis=1)
    return grad_middle


def assemble_kernel(plan, *refs):
    half = plan.place()[0]
    for (kept, sent, got), (rows, specials) in ((refs[:3], refs[6:8]), (refs[3:6], refs[8:10])):
        rows[half] = kept[...]
        rows[1 - half] = got[: plan.block, :].astype(rows.dtype)
        specials[half] = sent[plan.block :, :].astype(rows.dtype)
        specials[1 - half] = got[plan.block :, :].astype(rows.dtype)


def owner_scale(plan, place):
    row = lax.broadcasted_iota(jnp.int32, (plan.own, 1), 0)
    return jnp.where((row < plan.own_patch) | (place == 0), 1.0, 0.0)


def second_early_kernel(plan, masks, *refs):
    pieces, refs = refs[: len(masks)], refs[len(masks) :]
    normed_specials, w_qkv, qv_bias, mixed, weight = refs
    shift = shift_row(qv_bias[1:2, :])
    at = 0
    for piece in pieces:
        project(plan, piece[...], [(at, plan.own_patch)], w_qkv.ready(), shift, mixed)
        at += plan.own_patch
    rows = padded_specials(plan, normed_specials[...])
    project(plan, rows, [(at, plan.special_pad)], w_qkv.ready(), shift, mixed)
    weight[...] = w_qkv[...]


def second_kernel(plan, early, masks, *refs):
    pieces, refs = refs[: len(masks)], refs[len(masks) :]
    (mixed_in, key_extra, query_extra, start, grad_kept, grad_swapped, grad_specials,
     weight, qv_bias, w_proj, proj_bias, ln2_gain, ln2_bias, w_fc1, fc1_bias, w_fc2, fc2_bias,
     mixed, out_kept, out_send, grad_middle, send, out_grad, logs, small, second, second_grad,
     pre_grad, attended_low, first_grad, hidden,
     keys, joined, total, slope, middle) = refs
    half, place = plan.place()
    others = [jnp.bitwise_xor(place, mask) for mask in early]
    firsts = [plan.at(which, other) for other in others for which in range(2)]
    take_early(plan, mixed_in, firsts, mixed)
    project_pieces(plan, place, pieces, masks, weight, shift_row(qv_bias[1:2, :]), mixed)
    attend(plan, place, mixed, key_extra, query_extra, keys, joined, total)
    out = forward_rest(1, start[...], joined, w_proj, proj_bias, ln2_gain, ln2_bias, w_fc1,
                       fc1_bias, w_fc2, fc2_bias, hidden, slope, middle)
    low_out = out.astype(LOW)
    first, later = low_out[: plan.block], low_out[plan.block : plan.own_patch]
    out_kept[...] = jnp.where(half == 0, first, later)
    out_send[: plan.block, :] = jnp.where(half == 0, later, first)
    out_send[plan.block :, :] = low_out[plan.own_patch :]
    kept, swapped = grad_kept[...].astype(F32), grad_swapped[...].astype(F32)
    own_extra = plan.own_rows(key_extra, place)[: plan.own_patch].astype(F32)
    lane = lane_ids(plan.own_patch)
    live = jnp.sum(jnp.where(lane < plan.images, 1.0 - own_extra, 0.0), axis=-1, keepdims=True)
    patch_grad = jnp.concatenate(
        [jnp.where(half == 0, kept, swapped), jnp.where(half == 0, swapped, kept)], axis=0
    )
    grad_rows = jnp.concatenate([patch_grad * live, grad_specials[half].astype(F32)], axis=0)
    small[0:3, :] = jnp.zeros((3, small.shape[1]), F32)
    grad_middle[...] = backward_rest(
        plan, 1, grad_rows, owner_scale(plan, place), middle, joined, total, hidden, slope,
        ln2_gain, ln2_bias, w_fc1, w_fc2, w_proj, small, second, second_grad, pre_grad,
        attended_low, first_grad, send, out_grad, logs)


def placed(plan, rows, first_row, first_lane):
    row, lane = row_ids(rows), lane_ids(rows)
    out = []
    for split in range(SPLITS):
        head = row - first_row
        hit = (head >= 0) & (head < HEADS) & (lane == first_lane + SPLITS * head + split)
        out.append(jnp.where(hit, -1.0, 0.0).astype(LOW))
    return out


def spread_logs(plan, table, first_row):
    picks = placed(plan, LANES, first_row, plan.extra)
    return sum(dot(values, pick) for values, pick in zip(split_low(table), picks)).astype(LOW)


def head_lanes(plan, lane, head):
    first = plan.extra + SPLITS * head
    return (lane >= first) & (lane < first + SPLITS)


def query_grad_kernel(plan, mixed, key_extra, query_extra, out_grad, logs, grad_query, keys, values):
    _, place = plan.place()
    lane = lane_ids(plan.own)
    own_extra = plan.own_rows(query_extra, place)
    log_extra = spread_logs(plan, logs[...], 0)
    delta_extra = spread_logs(plan, logs[...], HEADS)
    keys[:, LANES:] = key_extra[...]
    values[:, LANES:] = key_extra[...]

    @pl.loop(0, PAIRS, unroll=plan.unroll)
    def _(pair):
        query = (plan.own_rows(mixed.at[pair], place).astype(F32) * 0.125).astype(LOW)
        here = pl.ds(pl.multiple_of(pair * LANES, LANES), LANES)
        grad_out = out_grad[:, here]
        keys[:, :LANES] = mixed[PAIRS + pair]
        values[:, :LANES] = mixed[2 * PAIRS + pair]
        out = []
        for side in range(2):
            mine = (lane // HEAD_DIM) == side
            head = head_lanes(plan, lane, 2 * pair + side)
            left = jnp.concatenate(
                [jnp.where(mine, query, 0), jnp.where(head, log_extra, own_extra)], axis=1
            )
            probs = jnp.exp(dot_nt(left, keys[...]))
            left = jnp.concatenate(
                [jnp.where(mine, grad_out, 0), jnp.where(head, delta_extra, 0)], axis=1
            )
            grad_scores = (probs * dot_nt(left, values[...])).astype(LOW)
            out.append(dot(grad_scores, mixed[PAIRS + pair]) * 0.125)
        grad_query[:, here] = jnp.where(lane < HEAD_DIM, out[0], out[1]).astype(LOW)


def key_grads(plan, place, pieces, mixed, key_extra, query_extra, out_grad, logs, grad_mixed,
              queries, grads, all_grads):
    log_rows = placed(plan, 16, 0, plan.extra)
    delta_rows = placed(plan, 16, HEADS, plan.extra)
    picks = [jnp.concatenate(two, axis=1) for two in zip(log_rows, delta_rows)]
    for index, ref in enumerate(pieces):
        other = jnp.bitwise_xor(place, index)
        for half in range(2):
            here = pl.ds(plan.at(half, other), plan.block)
            for pair in range(PAIRS):
                all_grads[pair, here, :] = ref[
                    half * plan.block : (half + 1) * plan.block, pair * LANES : (pair + 1) * LANES
                ]
            first = plan.own_patch + 16 * half
            both = sum(
                dot_tn(ref[first : first + 16, split * LANES : (split + 1) * LANES], picks[split])
                for split in range(SPLITS)
            )
            queries[here, LANES:] = (both[:, :LANES] + query_extra[here, :].astype(F32)).astype(LOW)
            grads[here, LANES:] = both[:, LANES:].astype(LOW)
    last, stop = plan.patch_rows, plan.patch_rows + plan.specials
    table = logs[plan.own_patch :, :]
    log_extra = spread_logs(plan, table, 0).astype(F32)
    queries[last:, LANES:] = query_extra[last:, :]
    queries[last:stop, LANES:] = (log_extra + query_extra[last:stop, :].astype(F32)).astype(LOW)
    grads[last:, LANES:] = jnp.zeros((plan.special_pad, LANES), LOW)
    grads[last:stop, LANES:] = spread_logs(plan, table, HEADS)
    for pair in range(PAIRS):
        all_grads[pair, last:, :] = jnp.zeros((plan.special_pad, LANES), LOW)
        all_grads[pair, last:stop, :] = out_grad[
            plan.own_patch :, pair * LANES : (pair + 1) * LANES
        ]
    lane = lane_ids(plan.own)
    own_extra = plan.own_rows(key_extra, place)
    own_extra = jnp.where(lane < plan.extra, own_extra, 0)

    @pl.loop(0, PAIRS)
    def _(pair):
        queries[:, :LANES] = (mixed[pair].astype(F32) * 0.125).astype(LOW)
        grads[:, :LANES] = all_grads[pair]
        key = plan.own_rows(mixed.at[PAIRS + pair], place)
        value = plan.own_rows(mixed.at[2 * PAIRS + pair], place)
        grad_key, grad_value = [], []
        for side in range(2):
            mine = (lane // HEAD_DIM) == side
            head = head_lanes(plan, lane, 2 * pair + side)
            extra = jnp.where(head, 1.0, own_extra.astype(F32)).astype(LOW)
            left = jnp.concatenate([jnp.where(mine, key, 0), extra], axis=1)
            probs = jnp.exp(dot_nt(left, queries[...]))
            left = jnp.concatenate([jnp.where(mine, value, 0), extra], axis=1)
            grad_scores = (probs * dot_nt(left, grads[...])).astype(LOW)
            grad_key.append(dot(grad_scores, queries[:, :LANES]))
            grad_value.append(dot(probs.astype(LOW), all_grads[pair]))
        width = PAIRS * LANES
        here = pl.ds(pl.multiple_of(width + pair * LANES, LANES), LANES)
        grad_mixed[:, here] = jnp.where(lane < HEAD_DIM, *grad_key).astype(LOW)
        here = pl.ds(pl.multiple_of(2 * width + pair * LANES, LANES), LANES)
        grad_mixed[:, here] = jnp.where(lane < HEAD_DIM, *grad_value).astype(LOW)


def first_norm_back(plan, layer, scale, grad_mixed, w_qkv, start, ln1_gain, small):
    width = start.shape[1]
    mixed = grad_mixed[...]
    sums = column_sum(mixed.astype(F32) * scale)
    small[2:3, : 2 * width] = jnp.concatenate([sums[:, :width], sums[:, 2 * width :]], axis=1)
    grad_normed = dot_nt(mixed, w_qkv.ready()[...])
    change, scaled = norm_back(grad_normed, start[...], ln1_gain[layer : layer + 1, :])
    weighted = grad_normed * scale
    small[0:1, :width] = column_sum(weighted * scaled)
    small[1:2, :width] = column_sum(weighted)
    return change


def third_kernel(plan, *refs):
    pieces, refs = refs[: plan.group], refs[plan.group :]
    (mixed, key_extra, query_extra, later_grad, later_logs, grad_query, later_start, later_middle,
     later_small, ln1_gain, later_qkv,
     middle, joined, total, hidden, slope, ln2_gain, ln2_bias, w_fc1, w_fc2, w_proj,
     grad_mixed, small_out, grad_middle, send, out_grad, logs, small, second, second_grad,
     pre_grad, attended_low, first_grad,
     queries, grads, all_grads) = refs
    _, place = plan.place()
    scale = owner_scale(plan, place)
    grad_mixed[:, : grad_query.shape[1]] = grad_query[...]
    key_grads(plan, place, pieces, mixed, key_extra, query_extra, later_grad, later_logs,
              grad_mixed, queries, grads, all_grads)
    small_out[...] = later_small[...]
    grad_rows = later_middle[...] + first_norm_back(
        plan, 1, scale, grad_mixed, later_qkv, later_start, ln1_gain, small_out
    )
    small[0:3, :] = jnp.zeros((3, small.shape[1]), F32)
    grad_middle[...] = backward_rest(
        plan, 0, grad_rows, scale, middle, joined, total, hidden, slope, ln2_gain, ln2_bias,
        w_fc1, w_fc2, w_proj, small, second, second_grad, pre_grad, attended_low, first_grad,
        send, out_grad, logs)


def fourth_kernel(plan, *refs):
    pieces, refs = refs[: plan.group], refs[plan.group :]
    (mixed, key_extra, query_extra, out_grad, logs, grad_query, start, grad_middle, small, ln1_gain,
     w_qkv,
     grad_mixed, small_out, grad_kept, grad_send,
     queries, grads, all_grads) = refs
    half, place = plan.place()
    scale = owner_scale(plan, place)
    grad_mixed[:, : grad_query.shape[1]] = grad_query[...]
    key_grads(plan, place, pieces, mixed, key_extra, query_extra, out_grad, logs, grad_mixed,
              queries, grads, all_grads)
    small_out[...] = small[...]
    out = grad_middle[...] + first_norm_back(
        plan, 0, scale, grad_mixed, w_qkv, start, ln1_gain, small_out
    )
    first, later = out[: plan.block], out[plan.block : plan.own_patch]
    grad_kept[...] = jnp.where(half == 0, first, later)
    grad_send[: plan.block, :] = jnp.where(half == 0, later, first).astype(LOW)
    grad_send[plan.block :, :] = out[plan.own_patch :].astype(LOW)


def weight_kernel(plan, groups, *refs):
    kept, sent, out = refs[-3:]
    keep = owner_scale(plan, plan.place()[1])
    refs, at, end = list(refs[:-3]), 0, 0
    for count, small_count, rows in groups:
        end += rows
        for _ in range(count):
            left = (refs.pop(0)[...].astype(F32) * keep).astype(LOW)
            right = refs.pop(0)
            step = min(384, right.shape[1])
            for first in range(0, right.shape[1], step):
                product = dot_tn(left, right[:, first : first + step]).astype(LOW)
                for column in range(0, step, LANES):
                    out[at : at + left.shape[1], :] = product[:, column : column + LANES]
                    at += left.shape[1]
        for _ in range(small_count):
            small = refs.pop(0)[...]
            for column in range(0, small.shape[1], 2 * LANES):
                two = small[:, column : column + 2 * LANES]
                both = jnp.concatenate([two[:, :LANES], two[:, LANES:]], axis=0)
                out[at : at + 16, :] = both.astype(LOW)
                at += 16
        if at < end:
            out[at:end, :] = jnp.zeros((end - at, LANES), LOW)
        at = end
    size = kept.shape[0]
    core = lax.axis_index("blk") % 2
    kept[...] = out[pl.ds(pl.multiple_of(core * size, 16), size), :]
    sent[...] = out[pl.ds(pl.multiple_of((1 - core) * size, 16), size), :]


def side_of(axis, bits):
    place = lax.axis_index("blk")
    bit = jnp.where(place % 2 == 0, bits[0], bits[1])
    if axis == "blk":
        return (place >> bit) & 1
    return (lax.axis_index("pack") >> bit) & 1


def split_kernel(axis, bits, mine, got, kept, sent):
    size = kept.shape[0]
    side = side_of(axis, bits)
    for which, out in ((side, kept), (1 - side, sent)):
        here = pl.ds(pl.multiple_of(which * size, 16), size)
        out[...] = (mine[here, :].astype(F32) + got[here, :].astype(F32)).astype(LOW)


def add_kernel(mine, got, out):
    out[...] = (mine[...].astype(F32) + got[...].astype(F32)).astype(LOW)


def join_kernel(axis, bits, mine, got, out):
    size = mine.shape[0]
    side = side_of(axis, bits)
    out[pl.ds(pl.multiple_of(side * size, 16), size), :] = mine[...]
    out[pl.ds(pl.multiple_of((1 - side) * size, 16), size), :] = got[...]


def unpack_kernel(entries, filled, *refs):
    outs = refs[2 + filled :]
    rows, semaphores = outs[-2], outs[-1]
    buffers = outs[len(outs) - 2 - len(entries) : -2]
    core = lax.axis_index("blk") % 2
    size = refs[0].shape[0]
    rows[pl.ds(pl.multiple_of(core * size, 16), size), :] = refs[0][...]
    rows[pl.ds(pl.multiple_of((1 - core) * size, 16), size), :] = refs[1][...]
    at, copies = 0, []
    for number, (output, layer, height, columns) in enumerate(entries):
        buffer = buffers[number]
        for first in range(0, columns, LANES):
            buffer[:, first : first + LANES] = rows[at : at + height, :].astype(F32)
            at += height
        copies.append(
            pltpu.make_async_copy(buffer, outs[output].at[layer], semaphores.at[number])
        )
        copies[-1].start()
    for copy in copies:
        copy.wait()


def unpack_half_kernel(first, *refs):
    if first:
        rows, stacked, small_out, buffer, semaphore = refs
    else:
        rows, _, own_small, stacked, *sums, buffer, semaphore = refs
    core = lax.axis_index("blk") % 2
    layer = core if first else 1 - core
    height, columns = buffer.shape
    at = 0
    for column in range(0, columns, LANES):
        buffer[:, column : column + LANES] = rows[at : at + height, :].astype(F32)
        at += height
    copy = pltpu.make_async_copy(buffer, stacked.at[layer], semaphore.at[0])
    copy.start()
    blocks = []
    width = (small_out if first else own_small).shape[1]
    for _ in range(width // (2 * LANES)):
        both = rows[at : at + 16, :].astype(F32)
        blocks += [both[:8], both[8:]]
        at += 16
    small = jnp.concatenate(blocks, axis=1)
    if first:
        small_out[...] = small
    else:
        own = own_small[...]
        parts = [jnp.where(core == 0, own, small), jnp.where(core == 0, small, own)]
        for row, out in enumerate(sums):
            count = out.shape[1]
            out[...] = jnp.concatenate([part[row : row + 1, :count] for part in parts], axis=0)
    copy.wait()


VMEM = pl.BlockSpec(memory_space=pltpu.VMEM)


ANY = pl.BlockSpec(memory_space=pl.ANY)
HBM = pl.BlockSpec(memory_space=pltpu.HBM)


WHOLE = -1


class Staged:
    def __init__(self, source, layer, target, semaphore):
        self.target = target
        source = source if layer == WHOLE else source.at[layer]
        self.copy = pltpu.make_async_copy(source, target, semaphore)
        self.copy.start()
        self.waits = True

    def ready(self):
        if self.waits:
            self.copy.wait()
            self.waits = False
        return self.target

    @property
    def shape(self):
        return self.target.shape

    def __getitem__(self, index):
        return self.ready()[index]


class Late:
    def __init__(self, out, buffer, semaphore):
        self.buffer, self.copy, self.sent = buffer, pltpu.make_async_copy(buffer, out, semaphore), False

    @property
    def shape(self):
        return self.buffer.shape

    def __getitem__(self, index):
        return self.buffer[index]

    def __setitem__(self, index, value):
        self.buffer[index] = value

    def send(self):
        self.copy.start()
        self.sent = True

    def finish(self):
        if not self.sent:
            self.send()
        self.copy.wait()


def staged_kernel(kernel, layers, out_count, late, *refs):
    ins, outs = list(refs[: len(layers)]), list(refs[len(layers) : len(layers) + out_count])
    rest = refs[len(layers) + out_count :]
    chosen = [index for index, layer in enumerate(layers) if layer is not None]
    if not chosen and not late:
        return kernel(*refs)
    count = len(chosen) + len(late)
    buffers, semaphores = rest[:count], rest[count]
    for number, index in enumerate(chosen):
        ins[index] = Staged(ins[index], layers[index], buffers[number], semaphores.at[number])
    for number, index in enumerate(late, len(chosen)):
        outs[index] = Late(outs[index], buffers[number], semaphores.at[number])
    kernel(*ins, *outs, *rest[count + 1 :])
    for index in late:
        outs[index].finish()
    for index in chosen:
        ins[index].ready()


def run(kernel, name, outs, ins, scratch=(), far_outs=(), aliases=None, plain=(), mib=12,
        late=()):
    micros = MICROS.get(name) or MICROS["unpack" if name.startswith("unpack") else "sum"]
    specs, values, layers, buffers = [], [], [], []
    far_ins = {index for index, output in (aliases or {}).items() if output in far_outs}
    for index, item in enumerate(ins):
        value, layer = item if isinstance(item, tuple) else (item, None)
        if layer is not None:
            specs.append(HBM)
        elif index in far_ins:
            specs.append(ANY)
        else:
            specs.append(VMEM)
        if layer is not None:
            space = pltpu.SMEM if value.dtype == jnp.int32 else pltpu.VMEM
            buffers.append(space(value.shape[0 if layer == WHOLE else 1 :], value.dtype))
            value = pltpu.with_memory_space_constraint(value, pltpu.HBM)
        layers.append(layer)
        values.append(value)
    buffers += [pltpu.VMEM(*outs[index]) for index in late]
    if buffers:
        buffers.append(pltpu.SemaphoreType.DMA((len(buffers),)))
    return pl.pallas_call(
        functools.partial(staged_kernel, kernel, layers, len(outs), late),
        out_shape=[
            (pltpu.HBM if index in late else jax.ShapeDtypeStruct)(shape, kind)
            for index, (shape, kind) in enumerate(outs)
        ],
        in_specs=specs,
        out_specs=[
            HBM if index in late else ANY if index in far_outs else VMEM for index in range(len(outs))
        ],
        scratch_shapes=buffers + [pltpu.VMEM(shape, kind) for shape, kind in scratch] + list(plain),
        input_output_aliases=aliases or {},
        compiler_params=pltpu.CompilerParams(vmem_limit_bytes=mib * MIB),
        cost_estimate=pl.CostEstimate(
            flops=int(micros * FLOPS_PER_MICRO), bytes_accessed=0, transcendentals=0
        ),
        name=name,
    )(*values)


def swap(value, mask):
    size = lax.axis_size("blk")
    return lax.ppermute(value, "blk", [(i, i ^ mask) for i in range(size)])


def spread(value, group, then=None, near=None):
    held = {0: value}
    mask = group // 2
    if then is not None:
        held[mask] = swap(value, mask)
        (held[0], held[mask]), then = tie([held[0], held[mask]], then)
        mask //= 2
    while mask:
        for index, item in list(held.items()):
            held[index | mask] = (near or {}).get(index | mask)
            if held[index | mask] is None:
                held[index | mask] = swap(item, mask)
        mask //= 2
    pieces = [held[index] for index in range(group)]
    return pieces if then is None else (pieces, then)


def exchange(value, axis, bits):
    masks = [1 << bit for bit in bits]
    cycle = lax.axis_size("blk")
    pairs = []
    for device in range(lax.axis_size("pack") * cycle):
        pack, place = divmod(device, cycle)
        mask = masks[place % 2]
        other = (pack, place ^ mask) if axis == "blk" else (pack ^ mask, place)
        pairs.append((device, other[0] * cycle + other[1]))
    return lax.ppermute(value, ("pack", "blk"), pairs)


def tie(*groups):
    return lax.optimization_barrier(groups)


class Summing:
    def __init__(self, name, kept, sent):
        self.name = name
        self.values = [kept, sent, None]
        chips = list(range(1, lax.axis_size("blk").bit_length() - 1))
        packs = list(range(lax.axis_size("pack").bit_length() - 1))
        parts = [("blk", pair) for pair in zip(chips, reversed(chips))]
        parts += [("pack", (bit, bit)) for bit in packs[:-1]]
        self.steps = [("split", part, part) for part in parts]
        self.steps += [("add", None, ("pack", (packs[-1], packs[-1]))), ("add", None, parts[-1])]
        for part, then in zip(parts[::-1], parts[-2::-1] + [None]):
            self.steps.append(("join", part, then))

    def after(self, *others):
        tied = tie(self.values[:1], list(others))
        self.values[0] = tied[0][0]
        return tied[1] if len(others) > 1 else tied[1][0]

    def arrived(self):
        if len(self.values) == 3:
            mine, sent, then = self.values
            self.values = [mine, swap(sent, 1) if then is None else exchange(sent, *then)]
        return self.values

    def step(self, last=None):
        if last is not None:
            self.after(last)
        self.arrived()
        kind, part, then = self.steps.pop(0)
        name = f"{self.name}_{kind}{len(self.steps)}"
        size = self.values[0].shape[0]
        shape = lambda count: ((count, LANES), LOW)
        if kind == "split":
            kernel = functools.partial(split_kernel, *part)
            mine, sent = run(kernel, name, [shape(size // 2)] * 2, self.values)
        elif kind == "add":
            mine = sent = run(add_kernel, name, [shape(size)], self.values)[0]
        else:
            kernel = functools.partial(join_kernel, *part)
            mine = sent = run(kernel, name, [shape(2 * size)], self.values)[0]
        self.values = [mine, swap(sent, 1) if then is None else exchange(sent, *then)]
        return mine


def unpacked(name, values, entries, shapes, filled):
    ins = list(values) + [filled[k] for k in sorted(filled)]
    aliases = {2 + index: output for index, output in enumerate(sorted(filled))}
    total = sum(value.shape[0] for value in values)
    scratch = [((rows, columns), F32) for _, _, rows, columns in entries] + [((total, LANES), LOW)]
    kernel = functools.partial(unpack_kernel, entries, len(filled))
    return run(kernel, name, [(shape, F32) for shape in shapes], ins, scratch,
               set(range(len(shapes))), aliases, [pltpu.SemaphoreType.DMA((len(entries),))], 24)


def on_device(patches, specials, image_lengths, pad_counts, ln1_gain, ln1_bias, w_qkv, qv_bias,
              w_proj, proj_bias, ln2_gain, ln2_bias, w_fc1, fc1_bias, w_fc2, fc2_bias, d_patches,
              d_specials):
    ln1, ln1_shift, ln2, ln2_shift = [(v, WHOLE) for v in (ln1_gain, ln1_bias, ln2_gain, ln2_bias)]
    qv_shift, proj_shift = (qv_bias, WHOLE), (proj_bias, WHOLE)
    fc1_shift, fc2_shift = (fc1_bias, WHOLE), (fc2_bias, WHOLE)
    cycle, pack_size = lax.axis_size("blk"), lax.axis_size("pack")
    patch_count, special_count, width = patches.shape[1], specials.shape[1], patches.shape[2]
    hidden_width = w_fc1.shape[2]
    plan = Plan(cycle, patch_count, special_count, image_lengths.shape[1])
    own, rows, group = plan.own, plan.rows, plan.group
    half = lax.axis_index("blk") // group

    def kept_and_sent(pair):
        return (lax.dynamic_index_in_dim(pair, half, 0, keepdims=False),
                lax.dynamic_index_in_dim(pair, 1 - half, 0, keepdims=False))

    kept, sent = kept_and_sent(patches)
    swapped = swap(sent, group)
    blocks = spread(kept, group) + [swapped]
    early = [0, group, 1 % group, group // 2]
    early = sorted(set(early))
    rest = [index for index in range(2 * group) if index not in early]

    mib = max(12, rows // 90)
    more = max(26, rows // 90)
    extra_shape = ((rows, LANES), LOW)
    mixed_shape = ((3 * PAIRS, rows, LANES), LOW)
    joined_shape = ((PAIRS, own, LANES), F32)
    wide, wide_low = ((own, width), F32), ((own, width), LOW)
    hidden_shape, slope_shape = ((own, hidden_width), LOW), ((own, hidden_width), LOW)
    table_shape = ((own, LANES), F32)
    small_shape = ((8, hidden_width), F32)
    send_shape = ((plan.own_patch + 32, width), LOW)
    double_shape = ((rows, 2 * LANES), LOW)
    all_grads_shape = ((PAIRS, rows, LANES), LOW)

    def weights(name, *groups):
        multiple = 16 * cycle * pack_size // len(groups)
        plans, flat = [], []
        for products, small in groups:
            used = sum(a.shape[1] * b.shape[1] for a, b in products) // LANES
            used += len(small) * 8 * hidden_width // LANES
            plans.append((len(products), len(small), -(-used // multiple) * multiple))
            flat += [x for pair in products for x in pair] + list(small)
        total = sum(rows for _, _, rows in plans)
        kernel = functools.partial(weight_kernel, plan, plans)
        half_rows = ((total // 2, LANES), LOW)
        return run(kernel, name, [half_rows, half_rows], flat, [((total, LANES), LOW)], mib=mib)

    def query_grad(name, mixed, out_grad, logs):
        kernel = functools.partial(query_grad_kernel, plan)
        ins = [mixed, key_extra, query_extra, out_grad, logs]
        return run(kernel, name, [wide_low], ins, [double_shape, double_shape], mib=more)[0]

    weight_shape = (w_qkv.shape[1:], LOW)

    def early_shape(count):
        return ((3 * PAIRS, count * patch_count + plan.special_pad, LANES), LOW)

    key_extra, query_extra, mixed_0, start_0, normed_0, weight_0 = run(
        functools.partial(early_kernel, plan, early), "layer_0_early",
        [extra_shape, extra_shape, early_shape(len(early)), wide, wide_low, weight_shape],
        [blocks[index] for index in early] + [(image_lengths, WHOLE), (pad_counts, WHOLE),
         (specials, WHOLE), ln1, ln1_shift, (w_qkv, 0), qv_shift], mib=more)
    swapped, (mixed_0,) = spread(swapped, group, [mixed_0], {1: swap(swapped, 1)})
    blocks += swapped[1:]
    (mixed_0, middle_0, joined_0, total_0, hidden_0, slope_0, start_1, send, normed_specials,
     normed_1) = run(
        functools.partial(first_kernel, plan, early, rest), "layer_0_forward",
        [mixed_shape, wide, joined_shape, table_shape, hidden_shape,
         slope_shape, wide, ((plan.own_patch, width), LOW), ((special_count, width), LOW), wide_low],
        [blocks[index] for index in rest] + [mixed_0, key_extra, query_extra, start_0, weight_0, ln1,
         ln1_shift, qv_shift, (w_proj, 0), proj_shift, ln2, ln2_shift, (w_fc1, 0),
         fc1_shift, (w_fc2, 0), fc2_shift],
        [double_shape], mib=more, late=(1, 2, 5))
    middle_0, joined_0, slope_0 = [(v, WHOLE) for v in (middle_0, joined_0, slope_0)]
    grad_kept, grad_sent = kept_and_sent(tie([d_patches], [send])[0][0])
    grad_swapped = swap(grad_sent, group)
    near = {0: send, 1: swap(send, 1)}
    mixed_1, weight_1 = run(
        functools.partial(second_early_kernel, plan, list(near)), "layer_1_early",
        [early_shape(2 * len(near)), weight_shape],
        list(near.values()) + [normed_specials, (w_qkv, 1), qv_shift], mib=more)
    pieces, (mixed_1, grad_swapped) = spread(send, group, [mixed_1, grad_swapped], near)
    masks = [mask for mask in range(group) if mask not in near]
    pieces = [pieces[mask] for mask in masks]
    (mixed_1, out_kept, out_send, grad_middle_1, send, out_grad_1, logs_1, small_1, second_1,
     second_grad_1, pre_grad_1, attended_1, first_grad_1, hidden_1) = run(
        functools.partial(second_kernel, plan, list(near), masks), "layer_1_forward",
        [mixed_shape, ((patch_count, width), LOW), ((patch_count + special_count, width), LOW),
         wide, send_shape, wide_low, table_shape, small_shape, wide_low, wide_low, hidden_shape,
         wide_low, wide_low, hidden_shape],
        pieces + [mixed_1, key_extra, query_extra, start_1, grad_kept, grad_swapped,
                  (d_specials, WHOLE), weight_1, qv_shift, (w_proj, 1), proj_shift, ln2,
                  ln2_shift, (w_fc1, 1), fc1_shift, (w_fc2, 1), fc2_shift],
        [double_shape, joined_shape, table_shape, slope_shape, wide], mib=more)
    halves = weights(
        "layer_1_weights",
        ([(hidden_1, second_grad_1), (second_1, pre_grad_1), (attended_1, first_grad_1)], ()),
    )
    first_sum = Summing("first_sum", *halves)
    (out_grad_1,), _ = tie([out_grad_1], [halves[0]])
    grad_query_1 = query_grad("layer_1_query_grad", mixed_1, out_grad_1, logs_1)
    later_pieces, (grad_query_1,) = spread(send, group, [grad_query_1])
    last = first_sum.step(grad_query_1)
    (grad_query_1,), _ = tie([grad_query_1], [last])
    (grad_mixed_1, small_1, grad_middle_0, send, out_grad_0, logs_0, small_0, second_0,
     second_grad_0, pre_grad_0, attended_0, first_grad_0) = run(
        functools.partial(third_kernel, plan), "layer_1_key_grad",
        [((own, 3 * width), LOW), small_shape, wide, send_shape, wide_low, table_shape, small_shape,
         wide_low, wide_low, hidden_shape, wide_low, wide_low],
        later_pieces + [mixed_1, key_extra, query_extra, out_grad_1, logs_1, grad_query_1, start_1,
                        grad_middle_1, small_1, ln1, (w_qkv, 1), middle_0, joined_0, total_0,
                        hidden_0, slope_0, ln2, ln2_shift, (w_fc1, 0), (w_fc2, 0), (w_proj, 0)],
        [double_shape, double_shape, all_grads_shape], mib=mib)
    halves = weights(
        "layer_0_weights",
        ([(hidden_0, second_grad_0), (second_0, pre_grad_0), (attended_0, first_grad_0)], ()),
    )
    last = first_sum.step(halves[0])
    later_pieces, (last, *halves) = spread(send, group, [last, *halves])
    second_sum = Summing("second_sum", *halves)
    (out_grad_0,), _ = tie([out_grad_0], halves)
    grad_query_0 = query_grad("layer_0_query_grad", mixed_0, out_grad_0, logs_0)
    last = first_sum.step(grad_query_0)
    last = second_sum.step(last)
    (grad_query_0,), _ = tie([grad_query_0], [last])
    grad_mixed_0, small_0, grad_kept_out, grad_send = run(
        functools.partial(fourth_kernel, plan), "layer_0_key_grad",
        [((own, 3 * width), LOW), small_shape, ((patch_count, width), F32),
         ((patch_count + special_count, width), LOW)],
        later_pieces + [mixed_0, key_extra, query_extra, out_grad_0, logs_0, grad_query_0, start_0,
                        grad_middle_0, small_0, ln1, (w_qkv, 0)],
        [double_shape, double_shape, all_grads_shape], mib=mib)
    halves = weights(
        "mix_weights",
        ([(normed_0, grad_mixed_0)], [small_0]),
        ([(normed_1, grad_mixed_1)], [small_1]),
    )
    last = second_sum.step(halves[0])
    last_sum = Summing("last_sum", *tie(list(halves), [last])[0])
    fc2_shape, fc1_shape, proj_shape = w_fc2.shape, w_fc1.shape, w_proj.shape
    entries = [(0,) + fc2_shape[1:], (1,) + fc1_shape[1:], (2,) + proj_shape[1:]]
    stacked = {}
    sums = {"a": (first_sum, 1, "unpack_first"), "b": (second_sum, 0, "unpack_second")}
    order = list(ORDER) + ["a", "b", "c"] * 9
    while order:
        which = order.pop(0)
        if which == "c" and last_sum.steps:
            last = last_sum.step(last)
        elif which == "g":
            grad_got = swap(tie([grad_send], [last])[0][0], group)
        elif which == "o":
            out_got = swap(tie([out_send], [last])[0][0], group)
        elif which == "G":
            grad_got = last_sum.after(grad_got)
        elif which == "O":
            out_got = last_sum.after(out_got)
        elif which in sums:
            this, layer, name = sums[which]
            if this.steps:
                last = this.step(last)
                continue
            del sums[which]
            this.after(last)
            where = [(output, layer, *shape) for output, *shape in entries]
            shapes = [fc2_shape, fc1_shape, proj_shape]
            stacked = dict(enumerate(unpacked(name, this.arrived(), where, shapes, stacked)))
            last = stacked[2]
    fc2, fc1, proj = stacked[0], stacked[1], stacked[2]
    widths = [width, width, 2 * width, width, width, width, hidden_width, width]
    buffer, semaphore = [(w_qkv.shape[1:], F32)], [pltpu.SemaphoreType.DMA((1,))]
    mine = tie(last_sum.values[:1], [stacked[2]])[0][0]
    qkv, own_small = run(
        functools.partial(unpack_half_kernel, True), "unpack_own",
        [(w_qkv.shape, F32), small_shape], [mine], buffer, {0}, None, semaphore, 24)
    got = last_sum.arrived()[1]
    qkv, *sums = run(
        functools.partial(unpack_half_kernel, False), "unpack_other",
        [(w_qkv.shape, F32)] + [((LAYERS, columns), F32) for columns in widths],
        [got, qkv, own_small], buffer, {0}, {1: 0}, semaphore, 24)
    pair = lambda count, kind: ((2, count, width), kind)
    out_patches, out_specials, grad_patches, grad_specials = run(
        functools.partial(assemble_kernel, plan), "assemble",
        [pair(patch_count, LOW), pair(special_count, LOW), pair(patch_count, F32),
         pair(special_count, F32)],
        [out_kept, out_send, out_got, grad_kept_out, grad_send, grad_got])
    return (
        out_patches, out_specials, grad_patches, grad_specials,
        sums[0], sums[1], qkv, sums[2], proj, sums[3], sums[4], sums[5], fc1, sums[6], fc2, sums[7],
    )


def solution(mesh):
    rows, one = P("pack", "blk", None), P("pack", None, None)
    in_specs = (rows, one, P("pack", None), P("pack", None)) + (P(),) * 12 + (rows, one)
    out_specs = (rows, one, rows, one) + (P(),) * 12
    return jax.shard_map(
        on_device, mesh=mesh, in_specs=in_specs, out_specs=out_specs, check_vma=False
    )
```

```python
import functools

import jax
import jax.numpy as jnp
from jax import lax
from jax.experimental import pallas as pl
from jax.experimental.pallas import tpu as pltpu
from jax.sharding import PartitionSpec as P

HEADS = 6
HEAD_DIM = 64
LAYERS = 2
PAIRS = HEADS // 2
LANES = 128
SPLITS = 3
BLOCKED = -1e30
NORM_EPS = 1e-06
ROOT_HALF = 0.7071067811865476
INV_ROOT_TWO_PI = 0.3989422804014327
F32 = jnp.float32
LOW = jnp.bfloat16
MIB = 1024 * 1024
ORDER = "acbcagbcabcabcGacbcabbcc"
FLOPS_PER_MICRO = 1.1e9
MICROS = {
    "layer_0_early": 1.0, "layer_1_early": 1.0, "layer_0_forward": 14.0, "layer_1_forward": 15.5, "layer_1_query_grad": 4.0,
    "layer_1_weights": 1.0, "layer_1_key_grad": 14.0, "layer_0_weights": 1.0,
    "layer_0_query_grad": 5.0, "layer_0_key_grad": 1.0, "mix_weights": 2.0, "unpack": 4.0,
    "sum": 10.0,
    "first_sum_split7": 10.0,
    "first_sum_split6": 10.0,
    "first_sum_split5": 10.0,
    "first_sum_add4": 10.0,
    "first_sum_add3": 1.0,
    "first_sum_join2": 10.0,
    "first_sum_join1": 10.0,
    "first_sum_join0": 10.0,
    "second_sum_split7": 10.0,
    "second_sum_split6": 10.0,
    "second_sum_split5": 10.0,
    "second_sum_add4": 10.0,
    "second_sum_add3": 3.0,
    "second_sum_join2": 10.0,
    "second_sum_join1": 10.0,
    "second_sum_join0": 1.0,
    "last_sum_split7": 1.0,
    "last_sum_split6": 10.0,
    "last_sum_split5": 10.0,
    "last_sum_add4": 10.0,
    "last_sum_add3": 10.0,
    "last_sum_join2": 10.0,
    "last_sum_join1": 10.0,
    "last_sum_join0": 10.0,
}


def dot(a, b):
    return jnp.dot(a, b, preferred_element_type=F32)


def dot_nt(a, b):
    return lax.dot_general(a, b, (((1,), (1,)), ((), ())), preferred_element_type=F32)


def dot_tn(a, b):
    return lax.dot_general(a, b, (((0,), (0,)), ((), ())), preferred_element_type=F32)


def lane_ids(rows):
    return lax.broadcasted_iota(jnp.int32, (rows, LANES), 1)


def row_ids(rows, lanes=LANES):
    return lax.broadcasted_iota(jnp.int32, (rows, lanes), 0)


def norm_parts(rows):
    centre = rows - jnp.mean(rows, axis=-1, keepdims=True)
    inverse = lax.rsqrt(jnp.mean(centre * centre, axis=-1, keepdims=True) + NORM_EPS)
    return centre * inverse, inverse


def normed(rows, gain, bias):
    return (norm_parts(rows)[0] * gain + bias).astype(LOW)


def norm_back(grad_out, rows, gain):
    scaled, inverse = norm_parts(rows)
    grad_scaled = grad_out * gain
    grad_rows = inverse * (
        grad_scaled
        - jnp.mean(grad_scaled, axis=-1, keepdims=True)
        - scaled * jnp.mean(grad_scaled * scaled, axis=-1, keepdims=True)
    )
    return grad_rows, scaled


def column_sum(rows):
    return jnp.sum(rows, axis=0, keepdims=True)


class Plan:
    def __init__(self, cycle, patch_count, special_count, image_count):
        self.cycle = cycle
        self.group = cycle // 2
        self.block = patch_count
        self.specials = special_count
        self.images = image_count
        self.patch_rows = cycle * patch_count
        self.special_pad = -(-special_count // LANES) * LANES
        self.rows = self.patch_rows + self.special_pad
        self.own_patch = 2 * patch_count
        self.own = self.own_patch + special_count
        self.extra = image_count + 1
        self.unroll = PAIRS if self.rows <= 2048 else 1

    def place(self):
        me = lax.axis_index("blk")
        return me // self.group, me % self.group

    def at(self, half, other):
        return pl.multiple_of((half * self.group + other) * self.block, self.block)

    def own_rows(self, ref, place):
        return jnp.concatenate(
            [
                ref[pl.ds(self.at(0, place), self.block), :],
                ref[pl.ds(self.at(1, place), self.block), :],
                ref[self.patch_rows : self.patch_rows + self.specials, :],
            ],
            axis=0,
        )


def image_lanes(plan, lengths, pads, pack):
    lane = lane_ids(1)
    start = jnp.zeros((1, LANES), jnp.int32)
    stop, live = start, start
    so_far = jnp.int32(0)
    for image in range(plan.images):
        start = jnp.where(lane == image, so_far, start)
        so_far = so_far + lengths[pack, image]
        stop = jnp.where(lane == image, so_far, stop)
        live = jnp.where(lane == image, so_far - pads[pack, image], live)
    return start, stop, live


def write_masks(plan, lengths, pads, pack, key_extra, query_extra):
    start, stop, live = image_lanes(plan, lengths, pads, pack)
    count = plan.block
    lane = lane_ids(count)
    one, zero = jnp.ones((count, LANES), F32), jnp.zeros((count, LANES), F32)

    @pl.loop(0, plan.cycle)
    def _(step):
        base = pl.multiple_of(step * count, count)
        token = row_ids(count) + base
        inside = (token >= start) & (token < stop)
        alive = (token >= start) & (token < live)
        key_extra[pl.ds(base, count), :] = jnp.where(alive, zero, one).astype(LOW)
        query_extra[pl.ds(base, count), :] = jnp.where(inside, BLOCKED, zero).astype(LOW)

    count = plan.special_pad
    lane, special = lane_ids(count), row_ids(count)
    one, zero = jnp.ones((count, LANES), F32), jnp.zeros((count, LANES), F32)
    mine = (lane == special // 2) & (special < plan.specials)
    never = (lane == plan.images) & (special >= plan.specials)
    key_extra[plan.patch_rows :, :] = jnp.where(mine, zero, one).astype(LOW)
    query_extra[plan.patch_rows :, :] = jnp.where(mine | never, BLOCKED, zero).astype(LOW)


def project(plan, rows, places, weight, shift, mixed):
    out = (dot(rows, weight[...]) + shift).astype(LOW)
    at = 0
    for first, count in places:
        here = pl.ds(first, count)
        for part in range(3 * PAIRS):
            mixed[part, here, :] = out[at : at + count, part * LANES : (part + 1) * LANES]
        at += count


def project_pieces(plan, place, pieces, masks, weight, shift, mixed):
    for piece, mask in zip(pieces, masks):
        other = jnp.bitwise_xor(place, mask)
        places = [(plan.at(half, other), plan.block) for half in range(2)]
        project(plan, piece[...], places, weight, shift, mixed)


def padded_specials(plan, rows):
    pad = jnp.zeros((plan.special_pad - plan.specials, rows.shape[1]), LOW)
    return jnp.concatenate([rows, pad], axis=0) if pad.shape[0] else rows


def shift_row(qv_bias):
    width = qv_bias.shape[1] // 2
    return jnp.concatenate(
        [qv_bias[:, :width], jnp.zeros((1, width), F32), qv_bias[:, width:]], axis=1
    )


def attend(plan, place, mixed, key_extra, query_extra, keys, joined, total):
    lane = lane_ids(plan.own)
    own_extra = plan.own_rows(query_extra, place)
    keys[:, LANES:] = key_extra[...]
    total[...] = jnp.zeros_like(total)

    ones = jnp.ones((plan.rows, LANES), LOW)

    @pl.loop(0, PAIRS, unroll=plan.unroll)
    def _(pair):
        query = (plan.own_rows(mixed.at[pair], place).astype(F32) * 0.125).astype(LOW)
        keys[:, :LANES] = mixed[PAIRS + pair]
        values = jnp.concatenate([mixed[2 * PAIRS + pair], ones], axis=1)
        scores, out, logs = [], [], total[...]
        for side in range(2):
            mine = (lane // HEAD_DIM) == side
            left = jnp.concatenate([jnp.where(mine, query, 0), own_extra], axis=1)
            scores.append(dot_nt(left, keys[...]))
        for side in range(2):
            top = jnp.max(scores[side], axis=-1, keepdims=True)
            both = dot(jnp.exp(scores[side] - top).astype(LOW), values)
            out.append(both[:, :LANES] / both[:, LANES:])
            logs = jnp.where(lane == 2 * pair + side, top + jnp.log(both[:, LANES:]), logs)
        joined[pair] = jnp.where(lane < HEAD_DIM, out[0], out[1])
        total[...] = logs


def feed_forward(second_normed, fc1, fc1_bias, fc2, hidden, slope):
    out = None
    width = second_normed.shape[1]
    for first in range(0, fc1.shape[1], width):
        here = slice(first, first + width)
        pre = dot(second_normed, fc1[:, here]) + fc1_bias[:, here]
        cdf = 0.5 * (1.0 + lax.erf(pre * ROOT_HALF))
        pdf = jnp.exp(-0.5 * pre * pre) * INV_ROOT_TWO_PI
        value = (pre * cdf).astype(LOW)
        hidden[:, here] = value
        slope[:, here] = (cdf + pre * pdf).astype(LOW)
        part = dot(value, fc2[here, :])
        out = part if out is None else out + part
    return out


def forward_rest(layer, start, joined, w_proj, proj_bias, ln2_gain, ln2_bias, w_fc1, fc1_bias,
                 w_fc2, fc2_bias, hidden, slope, middle):
    row = slice(layer, layer + 1)
    attended = jnp.concatenate([joined[pair] for pair in range(PAIRS)], axis=1)
    after = start + dot(attended.astype(LOW), w_proj.ready()[...]) + proj_bias[row, :]
    middle[...] = after
    second = normed(after, ln2_gain[row, :], ln2_bias[row, :])
    out = feed_forward(second, w_fc1.ready(), fc1_bias[row, :], w_fc2.ready(), hidden, slope)
    return after + out + fc2_bias[row, :]


def block_places(plan, place, half, indices):
    return [
        plan.at(half if index < plan.group else 1 - half, jnp.bitwise_xor(place, index % plan.group))
        for index in indices
    ]


def early_kernel(plan, indices, *refs):
    blocks, refs = refs[: len(indices)], refs[len(indices) :]
    (lengths, pads, specials, ln1_gain, ln1_bias, w_qkv, qv_bias,
     key_extra, query_extra, mixed, start, own_normed, weight) = refs
    half, place = plan.place()
    write_masks(plan, lengths, pads, half, key_extra, query_extra)
    gain, bias = ln1_gain[0:1, :], ln1_bias[0:1, :]
    low_rows = []
    for index, ref in zip(indices, blocks):
        rows = ref[...].astype(F32)
        low_rows.append(normed(rows, gain, bias))
        if index % plan.group == 0:
            side = half if index < plan.group else 1 - half
            here = pl.ds(pl.multiple_of(side * plan.block, plan.block), plan.block)
            start[here, :] = rows
            own_normed[here, :] = low_rows[-1]
    rows = specials[half].astype(F32)
    special_rows = normed(rows, gain, bias)
    start[plan.own_patch :, :] = rows
    own_normed[plan.own_patch :, :] = special_rows
    shift = shift_row(qv_bias[0:1, :])
    count = len(indices) * plan.block
    rows = jnp.concatenate(low_rows, axis=0)
    project(plan, rows, [(0, count)], w_qkv.ready(), shift, mixed)
    rows = padded_specials(plan, special_rows)
    project(plan, rows, [(count, plan.special_pad)], w_qkv.ready(), shift, mixed)
    weight[...] = w_qkv[...]


def take_early(plan, early, firsts, mixed):
    at = 0
    for first, count in [(first, plan.block) for first in firsts] + [(plan.patch_rows, plan.special_pad)]:
        mixed[:, pl.ds(first, count), :] = early[:, at : at + count, :]
        at += count


def first_kernel(plan, early, indices, *refs):
    blocks, refs = refs[: len(indices)], refs[len(indices) :]
    (mixed_in, key_extra, query_extra, start,
     weight, ln1_gain, ln1_bias, qv_bias, w_proj, proj_bias, ln2_gain,
     ln2_bias, w_fc1, fc1_bias, w_fc2, fc2_bias,
     mixed, middle, joined, total, hidden, slope, after, send, keep, next_normed, keys) = refs
    half, place = plan.place()
    gain, bias = ln1_gain[0:1, :], ln1_bias[0:1, :]
    take_early(plan, mixed_in, block_places(plan, place, half, early), mixed)
    places = block_places(plan, place, half, indices)
    for first in range(0, len(indices), 4):
        some = slice(first, first + 4)
        rows = [normed(ref[...].astype(F32), gain, bias) for ref in blocks[some]]
        project(plan, jnp.concatenate(rows, axis=0), [(at, plan.block) for at in places[some]],
                weight, shift_row(qv_bias[0:1, :]), mixed)
    attend(plan, place, mixed, key_extra, query_extra, keys, joined, total)
    joined.send()
    out = forward_rest(0, start[...], joined, w_proj, proj_bias, ln2_gain, ln2_bias, w_fc1,
                       fc1_bias, w_fc2, fc2_bias, hidden, slope, middle)
    for ref in (middle, slope):
        ref.send()
    after[...] = out
    following = normed(out, ln1_gain[1:2, :], ln1_bias[1:2, :])
    send[...] = following[: plan.own_patch]
    keep[...] = following[plan.own_patch :]
    next_normed[...] = following


def split_low(values):
    parts, rest = [], values
    for _ in range(SPLITS):
        part = rest.astype(LOW)
        parts.append(part)
        rest = rest - part.astype(F32)
    return parts


def backward_rest(plan, layer, grad_rows, scale, middle, joined, total, hidden, slope, ln2_gain,
                  ln2_bias, w_fc1, w_fc2, w_proj, small, second, second_grad, pre_grad,
                  attended_low, first_grad, send, out_grad, logs):
    row = slice(layer, layer + 1)
    width = grad_rows.shape[1]
    low_grad = grad_rows.astype(LOW)
    second_grad[...] = low_grad
    after = middle[...]
    second[...] = normed(after, ln2_gain[row, :], ln2_bias[row, :])
    grad_second = None
    for first in range(0, slope.shape[1], width):
        here = slice(first, first + width)
        value = (dot_nt(low_grad, w_fc2.ready()[here, :]) * slope[:, here].astype(F32)).astype(LOW)
        pre_grad[:, here] = value
        small[6:7, here] = column_sum(value.astype(F32) * scale)
        part = dot_nt(value, w_fc1.ready()[:, here])
        grad_second = part if grad_second is None else grad_second + part
    change, scaled = norm_back(grad_second, after, ln2_gain[row, :])
    weighted = grad_second * scale
    grad_middle = grad_rows + change
    low_middle = grad_middle.astype(LOW)
    first_grad[...] = low_middle
    small[3:4, :width] = column_sum(low_middle.astype(F32) * scale)
    small[4:5, :width] = column_sum(weighted * scaled)
    small[5:6, :width] = column_sum(weighted)
    small[7:8, :width] = column_sum(low_grad.astype(F32) * scale)
    grad_out = dot_nt(low_middle, w_proj.ready()[...]).astype(LOW)
    out_grad[...] = grad_out
    lane = lane_ids(plan.own)
    table = total[...]
    for pair in range(PAIRS):
        here = slice(pair * LANES, (pair + 1) * LANES)
        attended = joined[pair]
        attended_low[:, here] = attended.astype(LOW)
        product = grad_out[:, here].astype(F32) * attended
        for side in range(2):
            mine = (lane // HEAD_DIM) == side
            delta = jnp.sum(jnp.where(mine, product, 0.0), axis=-1, keepdims=True)
            table = jnp.where(lane == HEADS + 2 * pair + side, delta, table)
    logs[...] = table
    send[: plan.own_patch, :] = grad_out[: plan.own_patch]
    pick = jnp.where(row_ids(16) == lane_ids(16), 1.0, 0.0).astype(LOW)
    parts = split_low(table)
    for part in range(2):
        rows = slice(part * plan.block, (part + 1) * plan.block)
        turned = [dot_nt(pick, values[rows]).astype(LOW) for values in parts]
        first = plan.own_patch + 16 * part
        send[first : first + 16, :] = jnp.concatenate(turned, axis=1)
    return grad_middle


def assemble_kernel(plan, *refs):
    half = plan.place()[0]
    for (kept, sent, got), (rows, specials) in ((refs[:3], refs[6:8]), (refs[3:6], refs[8:10])):
        rows[half] = kept[...]
        rows[1 - half] = got[: plan.block, :].astype(rows.dtype)
        specials[half] = sent[plan.block :, :].astype(rows.dtype)
        specials[1 - half] = got[plan.block :, :].astype(rows.dtype)


def owner_scale(plan, place):
    row = lax.broadcasted_iota(jnp.int32, (plan.own, 1), 0)
    return jnp.where((row < plan.own_patch) | (place == 0), 1.0, 0.0)


def second_early_kernel(plan, masks, *refs):
    pieces, refs = refs[: len(masks)], refs[len(masks) :]
    normed_specials, w_qkv, qv_bias, mixed, weight = refs
    shift = shift_row(qv_bias[1:2, :])
    at = 0
    for piece in pieces:
        project(plan, piece[...], [(at, plan.own_patch)], w_qkv.ready(), shift, mixed)
        at += plan.own_patch
    rows = padded_specials(plan, normed_specials[...])
    project(plan, rows, [(at, plan.special_pad)], w_qkv.ready(), shift, mixed)
    weight[...] = w_qkv[...]


def second_kernel(plan, early, masks, *refs):
    pieces, refs = refs[: len(masks)], refs[len(masks) :]
    (mixed_in, key_extra, query_extra, start, grad_kept, grad_swapped, grad_specials,
     weight, qv_bias, w_proj, proj_bias, ln2_gain, ln2_bias, w_fc1, fc1_bias, w_fc2, fc2_bias,
     mixed, out_kept, out_send, grad_middle, send, out_grad, logs, small, second, second_grad,
     pre_grad, attended_low, first_grad, hidden,
     keys, joined, total, slope, middle) = refs
    half, place = plan.place()
    others = [jnp.bitwise_xor(place, mask) for mask in early]
    firsts = [plan.at(which, other) for other in others for which in range(2)]
    take_early(plan, mixed_in, firsts, mixed)
    project_pieces(plan, place, pieces, masks, weight, shift_row(qv_bias[1:2, :]), mixed)
    attend(plan, place, mixed, key_extra, query_extra, keys, joined, total)
    out = forward_rest(1, start[...], joined, w_proj, proj_bias, ln2_gain, ln2_bias, w_fc1,
                       fc1_bias, w_fc2, fc2_bias, hidden, slope, middle)
    low_out = out.astype(LOW)
    first, later = low_out[: plan.block], low_out[plan.block : plan.own_patch]
    out_kept[...] = jnp.where(half == 0, first, later)
    out_send[: plan.block, :] = jnp.where(half == 0, later, first)
    out_send[plan.block :, :] = low_out[plan.own_patch :]
    kept, swapped = grad_kept[...].astype(F32), grad_swapped[...].astype(F32)
    own_extra = plan.own_rows(key_extra, place)[: plan.own_patch].astype(F32)
    lane = lane_ids(plan.own_patch)
    live = jnp.sum(jnp.where(lane < plan.images, 1.0 - own_extra, 0.0), axis=-1, keepdims=True)
    patch_grad = jnp.concatenate(
        [jnp.where(half == 0, kept, swapped), jnp.where(half == 0, swapped, kept)], axis=0
    )
    grad_rows = jnp.concatenate([patch_grad * live, grad_specials[half].astype(F32)], axis=0)
    small[0:3, :] = jnp.zeros((3, small.shape[1]), F32)
    grad_middle[...] = backward_rest(
        plan, 1, grad_rows, owner_scale(plan, place), middle, joined, total, hidden, slope,
        ln2_gain, ln2_bias, w_fc1, w_fc2, w_proj, small, second, second_grad, pre_grad,
        attended_low, first_grad, send, out_grad, logs)


def placed(plan, rows, first_row, first_lane):
    row, lane = row_ids(rows), lane_ids(rows)
    out = []
    for split in range(SPLITS):
        head = row - first_row
        hit = (head >= 0) & (head < HEADS) & (lane == first_lane + SPLITS * head + split)
        out.append(jnp.where(hit, -1.0, 0.0).astype(LOW))
    return out


def spread_logs(plan, table, first_row):
    picks = placed(plan, LANES, first_row, plan.extra)
    return sum(dot(values, pick) for values, pick in zip(split_low(table), picks)).astype(LOW)


def head_lanes(plan, lane, head):
    first = plan.extra + SPLITS * head
    return (lane >= first) & (lane < first + SPLITS)


def query_grad_kernel(plan, mixed, key_extra, query_extra, out_grad, logs, grad_query, keys, values):
    _, place = plan.place()
    lane = lane_ids(plan.own)
    own_extra = plan.own_rows(query_extra, place)
    log_extra = spread_logs(plan, logs[...], 0)
    delta_extra = spread_logs(plan, logs[...], HEADS)
    keys[:, LANES:] = key_extra[...]
    values[:, LANES:] = key_extra[...]

    @pl.loop(0, PAIRS, unroll=plan.unroll)
    def _(pair):
        query = (plan.own_rows(mixed.at[pair], place).astype(F32) * 0.125).astype(LOW)
        here = pl.ds(pl.multiple_of(pair * LANES, LANES), LANES)
        grad_out = out_grad[:, here]
        keys[:, :LANES] = mixed[PAIRS + pair]
        values[:, :LANES] = mixed[2 * PAIRS + pair]
        out = []
        for side in range(2):
            mine = (lane // HEAD_DIM) == side
            head = head_lanes(plan, lane, 2 * pair + side)
            left = jnp.concatenate(
                [jnp.where(mine, query, 0), jnp.where(head, log_extra, own_extra)], axis=1
            )
            probs = jnp.exp(dot_nt(left, keys[...]))
            left = jnp.concatenate(
                [jnp.where(mine, grad_out, 0), jnp.where(head, delta_extra, 0)], axis=1
            )
            grad_scores = (probs * dot_nt(left, values[...])).astype(LOW)
            out.append(dot(grad_scores, mixed[PAIRS + pair]) * 0.125)
        grad_query[:, here] = jnp.where(lane < HEAD_DIM, out[0], out[1]).astype(LOW)


def key_grads(plan, place, pieces, mixed, key_extra, query_extra, out_grad, logs, grad_mixed,
              queries, grads, all_grads, unroll=1):
    log_rows = placed(plan, 16, 0, plan.extra)
    delta_rows = placed(plan, 16, HEADS, plan.extra)
    picks = [jnp.concatenate(two, axis=1) for two in zip(log_rows, delta_rows)]
    for index, ref in enumerate(pieces):
        other = jnp.bitwise_xor(place, index)
        for half in range(2):
            here = pl.ds(plan.at(half, other), plan.block)
            for pair in range(PAIRS):
                all_grads[pair, here, :] = ref[
                    half * plan.block : (half + 1) * plan.block, pair * LANES : (pair + 1) * LANES
                ]
            first = plan.own_patch + 16 * half
            both = sum(
                dot_tn(ref[first : first + 16, split * LANES : (split + 1) * LANES], picks[split])
                for split in range(SPLITS)
            )
            queries[here, LANES:] = (both[:, :LANES] + query_extra[here, :].astype(F32)).astype(LOW)
            grads[here, LANES:] = both[:, LANES:].astype(LOW)
    last, stop = plan.patch_rows, plan.patch_rows + plan.specials
    table = logs[plan.own_patch :, :]
    log_extra = spread_logs(plan, table, 0).astype(F32)
    queries[last:, LANES:] = query_extra[last:, :]
    queries[last:stop, LANES:] = (log_extra + query_extra[last:stop, :].astype(F32)).astype(LOW)
    grads[last:, LANES:] = jnp.zeros((plan.special_pad, LANES), LOW)
    grads[last:stop, LANES:] = spread_logs(plan, table, HEADS)
    for pair in range(PAIRS):
        all_grads[pair, last:, :] = jnp.zeros((plan.special_pad, LANES), LOW)
        all_grads[pair, last:stop, :] = out_grad[
            plan.own_patch :, pair * LANES : (pair + 1) * LANES
        ]
    lane = lane_ids(plan.own)
    own_extra = plan.own_rows(key_extra, place)
    own_extra = jnp.where(lane < plan.extra, own_extra, 0)

    @pl.loop(0, PAIRS, unroll=unroll)
    def _(pair):
        queries[:, :LANES] = (mixed[pair].astype(F32) * 0.125).astype(LOW)
        grads[:, :LANES] = all_grads[pair]
        key = plan.own_rows(mixed.at[PAIRS + pair], place)
        value = plan.own_rows(mixed.at[2 * PAIRS + pair], place)
        grad_key, grad_value = [], []
        for side in range(2):
            mine = (lane // HEAD_DIM) == side
            head = head_lanes(plan, lane, 2 * pair + side)
            extra = jnp.where(head, 1.0, own_extra.astype(F32)).astype(LOW)
            left = jnp.concatenate([jnp.where(mine, key, 0), extra], axis=1)
            probs = jnp.exp(dot_nt(left, queries[...]))
            left = jnp.concatenate([jnp.where(mine, value, 0), extra], axis=1)
            grad_scores = (probs * dot_nt(left, grads[...])).astype(LOW)
            grad_key.append(dot(grad_scores, queries[:, :LANES]))
            grad_value.append(dot(probs.astype(LOW), all_grads[pair]))
        width = PAIRS * LANES
        here = pl.ds(pl.multiple_of(width + pair * LANES, LANES), LANES)
        grad_mixed[:, here] = jnp.where(lane < HEAD_DIM, *grad_key).astype(LOW)
        here = pl.ds(pl.multiple_of(2 * width + pair * LANES, LANES), LANES)
        grad_mixed[:, here] = jnp.where(lane < HEAD_DIM, *grad_value).astype(LOW)


def first_norm_back(plan, layer, scale, grad_mixed, w_qkv, start, ln1_gain, small):
    width = start.shape[1]
    mixed = grad_mixed[...]
    sums = column_sum(mixed.astype(F32) * scale)
    small[2:3, : 2 * width] = jnp.concatenate([sums[:, :width], sums[:, 2 * width :]], axis=1)
    grad_normed = dot_nt(mixed, w_qkv.ready()[...])
    change, scaled = norm_back(grad_normed, start[...], ln1_gain[layer : layer + 1, :])
    weighted = grad_normed * scale
    small[0:1, :width] = column_sum(weighted * scaled)
    small[1:2, :width] = column_sum(weighted)
    return change


def third_kernel(plan, *refs):
    pieces, refs = refs[: plan.group], refs[plan.group :]
    (mixed, key_extra, query_extra, later_grad, later_logs, grad_query, later_start, later_middle,
     later_small, ln1_gain, later_qkv,
     middle, joined, total, hidden, slope, ln2_gain, ln2_bias, w_fc1, w_fc2, w_proj,
     grad_mixed, small_out, grad_middle, send, out_grad, logs, small, second, second_grad,
     pre_grad, attended_low, first_grad,
     queries, grads, all_grads) = refs
    _, place = plan.place()
    scale = owner_scale(plan, place)
    grad_mixed[:, : grad_query.shape[1]] = grad_query[...]
    key_grads(plan, place, pieces, mixed, key_extra, query_extra, later_grad, later_logs,
              grad_mixed, queries, grads, all_grads)
    small_out[...] = later_small[...]
    grad_rows = later_middle[...] + first_norm_back(
        plan, 1, scale, grad_mixed, later_qkv, later_start, ln1_gain, small_out
    )
    small[0:3, :] = jnp.zeros((3, small.shape[1]), F32)
    grad_middle[...] = backward_rest(
        plan, 0, grad_rows, scale, middle, joined, total, hidden, slope, ln2_gain, ln2_bias,
        w_fc1, w_fc2, w_proj, small, second, second_grad, pre_grad, attended_low, first_grad,
        send, out_grad, logs)


def fourth_kernel(plan, *refs):
    pieces, refs = refs[: plan.group], refs[plan.group :]
    (mixed, key_extra, query_extra, out_grad, logs, grad_query, start, grad_middle, small, ln1_gain,
     w_qkv,
     grad_mixed, small_out, grad_kept, grad_send,
     queries, grads, all_grads) = refs
    half, place = plan.place()
    scale = owner_scale(plan, place)
    grad_mixed[:, : grad_query.shape[1]] = grad_query[...]
    key_grads(plan, place, pieces, mixed, key_extra, query_extra, out_grad, logs, grad_mixed,
              queries, grads, all_grads, plan.unroll)
    small_out[...] = small[...]
    out = grad_middle[...] + first_norm_back(
        plan, 0, scale, grad_mixed, w_qkv, start, ln1_gain, small_out
    )
    first, later = out[: plan.block], out[plan.block : plan.own_patch]
    grad_kept[...] = jnp.where(half == 0, first, later)
    grad_send[: plan.block, :] = jnp.where(half == 0, later, first).astype(LOW)
    grad_send[plan.block :, :] = out[plan.own_patch :].astype(LOW)


def weight_kernel(plan, groups, *refs):
    kept, sent, out = refs[-3:]
    keep = owner_scale(plan, plan.place()[1])
    refs, at, end = list(refs[:-3]), 0, 0
    for count, small_count, rows in groups:
        end += rows
        for _ in range(count):
            left = (refs.pop(0)[...].astype(F32) * keep).astype(LOW)
            right = refs.pop(0)
            step = min(384, right.shape[1])
            for first in range(0, right.shape[1], step):
                product = dot_tn(left, right[:, first : first + step]).astype(LOW)
                for column in range(0, step, LANES):
                    out[at : at + left.shape[1], :] = product[:, column : column + LANES]
                    at += left.shape[1]
        for _ in range(small_count):
            small = refs.pop(0)[...]
            for column in range(0, small.shape[1], 2 * LANES):
                two = small[:, column : column + 2 * LANES]
                both = jnp.concatenate([two[:, :LANES], two[:, LANES:]], axis=0)
                out[at : at + 16, :] = both.astype(LOW)
                at += 16
        if at < end:
            out[at:end, :] = jnp.zeros((end - at, LANES), LOW)
        at = end
    size = kept.shape[0]
    core = lax.axis_index("blk") % 2
    kept[...] = out[pl.ds(pl.multiple_of(core * size, 16), size), :]
    sent[...] = out[pl.ds(pl.multiple_of((1 - core) * size, 16), size), :]


def side_of(axis, bits):
    place = lax.axis_index("blk")
    bit = jnp.where(place % 2 == 0, bits[0], bits[1])
    if axis == "blk":
        return (place >> bit) & 1
    return (lax.axis_index("pack") >> bit) & 1


def split_kernel(axis, bits, mine, got, kept, sent):
    size = kept.shape[0]
    side = side_of(axis, bits)
    for which, out in ((side, kept), (1 - side, sent)):
        here = pl.ds(pl.multiple_of(which * size, 16), size)
        out[...] = (mine[here, :].astype(F32) + got[here, :].astype(F32)).astype(LOW)


def add_kernel(mine, got, out):
    out[...] = (mine[...].astype(F32) + got[...].astype(F32)).astype(LOW)


def join_kernel(axis, bits, mine, got, out):
    size = mine.shape[0]
    side = side_of(axis, bits)
    out[pl.ds(pl.multiple_of(side * size, 16), size), :] = mine[...]
    out[pl.ds(pl.multiple_of((1 - side) * size, 16), size), :] = got[...]


def unpack_kernel(entries, filled, *refs):
    outs = refs[2 + filled :]
    rows, semaphores = outs[-2], outs[-1]
    buffers = outs[len(outs) - 2 - len(entries) : -2]
    core = lax.axis_index("blk") % 2
    size = refs[0].shape[0]
    rows[pl.ds(pl.multiple_of(core * size, 16), size), :] = refs[0][...]
    rows[pl.ds(pl.multiple_of((1 - core) * size, 16), size), :] = refs[1][...]
    at, copies = 0, []
    for number, (output, layer, height, columns) in enumerate(entries):
        buffer = buffers[number]
        for first in range(0, columns, LANES):
            buffer[:, first : first + LANES] = rows[at : at + height, :].astype(F32)
            at += height
        copies.append(
            pltpu.make_async_copy(buffer, outs[output].at[layer], semaphores.at[number])
        )
        copies[-1].start()
    for copy in copies:
        copy.wait()


def unpack_half_kernel(first, *refs):
    if first:
        rows, stacked, small_out, buffer, semaphore = refs
    else:
        rows, _, own_small, stacked, *sums, buffer, semaphore = refs
    core = lax.axis_index("blk") % 2
    layer = core if first else 1 - core
    height, columns = buffer.shape
    at = 0
    for column in range(0, columns, LANES):
        buffer[:, column : column + LANES] = rows[at : at + height, :].astype(F32)
        at += height
    copy = pltpu.make_async_copy(buffer, stacked.at[layer], semaphore.at[0])
    copy.start()
    blocks = []
    width = (small_out if first else own_small).shape[1]
    for _ in range(width // (2 * LANES)):
        both = rows[at : at + 16, :].astype(F32)
        blocks += [both[:8], both[8:]]
        at += 16
    small = jnp.concatenate(blocks, axis=1)
    if first:
        small_out[...] = small
    else:
        own = own_small[...]
        parts = [jnp.where(core == 0, own, small), jnp.where(core == 0, small, own)]
        for row, out in enumerate(sums):
            count = out.shape[1]
            out[...] = jnp.concatenate([part[row : row + 1, :count] for part in parts], axis=0)
    copy.wait()


VMEM = pl.BlockSpec(memory_space=pltpu.VMEM)


ANY = pl.BlockSpec(memory_space=pl.ANY)
HBM = pl.BlockSpec(memory_space=pltpu.HBM)


WHOLE = -1


class Staged:
    def __init__(self, source, layer, target, semaphore):
        self.target = target
        source = source if layer == WHOLE else source.at[layer]
        self.copy = pltpu.make_async_copy(source, target, semaphore)
        self.copy.start()
        self.waits = True

    def ready(self):
        if self.waits:
            self.copy.wait()
            self.waits = False
        return self.target

    @property
    def shape(self):
        return self.target.shape

    def __getitem__(self, index):
        return self.ready()[index]


class Late:
    def __init__(self, out, buffer, semaphore):
        self.buffer, self.copy, self.sent = buffer, pltpu.make_async_copy(buffer, out, semaphore), False

    @property
    def shape(self):
        return self.buffer.shape

    def __getitem__(self, index):
        return self.buffer[index]

    def __setitem__(self, index, value):
        self.buffer[index] = value

    def send(self):
        self.copy.start()
        self.sent = True

    def finish(self):
        if not self.sent:
            self.send()
        self.copy.wait()


def staged_kernel(kernel, layers, out_count, late, *refs):
    ins, outs = list(refs[: len(layers)]), list(refs[len(layers) : len(layers) + out_count])
    rest = refs[len(layers) + out_count :]
    chosen = [index for index, layer in enumerate(layers) if layer is not None]
    if not chosen and not late:
        return kernel(*refs)
    count = len(chosen) + len(late)
    buffers, semaphores = rest[:count], rest[count]
    for number, index in enumerate(chosen):
        ins[index] = Staged(ins[index], layers[index], buffers[number], semaphores.at[number])
    for number, index in enumerate(late, len(chosen)):
        outs[index] = Late(outs[index], buffers[number], semaphores.at[number])
    kernel(*ins, *outs, *rest[count + 1 :])
    for index in late:
        outs[index].finish()
    for index in chosen:
        ins[index].ready()


def run(kernel, name, outs, ins, scratch=(), far_outs=(), aliases=None, plain=(), mib=12,
        late=()):
    micros = MICROS.get(name) or MICROS["unpack" if name.startswith("unpack") else "sum"]
    specs, values, layers, buffers = [], [], [], []
    far_ins = {index for index, output in (aliases or {}).items() if output in far_outs}
    for index, item in enumerate(ins):
        value, layer = item if isinstance(item, tuple) else (item, None)
        if layer is not None:
            specs.append(HBM)
        elif index in far_ins:
            specs.append(ANY)
        else:
            specs.append(VMEM)
        if layer is not None:
            space = pltpu.SMEM if value.dtype == jnp.int32 else pltpu.VMEM
            buffers.append(space(value.shape[0 if layer == WHOLE else 1 :], value.dtype))
            value = pltpu.with_memory_space_constraint(value, pltpu.HBM)
        layers.append(layer)
        values.append(value)
    buffers += [pltpu.VMEM(*outs[index]) for index in late]
    if buffers:
        buffers.append(pltpu.SemaphoreType.DMA((len(buffers),)))
    return pl.pallas_call(
        functools.partial(staged_kernel, kernel, layers, len(outs), late),
        out_shape=[
            (pltpu.HBM if index in late else jax.ShapeDtypeStruct)(shape, kind)
            for index, (shape, kind) in enumerate(outs)
        ],
        in_specs=specs,
        out_specs=[
            HBM if index in late else ANY if index in far_outs else VMEM for index in range(len(outs))
        ],
        scratch_shapes=buffers + [pltpu.VMEM(shape, kind) for shape, kind in scratch] + list(plain),
        input_output_aliases=aliases or {},
        compiler_params=pltpu.CompilerParams(vmem_limit_bytes=mib * MIB),
        cost_estimate=pl.CostEstimate(
            flops=int(micros * FLOPS_PER_MICRO), bytes_accessed=0, transcendentals=0
        ),
        name=name,
    )(*values)


def swap(value, mask):
    size = lax.axis_size("blk")
    return lax.ppermute(value, "blk", [(i, i ^ mask) for i in range(size)])


def spread(value, group, then=None, near=None):
    held = {0: value}
    mask = group // 2
    if then is not None:
        held[mask] = swap(value, mask)
        (held[0], held[mask]), then = tie([held[0], held[mask]], then)
        mask //= 2
    while mask:
        for index, item in list(held.items()):
            held[index | mask] = (near or {}).get(index | mask)
            if held[index | mask] is None:
                held[index | mask] = swap(item, mask)
        mask //= 2
    pieces = [held[index] for index in range(group)]
    return pieces if then is None else (pieces, then)


def exchange(value, axis, bits):
    masks = [1 << bit for bit in bits]
    cycle = lax.axis_size("blk")
    pairs = []
    for device in range(lax.axis_size("pack") * cycle):
        pack, place = divmod(device, cycle)
        mask = masks[place % 2]
        other = (pack, place ^ mask) if axis == "blk" else (pack ^ mask, place)
        pairs.append((device, other[0] * cycle + other[1]))
    return lax.ppermute(value, ("pack", "blk"), pairs)


def tie(*groups):
    return lax.optimization_barrier(groups)


class Summing:
    def __init__(self, name, kept, sent):
        self.name = name
        self.values = [kept, sent, None]
        chips = list(range(1, lax.axis_size("blk").bit_length() - 1))
        packs = list(range(lax.axis_size("pack").bit_length() - 1))
        parts = [("blk", pair) for pair in zip(chips, reversed(chips))]
        parts += [("pack", (bit, bit)) for bit in packs[:-1]]
        self.steps = [("split", part, part) for part in parts]
        self.steps += [("add", None, ("pack", (packs[-1], packs[-1]))), ("add", None, parts[-1])]
        for part, then in zip(parts[::-1], parts[-2::-1] + [None]):
            self.steps.append(("join", part, then))

    def after(self, *others):
        tied = tie(self.values[:1], list(others))
        self.values[0] = tied[0][0]
        return tied[1] if len(others) > 1 else tied[1][0]

    def arrived(self):
        if len(self.values) == 3:
            mine, sent, then = self.values
            self.values = [mine, swap(sent, 1) if then is None else exchange(sent, *then)]
        return self.values

    def step(self, last=None):
        if last is not None:
            self.after(last)
        self.arrived()
        kind, part, then = self.steps.pop(0)
        name = f"{self.name}_{kind}{len(self.steps)}"
        size = self.values[0].shape[0]
        shape = lambda count: ((count, LANES), LOW)
        if kind == "split":
            kernel = functools.partial(split_kernel, *part)
            mine, sent = run(kernel, name, [shape(size // 2)] * 2, self.values)
        elif kind == "add":
            mine = sent = run(add_kernel, name, [shape(size)], self.values)[0]
        else:
            kernel = functools.partial(join_kernel, *part)
            mine = sent = run(kernel, name, [shape(2 * size)], self.values)[0]
        self.values = [mine, swap(sent, 1) if then is None else exchange(sent, *then)]
        return mine


def unpacked(name, values, entries, shapes, filled):
    ins = list(values) + [filled[k] for k in sorted(filled)]
    aliases = {2 + index: output for index, output in enumerate(sorted(filled))}
    total = sum(value.shape[0] for value in values)
    scratch = [((rows, columns), F32) for _, _, rows, columns in entries] + [((total, LANES), LOW)]
    kernel = functools.partial(unpack_kernel, entries, len(filled))
    return run(kernel, name, [(shape, F32) for shape in shapes], ins, scratch,
               set(range(len(shapes))), aliases, [pltpu.SemaphoreType.DMA((len(entries),))], 24)


def on_device(patches, specials, image_lengths, pad_counts, ln1_gain, ln1_bias, w_qkv, qv_bias,
              w_proj, proj_bias, ln2_gain, ln2_bias, w_fc1, fc1_bias, w_fc2, fc2_bias, d_patches,
              d_specials):
    ln1, ln1_shift, ln2, ln2_shift = [(v, WHOLE) for v in (ln1_gain, ln1_bias, ln2_gain, ln2_bias)]
    qv_shift, proj_shift = (qv_bias, WHOLE), (proj_bias, WHOLE)
    fc1_shift, fc2_shift = (fc1_bias, WHOLE), (fc2_bias, WHOLE)
    cycle, pack_size = lax.axis_size("blk"), lax.axis_size("pack")
    patch_count, special_count, width = patches.shape[1], specials.shape[1], patches.shape[2]
    hidden_width = w_fc1.shape[2]
    plan = Plan(cycle, patch_count, special_count, image_lengths.shape[1])
    own, rows, group = plan.own, plan.rows, plan.group
    half = lax.axis_index("blk") // group

    def kept_and_sent(pair):
        return (lax.dynamic_index_in_dim(pair, half, 0, keepdims=False),
                lax.dynamic_index_in_dim(pair, 1 - half, 0, keepdims=False))

    kept, sent = kept_and_sent(patches)
    swapped = swap(sent, group)
    blocks = spread(kept, group) + [swapped]
    early = [0, group, 1 % group, group // 2]
    early = sorted(set(early))
    rest = [index for index in range(2 * group) if index not in early]

    mib = max(12, rows // 90)
    more = max(26, rows // 90)
    extra_shape = ((rows, LANES), LOW)
    mixed_shape = ((3 * PAIRS, rows, LANES), LOW)
    joined_shape = ((PAIRS, own, LANES), F32)
    wide, wide_low = ((own, width), F32), ((own, width), LOW)
    hidden_shape, slope_shape = ((own, hidden_width), LOW), ((own, hidden_width), LOW)
    table_shape = ((own, LANES), F32)
    small_shape = ((8, hidden_width), F32)
    send_shape = ((plan.own_patch + 32, width), LOW)
    double_shape = ((rows, 2 * LANES), LOW)
    all_grads_shape = ((PAIRS, rows, LANES), LOW)

    def weights(name, *groups):
        multiple = 16 * cycle * pack_size // len(groups)
        plans, flat = [], []
        for products, small in groups:
            used = sum(a.shape[1] * b.shape[1] for a, b in products) // LANES
            used += len(small) * 8 * hidden_width // LANES
            plans.append((len(products), len(small), -(-used // multiple) * multiple))
            flat += [x for pair in products for x in pair] + list(small)
        total = sum(rows for _, _, rows in plans)
        kernel = functools.partial(weight_kernel, plan, plans)
        half_rows = ((total // 2, LANES), LOW)
        return run(kernel, name, [half_rows, half_rows], flat, [((total, LANES), LOW)], mib=mib)

    def query_grad(name, mixed, out_grad, logs):
        kernel = functools.partial(query_grad_kernel, plan)
        ins = [mixed, key_extra, query_extra, out_grad, logs]
        return run(kernel, name, [wide_low], ins, [double_shape, double_shape], mib=more)[0]

    weight_shape = (w_qkv.shape[1:], LOW)

    def early_shape(count):
        return ((3 * PAIRS, count * patch_count + plan.special_pad, LANES), LOW)

    key_extra, query_extra, mixed_0, start_0, normed_0, weight_0 = run(
        functools.partial(early_kernel, plan, early), "layer_0_early",
        [extra_shape, extra_shape, early_shape(len(early)), wide, wide_low, weight_shape],
        [blocks[index] for index in early] + [(image_lengths, WHOLE), (pad_counts, WHOLE),
         (specials, WHOLE), ln1, ln1_shift, (w_qkv, 0), qv_shift], mib=more)
    swapped, (mixed_0,) = spread(swapped, group, [mixed_0], {1: swap(swapped, 1)})
    blocks += swapped[1:]
    (mixed_0, middle_0, joined_0, total_0, hidden_0, slope_0, start_1, send, normed_specials,
     normed_1) = run(
        functools.partial(first_kernel, plan, early, rest), "layer_0_forward",
        [mixed_shape, wide, joined_shape, table_shape, hidden_shape,
         slope_shape, wide, ((plan.own_patch, width), LOW), ((special_count, width), LOW), wide_low],
        [blocks[index] for index in rest] + [mixed_0, key_extra, query_extra, start_0, weight_0, ln1,
         ln1_shift, qv_shift, (w_proj, 0), proj_shift, ln2, ln2_shift, (w_fc1, 0),
         fc1_shift, (w_fc2, 0), fc2_shift],
        [double_shape], mib=more, late=(1, 2, 5))
    middle_0, joined_0, slope_0 = [(v, WHOLE) for v in (middle_0, joined_0, slope_0)]
    grad_kept, grad_sent = kept_and_sent(tie([d_patches], [send])[0][0])
    grad_swapped = swap(grad_sent, group)
    near = {0: send, 1: swap(send, 1)}
    mixed_1, weight_1 = run(
        functools.partial(second_early_kernel, plan, list(near)), "layer_1_early",
        [early_shape(2 * len(near)), weight_shape],
        list(near.values()) + [normed_specials, (w_qkv, 1), qv_shift], mib=more)
    pieces, (mixed_1, grad_swapped) = spread(send, group, [mixed_1, grad_swapped], near)
    masks = [mask for mask in range(group) if mask not in near]
    pieces = [pieces[mask] for mask in masks]
    (mixed_1, out_kept, out_send, grad_middle_1, send, out_grad_1, logs_1, small_1, second_1,
     second_grad_1, pre_grad_1, attended_1, first_grad_1, hidden_1) = run(
        functools.partial(second_kernel, plan, list(near), masks), "layer_1_forward",
        [mixed_shape, ((patch_count, width), LOW), ((patch_count + special_count, width), LOW),
         wide, send_shape, wide_low, table_shape, small_shape, wide_low, wide_low, hidden_shape,
         wide_low, wide_low, hidden_shape],
        pieces + [mixed_1, key_extra, query_extra, start_1, grad_kept, grad_swapped,
                  (d_specials, WHOLE), weight_1, qv_shift, (w_proj, 1), proj_shift, ln2,
                  ln2_shift, (w_fc1, 1), fc1_shift, (w_fc2, 1), fc2_shift],
        [double_shape, joined_shape, table_shape, slope_shape, wide], mib=more)
    halves = weights(
        "layer_1_weights",
        ([(hidden_1, second_grad_1), (second_1, pre_grad_1), (attended_1, first_grad_1)], ()),
    )
    first_sum = Summing("first_sum", *halves)
    (out_grad_1,), _ = tie([out_grad_1], [halves[0]])
    grad_query_1 = query_grad("layer_1_query_grad", mixed_1, out_grad_1, logs_1)
    later_pieces, (grad_query_1,) = spread(send, group, [grad_query_1])
    out_got = swap(out_send, group)
    last = first_sum.step(grad_query_1)
    (grad_query_1, out_got), _ = tie([grad_query_1, out_got], [last])
    (grad_mixed_1, small_1, grad_middle_0, send, out_grad_0, logs_0, small_0, second_0,
     second_grad_0, pre_grad_0, attended_0, first_grad_0) = run(
        functools.partial(third_kernel, plan), "layer_1_key_grad",
        [((own, 3 * width), LOW), small_shape, wide, send_shape, wide_low, table_shape, small_shape,
         wide_low, wide_low, hidden_shape, wide_low, wide_low],
        later_pieces + [mixed_1, key_extra, query_extra, out_grad_1, logs_1, grad_query_1, start_1,
                        grad_middle_1, small_1, ln1, (w_qkv, 1), middle_0, joined_0, total_0,
                        hidden_0, slope_0, ln2, ln2_shift, (w_fc1, 0), (w_fc2, 0), (w_proj, 0)],
        [double_shape, double_shape, all_grads_shape], mib=mib)
    halves = weights(
        "layer_0_weights",
        ([(hidden_0, second_grad_0), (second_0, pre_grad_0), (attended_0, first_grad_0)], ()),
    )
    last = first_sum.step(halves[0])
    later_pieces, (last, *halves) = spread(send, group, [last, *halves])
    second_sum = Summing("second_sum", *halves)
    (out_grad_0,), _ = tie([out_grad_0], halves)
    grad_query_0 = query_grad("layer_0_query_grad", mixed_0, out_grad_0, logs_0)
    last = first_sum.step(grad_query_0)
    last = second_sum.step(last)
    (grad_query_0,), _ = tie([grad_query_0], [last])
    grad_mixed_0, small_0, grad_kept_out, grad_send = run(
        functools.partial(fourth_kernel, plan), "layer_0_key_grad",
        [((own, 3 * width), LOW), small_shape, ((patch_count, width), F32),
         ((patch_count + special_count, width), LOW)],
        later_pieces + [mixed_0, key_extra, query_extra, out_grad_0, logs_0, grad_query_0, start_0,
                        grad_middle_0, small_0, ln1, (w_qkv, 0)],
        [double_shape, double_shape, all_grads_shape], mib=max(20, mib))
    halves = weights(
        "mix_weights",
        ([(normed_0, grad_mixed_0)], [small_0]),
        ([(normed_1, grad_mixed_1)], [small_1]),
    )
    last = second_sum.step(halves[0])
    last_sum = Summing("last_sum", *tie(list(halves), [last])[0])
    fc2_shape, fc1_shape, proj_shape = w_fc2.shape, w_fc1.shape, w_proj.shape
    entries = [(0,) + fc2_shape[1:], (1,) + fc1_shape[1:], (2,) + proj_shape[1:]]
    stacked = {}
    sums = {"a": (first_sum, 1, "unpack_first"), "b": (second_sum, 0, "unpack_second")}
    order = list(ORDER) + ["a", "b", "c"] * 9
    while order:
        which = order.pop(0)
        if which == "c" and last_sum.steps:
            last = last_sum.step(last)
        elif which == "g":
            grad_got = swap(tie([grad_send], [last])[0][0], group)
        elif which == "G":
            grad_got = last_sum.after(grad_got)
        elif which in sums:
            this, layer, name = sums[which]
            if this.steps:
                last = this.step(last)
                continue
            del sums[which]
            this.after(last)
            where = [(output, layer, *shape) for output, *shape in entries]
            shapes = [fc2_shape, fc1_shape, proj_shape]
            stacked = dict(enumerate(unpacked(name, this.arrived(), where, shapes, stacked)))
            last = stacked[2]
    fc2, fc1, proj = stacked[0], stacked[1], stacked[2]
    widths = [width, width, 2 * width, width, width, width, hidden_width, width]
    buffer, semaphore = [(w_qkv.shape[1:], F32)], [pltpu.SemaphoreType.DMA((1,))]
    mine = tie(last_sum.values[:1], [stacked[2]])[0][0]
    qkv, own_small = run(
        functools.partial(unpack_half_kernel, True), "unpack_own",
        [(w_qkv.shape, F32), small_shape], [mine], buffer, {0}, None, semaphore, 24)
    got = last_sum.arrived()[1]
    qkv, *sums = run(
        functools.partial(unpack_half_kernel, False), "unpack_other",
        [(w_qkv.shape, F32)] + [((LAYERS, columns), F32) for columns in widths],
        [got, qkv, own_small], buffer, {0}, {1: 0}, semaphore, 24)
    pair = lambda count, kind: ((2, count, width), kind)
    out_patches, out_specials, grad_patches, grad_specials = run(
        functools.partial(assemble_kernel, plan), "assemble",
        [pair(patch_count, LOW), pair(special_count, LOW), pair(patch_count, F32),
         pair(special_count, F32)],
        [out_kept, out_send, out_got, grad_kept_out, grad_send, grad_got])
    return (
        out_patches, out_specials, grad_patches, grad_specials,
        sums[0], sums[1], qkv, sums[2], proj, sums[3], sums[4], sums[5], fc1, sums[6], fc2, sums[7],
    )


def solution(mesh):
    rows, one = P("pack", "blk", None), P("pack", None, None)
    in_specs = (rows, one, P("pack", None), P("pack", None)) + (P(),) * 12 + (rows, one)
    out_specs = (rows, one, rows, one) + (P(),) * 12
    return jax.shard_map(
        on_device, mesh=mesh, in_specs=in_specs, out_specs=out_specs, check_vma=False
    )
```
